32 devices in a mesh: shot: 4 (over y, core), band: 8 (over z, x).
Axes of the slice: x: 2, y: 2, z: 4, core: 2. Of those that a mesh axis runs over, the one named last changes fastest.
Arguments:
- sensitivity: bfloat16 [2048, 128, 128], P(('shot', 'band')), may hold values from -0.0625 to 0.0625
- bundle_of: int32 [2048], P(('shot', 'band')), may hold values from 0 to 7
- cellblock_of: int32 [2048], P(('shot', 'band')), may hold values from 0 to 15
- state: float32 [16384, 128], P('band'), may hold values from -6 to 6
- prior_velocity: float32 [16384, 128], P('band'), may hold values from -6 to 6
- observed: float32 [32, 128], P(('shot', 'band')), may hold values from -6 to 6
- pick_weight: float32 [32, 128], P(('shot', 'band')), may hold values from 0.3 to 3
Outputs:
- new_state: float32 [16384, 128], P('band')
- weighted_residual: float32 [32, 128, 128], P(('shot', 'band'))
The draws below stay inside these ranges and needn't reach their ends.
Inputs may be any that keep to these rules, and one draw needn't show every extreme that they name: bundle_of names a bundle of the block's own source group. cellblock_of names a cell block of the block's own depth band.
All inputs are finite; a program needn't handle non-finite values.
Results may differ from the reference program's by a relative error of at most 0.0059.
Values may be sent and summed in bfloat16 or wider, within the bound.
No kernel may reach another device: no remote copies, remote signals or barrier semaphores. Data moves between devices by JAX's collectives and lax.ppermute only.
A program may use at most 64 MiB of HBM per device.

```python
import math
import jax
import jax.numpy as jnp
from jax import lax

RAYS = 128
CBLK = 128
SAMPLES = 128
NBLK = 64
CB_DEV = 16
BUNDLES = 8
CELLS = 16384
N_SHOT = 4
N_BAND = 8


def touch_ends(drawn, own_key, least, high):
    place = [jax.random.randint(jax.random.fold_in(own_key, axis), (), 0, length) for axis, length in enumerate(drawn.shape)]
    longest = drawn.shape.index(max(drawn.shape))
    next_to = place[:longest] + [(place[longest] + 1) % drawn.shape[longest]] + place[longest + 1:]
    return drawn.at[tuple(place)].set(least).at[tuple(next_to)].set(high)


def steps_of(own_key, dims, split, smallest, top_value):
    def one(dim, shards_of):
        heights = jax.random.uniform(jax.random.fold_in(jax.random.fold_in(own_key, 6), dim), (shards_of,), jnp.float32, smallest / len(split), top_value / len(split))
        return jnp.repeat(jnp.exp(heights), dims[dim] // shards_of).reshape((-1,) + (1,) * (len(dims) - dim - 1))

    level = one(*split[0])
    for cut in split[1:]:
        level = level * one(*cut)
    return level


def gaussian(stream_key, dims, deviation, bound, split=(), dtype=jnp.bfloat16):
    array = jax.random.normal(stream_key, dims, jnp.float32) * deviation
    if len(split) > 0:
        array = steps_of(stream_key, dims, split, -0.22, 0.18) * array
    return jnp.clip(array, min=-bound, max=bound).astype(dtype)


def setup_inputs(seed: int = 0) -> dict:
    seeds = jax.random.split(jax.random.key(seed), 8)
    sensitivity = gaussian(seeds[0], (N_SHOT * N_BAND * NBLK, RAYS, CBLK), (CBLK * NBLK * N_BAND // BUNDLES) ** -0.5, 0.0625, ((0, 32),))
    bundle_of = touch_ends(jax.random.randint(seeds[1], (N_SHOT * N_BAND * NBLK,), 0, BUNDLES), jax.random.fold_in(seeds[1], 1), 0, BUNDLES - 1).astype(jnp.int32)
    cellblock_of = touch_ends(jax.random.randint(seeds[2], (N_SHOT * N_BAND * NBLK,), 0, CB_DEV), jax.random.fold_in(seeds[2], 1), 0, CB_DEV - 1).astype(jnp.int32)
    state = gaussian(seeds[3], (CELLS, SAMPLES), 1.0, 6.0, ((0, 8),), jnp.float32)
    prior_velocity = gaussian(seeds[4], (CELLS, SAMPLES), 1.0, 6.0, ((0, 8),), jnp.float32)
    observed = gaussian(seeds[5], (N_SHOT * BUNDLES, RAYS), 1.0, 6.0, ((0, 32),), jnp.float32)
    pick_weight = jnp.clip(jnp.exp(math.log(3.0) - 2.3025851 * jax.random.uniform(seeds[6], (N_SHOT * BUNDLES, RAYS), jnp.float32) ** steps_of(seeds[6], (N_SHOT * BUNDLES, RAYS), ((0, 32),), -0.2, 0.2)), 0.3, 3.0)
    return dict(sensitivity=sensitivity, bundle_of=bundle_of, cellblock_of=cellblock_of, state=state, prior_velocity=prior_velocity, observed=observed, pick_weight=pick_weight)


def forward(sens, bund, cblk, probe):
    def per_shot(shot_index):
        def step(acc, band_index):
            columns = probe[band_index][cblk[shot_index, band_index]]
            prod = jnp.einsum('krc,kce->kre', sens[shot_index, band_index].astype(jnp.float32), columns.astype(jnp.float32))
            return acc + jax.ops.segment_sum(prod, bund[shot_index, band_index], num_segments=BUNDLES), None
        start = jnp.zeros((BUNDLES, RAYS, SAMPLES), jnp.float32)
        acc, _ = lax.scan(step, start, jnp.arange(N_BAND))
        return acc
    return lax.map(per_shot, jnp.arange(N_SHOT))


def adjoint(sens, bund, cblk, resid):
    def per_band(band_index):
        def step(acc, shot_index):
            rows = resid[shot_index][bund[shot_index, band_index]]
            contrib = jnp.einsum('krc,kre->kce', sens[shot_index, band_index].astype(jnp.float32), rows.astype(jnp.float32))
            return acc + jax.ops.segment_sum(contrib, cblk[shot_index, band_index], num_segments=CB_DEV), None
        start = jnp.zeros((CB_DEV, CBLK, SAMPLES), jnp.float32)
        acc, _ = lax.scan(step, start, jnp.arange(N_SHOT))
        return acc
    return lax.map(per_band, jnp.arange(N_BAND)).reshape(CELLS, SAMPLES)


def reference(sensitivity, bundle_of, cellblock_of, state, prior_velocity, observed, pick_weight):
    sens = sensitivity.reshape(N_SHOT, N_BAND, NBLK, RAYS, CBLK)
    bund = bundle_of.reshape(N_SHOT, N_BAND, NBLK)
    cblk = cellblock_of.reshape(N_SHOT, N_BAND, NBLK)
    obs = observed.reshape(N_SHOT, BUNDLES, RAYS)[..., None]
    wts = pick_weight.reshape(N_SHOT, BUNDLES, RAYS)[..., None]
    probe1 = (state + 0.5 * prior_velocity).astype(jnp.bfloat16).reshape(N_BAND, CB_DEV, CBLK, SAMPLES)
    res1 = wts * (forward(sens, bund, cblk, probe1) - obs)
    grad1 = adjoint(sens, bund, cblk, res1.astype(jnp.bfloat16))
    middle = state + 0.5 * (prior_velocity - 0.5 * grad1)
    probe2 = (middle + 0.5 * prior_velocity).astype(jnp.bfloat16).reshape(N_BAND, CB_DEV, CBLK, SAMPLES)
    res2 = wts * (forward(sens, bund, cblk, probe2) - obs)
    grad2 = adjoint(sens, bund, cblk, res2.astype(jnp.bfloat16))
    new_state = state + 0.5 * (prior_velocity - 0.25 * (grad1 + grad2))
    return new_state, res2.reshape(N_SHOT * BUNDLES, RAYS, SAMPLES)
```

```python
import functools

import jax
import jax.numpy as jnp
from jax import lax
from jax.experimental import pallas as pl
from jax.experimental.pallas import tpu as pltpu
from jax.sharding import PartitionSpec as P

CBLK = 128
GROUP = 4

VMEM = pl.BlockSpec(memory_space=pltpu.VMEM)
SMEM = pl.BlockSpec(memory_space=pltpu.SMEM)


def call(body, outs, scratch, in_specs, name, flops=0, bytes_accessed=0):
    return pl.pallas_call(
        body,
        out_shape=outs,
        in_specs=in_specs,
        out_specs=jax.tree.map(lambda _: VMEM, outs),
        scratch_shapes=scratch,
        compiler_params=pltpu.CompilerParams(vmem_limit_bytes=32 * 1024 * 1024),
        cost_estimate=pl.CostEstimate(
            flops=flops, bytes_accessed=bytes_accessed, transcendentals=0
        ),
        name=name,
    )


def forward_blocks(bund_ref, cblk_ref, sens_ref, probe_ref, out_ref, acc_ref):
    acc_ref[...] = jnp.zeros_like(acc_ref)

    def group(g, carry):
        ks = [g * GROUP + j for j in range(GROUP)]
        prods = [
            jnp.dot(sens_ref[k], probe_ref[cblk_ref[k]], preferred_element_type=jnp.float32)
            for k in ks
        ]
        for k, prod in zip(ks, prods):
            acc_ref[bund_ref[k]] += prod
        return carry

    lax.fori_loop(0, sens_ref.shape[0] // GROUP, group, 0)
    out_ref[...] = acc_ref[...].astype(jnp.bfloat16)


def first_forward_kernel(bund_ref, cblk_ref, sens_ref, state_ref, prior_ref, out_ref, acc_ref, probe_ref):
    probe_ref[...] = (state_ref[...] + 0.5 * prior_ref[...]).astype(jnp.bfloat16)
    forward_blocks(bund_ref, cblk_ref, sens_ref, probe_ref, out_ref, acc_ref)


def adjoint_kernel(bund_ref, cblk_ref, sens_ref, resid_ref, out_ref, acc_ref):
    acc_ref[...] = jnp.zeros_like(acc_ref)

    def group(g, carry):
        ks = [g * GROUP + j for j in range(GROUP)]
        prods = [
            jnp.dot(resid_ref[bund_ref[k]], sens_ref[k], preferred_element_type=jnp.float32)
            for k in ks
        ]
        for k, prod in zip(ks, prods):
            acc_ref[cblk_ref[k]] += prod
        return carry

    lax.fori_loop(0, sens_ref.shape[0] // GROUP, group, 0)
    out_ref[...] = acc_ref[...].astype(jnp.bfloat16)


def residual_kernel(parts_ref, obs_ref, wt_ref, out_ref, resid_ref):
    for m in range(parts_ref.shape[1]):
        total = parts_ref[0, m].astype(jnp.float32)
        for d in range(1, parts_ref.shape[0]):
            total += parts_ref[d, m].astype(jnp.float32)
        resid = wt_ref[pl.ds(m, 1), :] * (total.T - obs_ref[pl.ds(m, 1), :])
        resid_ref[m] = resid.T
        for d in range(parts_ref.shape[0]):
            out_ref[d, m] = resid.astype(jnp.bfloat16)


def probe_kernel(parts_ref, state_ref, prior_ref, out_ref, grad_ref):
    for c in range(parts_ref.shape[1]):
        total = parts_ref[0, c].astype(jnp.float32)
        for d in range(1, parts_ref.shape[0]):
            total += parts_ref[d, c].astype(jnp.float32)
        grad = total.T
        grad_ref[c] = grad
        middle = state_ref[c] + 0.5 * (prior_ref[c] - 0.5 * grad)
        probe = (middle + 0.5 * prior_ref[c]).astype(jnp.bfloat16)
        for d in range(parts_ref.shape[0]):
            out_ref[d, c] = probe


def total_kernel(parts_ref, grad_ref, out_ref):
    for c in range(parts_ref.shape[1]):
        total = parts_ref[0, c].astype(jnp.float32)
        for d in range(1, parts_ref.shape[0]):
            total += parts_ref[d, c].astype(jnp.float32)
        both = (grad_ref[c] + total.T).astype(jnp.bfloat16)
        for d in range(parts_ref.shape[0]):
            out_ref[d, c] = both


def exchange(array, axis):
    return lax.all_to_all(array, axis, split_axis=0, concat_axis=0, tiled=True)


def per_device(nshot, nband, sens, bund, cblk, state, prior, observed, pick_weight):
    nblk = sens.shape[0]
    samples = state.shape[1]
    owned, rays = observed.shape
    bundles = owned * nband
    cells = state.shape[0] // CBLK
    mine = cells // nshot
    bf16, f32 = jnp.bfloat16, jnp.float32
    arr = jax.ShapeDtypeStruct
    flops = 2 * nblk * rays * CBLK * samples
    sens_bytes = nblk * rays * CBLK * 2

    state_b = state.reshape(cells, CBLK, samples)
    prior_b = prior.reshape(cells, CBLK, samples)
    at = lax.axis_index("shot") * mine
    state_q = lax.dynamic_slice_in_dim(state_b, at, mine, 0)
    prior_q = lax.dynamic_slice_in_dim(prior_b, at, mine, 0)

    part_out = arr((bundles, rays, samples), bf16)
    part_acc = pltpu.VMEM((bundles, rays, samples), f32)

    def residual(part, name):
        parts = exchange(part, "band").reshape(nband, owned, rays, samples)
        copies, resid = call(
            residual_kernel,
            (arr((nband, owned, samples, rays), bf16), arr((owned, rays, samples), f32)),
            [],
            [VMEM] * 3,
            name,
            bytes_accessed=1 << 20,
        )(parts, observed, pick_weight)
        resid_all = exchange(copies, "band").reshape(bundles, samples, rays)
        return resid, resid_all

    def adjoint(resid_all, name):
        out = call(
            adjoint_kernel,
            arr((cells, samples, CBLK), bf16),
            [pltpu.VMEM((cells, samples, CBLK), f32)],
            [SMEM, SMEM, VMEM, VMEM],
            name,
            flops,
            sens_bytes,
        )(bund, cblk, sens, resid_all)
        return exchange(out, "shot").reshape(nshot, mine, samples, CBLK)

    part1 = call(
        first_forward_kernel,
        part_out,
        [part_acc, pltpu.VMEM((cells, CBLK, samples), bf16)],
        [SMEM, SMEM, VMEM, VMEM, VMEM],
        "forward1",
        flops,
        sens_bytes,
    )(bund, cblk, sens, state_b, prior_b)
    _, resid_all1 = residual(part1, "residual1")
    gparts1 = adjoint(resid_all1, "adjoint1")
    probes, grad1 = call(
        probe_kernel,
        (arr((nshot, mine, CBLK, samples), bf16), arr((mine, CBLK, samples), f32)),
        [],
        [VMEM] * 3,
        "probe2",
        bytes_accessed=1 << 20,
    )(gparts1, state_q, prior_q)
    probe2 = exchange(probes, "shot").reshape(cells, CBLK, samples)
    part2 = call(
        forward_blocks,
        part_out,
        [part_acc],
        [SMEM, SMEM, VMEM, VMEM],
        "forward2",
        flops,
        sens_bytes,
    )(bund, cblk, sens, probe2)
    resid2, resid_all2 = residual(part2, "residual2")
    gparts2 = adjoint(resid_all2, "adjoint2")
    boths = call(
        total_kernel,
        arr((nshot, mine, CBLK, samples), bf16),
        [],
        [VMEM] * 2,
        "total",
        bytes_accessed=1 << 20,
    )(gparts2, grad1)
    both = exchange(boths, "shot").reshape(state.shape)
    new_state = state + 0.5 * (prior - 0.25 * both.astype(f32))
    return new_state, resid2


def solution(mesh):
    in_specs = (
        P(("shot", "band"), None, None),
        P(("shot", "band")),
        P(("shot", "band")),
        P("band", None),
        P("band", None),
        P(("shot", "band"), None),
        P(("shot", "band"), None),
    )
    out_specs = (P("band", None), P(("shot", "band"), None, None))
    return jax.shard_map(
        functools.partial(per_device, mesh.shape["shot"], mesh.shape["band"]),
        mesh=mesh,
        in_specs=in_specs,
        out_specs=out_specs,
        check_vma=False,
    )
```

```python
import functools

import jax
import jax.numpy as jnp
from jax import lax
from jax.experimental import pallas as pl
from jax.experimental.pallas import tpu as pltpu
from jax.sharding import PartitionSpec as P

CBLK = 128
GROUP = 4
CHUNKS = 4
FIRST_VMEM = 62 << 20

VMEM = pl.BlockSpec(memory_space=pltpu.VMEM)
SMEM = pl.BlockSpec(memory_space=pltpu.SMEM)
HBM = pl.BlockSpec(memory_space=pltpu.HBM)

bf16, f32 = jnp.bfloat16, jnp.float32
arr = jax.ShapeDtypeStruct


def call(body, outs, scratch, in_specs, name, flops=0, bytes_accessed=0, vmem=32 << 20):
    return pl.pallas_call(
        body,
        out_shape=outs,
        in_specs=in_specs,
        out_specs=jax.tree.map(lambda _: VMEM, outs),
        scratch_shapes=scratch,
        compiler_params=pltpu.CompilerParams(vmem_limit_bytes=vmem),
        cost_estimate=pl.CostEstimate(
            flops=flops, bytes_accessed=bytes_accessed, transcendentals=0
        ),
        name=name,
    )


def products(lo, hi, lhs_of, rhs_of, slot_of, acc_ref):
    def group(g, carry):
        ks = [g * GROUP + j for j in range(GROUP)]
        prods = [jnp.dot(lhs_of(k), rhs_of(k), preferred_element_type=f32) for k in ks]
        for k, prod in zip(ks, prods):
            acc_ref[slot_of(k)] += prod
        return carry

    lax.fori_loop(lo // GROUP, hi // GROUP, group, 0)


def split_out(me, acc_ref, out_refs):
    size = out_refs[0].shape[0]
    for d, out_ref in enumerate(out_refs):
        out_ref[...] = acc_ref[pl.ds((me ^ d) * size, size)].astype(bf16)


def first_forward_kernel(n, me_ref, bund_hbm, cblk_hbm, sens_hbm, state_hbm, prior_hbm, *rest):
    out_refs, (acc, probe, bund, cblk, sens, state, prior, sems) = rest[:n], rest[n:]
    nblk = sens.shape[0]
    step = nblk // CHUNKS
    half = state.shape[0] // 2
    small = [
        pltpu.make_async_copy(bund_hbm, bund, sems.at[0]),
        pltpu.make_async_copy(cblk_hbm, cblk, sems.at[1]),
    ]
    fields = []
    for h in range(2):
        part = pl.ds(h * half, half)
        fields.append(
            [
                pltpu.make_async_copy(state_hbm.at[part], state.at[part], sems.at[2 + 2 * h]),
                pltpu.make_async_copy(prior_hbm.at[part], prior.at[part], sems.at[3 + 2 * h]),
            ]
        )
    blocks = [
        pltpu.make_async_copy(
            sens_hbm.at[pl.ds(c * step, step)], sens.at[pl.ds(c * step, step)], sems.at[6 + c]
        )
        for c in range(CHUNKS)
    ]
    for copy in small + fields[0] + fields[1] + blocks:
        copy.start()
    acc[...] = jnp.zeros_like(acc)
    for h in range(2):
        part = pl.ds(h * half, half)
        for copy in fields[h]:
            copy.wait()
        probe[part] = (state[part] + 0.5 * prior[part]).astype(bf16)
    for copy in small:
        copy.wait()
    for c in range(CHUNKS):
        blocks[c].wait()
        products(
            c * step,
            (c + 1) * step,
            lambda k: sens[k],
            lambda k: probe[cblk[k]],
            lambda k: bund[k],
            acc,
        )
    split_out(me_ref[0], acc, out_refs)


def forward_kernel(n, m, me_ref, shot_ref, bund, cblk, sens, *rest):
    probe_refs, out_refs, (acc, probe) = rest[:m], rest[m : m + n], rest[m + n :]
    acc[...] = jnp.zeros_like(acc)
    join_in(shot_ref[0], probe_refs, probe)
    products(
        0,
        sens.shape[0],
        lambda k: sens[k],
        lambda k: probe[cblk[k]],
        lambda k: bund[k],
        acc,
    )
    split_out(me_ref[0], acc, out_refs)


def join_in(me, in_refs, whole_ref):
    size = in_refs[0].shape[0]
    for d, in_ref in enumerate(in_refs):
        whole_ref[pl.ds((me ^ d) * size, size)] = in_ref[...]


def adjoint_kernel(n, m, me_ref, shot_ref, bund, cblk, sens, *rest):
    resid_refs, out_refs, (acc, resid) = rest[:n], rest[n : n + m], rest[n + m :]
    acc[...] = jnp.zeros_like(acc)
    join_in(me_ref[0], resid_refs, resid)
    products(
        0,
        sens.shape[0],
        lambda k: resid[bund[k]],
        lambda k: sens[k],
        lambda k: cblk[k],
        acc,
    )
    split_out(shot_ref[0], acc, out_refs)


def sum_of(part_refs, i):
    total = part_refs[0][i].astype(f32)
    for part_ref in part_refs[1:]:
        total += part_ref[i].astype(f32)
    return total


def residual_kernel(n, obs_ref, wt_ref, *rest):
    part_refs, (out_ref, resid_ref) = rest[:n], rest[n:]
    for i in range(out_ref.shape[0]):
        total = sum_of(part_refs, i)
        resid = wt_ref[pl.ds(i, 1), :] * (total.T - obs_ref[pl.ds(i, 1), :])
        resid_ref[i] = resid.T
        out_ref[i] = resid.astype(bf16)


def probe_kernel(m, shot_ref, state_hbm, prior_hbm, *rest):
    part_refs, (out_ref, grad_ref, state, prior, sems) = rest[:m], rest[m:]
    mine = out_ref.shape[0]
    part = pl.ds(shot_ref[0] * mine, mine)
    copies = [
        pltpu.make_async_copy(state_hbm.at[part], state, sems.at[0]),
        pltpu.make_async_copy(prior_hbm.at[part], prior, sems.at[1]),
    ]
    for copy in copies:
        copy.start()
    for i in range(mine):
        grad_ref[i] = sum_of(part_refs, i).T
    for copy in copies:
        copy.wait()
    middle = state[...] + 0.5 * (prior[...] - 0.5 * grad_ref[...])
    out_ref[...] = (middle + 0.5 * prior[...]).astype(bf16)


def total_kernel(m, grad_ref, *rest):
    part_refs, out_ref = rest[:m], rest[m]
    for i in range(out_ref.shape[0]):
        out_ref[i] = (grad_ref[i] + sum_of(part_refs, i).T).astype(bf16)


def last_kernel(m, shot_ref, state, prior, *rest):
    part_refs, out_ref = rest[:m], rest[m]
    size = part_refs[0].shape[0]
    for d, part_ref in enumerate(part_refs):
        at = pl.ds((shot_ref[0] ^ d) * size, size)
        out_ref[at] = state[at] + 0.5 * (prior[at] - 0.25 * part_ref[...].astype(f32))


def send(array, axis, n, d):
    return lax.ppermute(array, axis, [(i, i ^ d) for i in range(n)])


def per_device(nshot, nband, sens, bund, cblk, state, prior, observed, pick_weight):
    nblk = sens.shape[0]
    samples = state.shape[1]
    owned, rays = observed.shape
    bundles = owned * nband
    cells = state.shape[0] // CBLK
    mine = cells // nshot
    flops = 2 * nblk * rays * CBLK * samples
    sens_bytes = nblk * rays * CBLK * 2

    state_b = state.reshape(cells, CBLK, samples)
    prior_b = prior.reshape(cells, CBLK, samples)
    shot = lax.axis_index("shot").reshape(1)
    band = lax.axis_index("band").reshape(1)

    def scatter(parts, axis, n):
        return [parts[0]] + [send(parts[d], axis, n, d) for d in range(1, n)]

    def gather(part, axis, n):
        return [part] + [send(part, axis, n, d) for d in range(1, n)]

    part_out = tuple(arr((owned, rays, samples), bf16) for _ in range(nband))
    part_acc = pltpu.VMEM((bundles, rays, samples), f32)
    whole_field = pltpu.VMEM((cells, CBLK, samples), bf16)

    def residual(parts, name):
        resid_t, resid = call(
            functools.partial(residual_kernel, nband),
            (arr((owned, samples, rays), bf16), arr((owned, rays, samples), f32)),
            [],
            [VMEM] * (2 + nband),
            name,
            bytes_accessed=1 << 20,
        )(observed, pick_weight, *scatter(parts, "band", nband))
        return resid, gather(resid_t, "band", nband)

    def adjoint(resids, name):
        outs = call(
            functools.partial(adjoint_kernel, nband, nshot),
            tuple(arr((mine, samples, CBLK), bf16) for _ in range(nshot)),
            [pltpu.VMEM((cells, samples, CBLK), f32), pltpu.VMEM((bundles, samples, rays), bf16)],
            [SMEM] * 4 + [VMEM] * (1 + nband),
            name,
            flops,
            sens_bytes,
        )(band, shot, bund, cblk, sens, *resids)
        return scatter(outs, "shot", nshot)

    parts1 = call(
        functools.partial(first_forward_kernel, nband),
        part_out,
        [
            part_acc,
            whole_field,
            pltpu.SMEM((nblk,), jnp.int32),
            pltpu.SMEM((nblk,), jnp.int32),
            pltpu.VMEM(sens.shape, bf16),
            pltpu.VMEM(state_b.shape, f32),
            pltpu.VMEM(state_b.shape, f32),
            pltpu.SemaphoreType.DMA((6 + CHUNKS,)),
        ],
        [SMEM] + [HBM] * 5,
        "forward1",
        flops,
        sens_bytes,
        vmem=FIRST_VMEM,
    )(band, bund, cblk, sens, state_b, prior_b)
    _, resids1 = residual(parts1, "residual1")
    gparts1 = adjoint(resids1, "adjoint1")
    probe_part, grad1 = call(
        functools.partial(probe_kernel, nshot),
        (arr((mine, CBLK, samples), bf16), arr((mine, CBLK, samples), f32)),
        [
            pltpu.VMEM((mine, CBLK, samples), f32),
            pltpu.VMEM((mine, CBLK, samples), f32),
            pltpu.SemaphoreType.DMA((2,)),
        ],
        [SMEM, HBM, HBM] + [VMEM] * nshot,
        "probe2",
        bytes_accessed=1 << 20,
    )(shot, state_b, prior_b, *gparts1)
    probes = gather(probe_part, "shot", nshot)
    parts2 = call(
        functools.partial(forward_kernel, nband, nshot),
        part_out,
        [part_acc, whole_field],
        [SMEM] * 4 + [VMEM] * (1 + nshot),
        "forward2",
        flops,
        sens_bytes,
    )(band, shot, bund, cblk, sens, *probes)
    resid2, resids2 = residual(parts2, "residual2")
    gparts2 = adjoint(resids2, "adjoint2")
    total = call(
        functools.partial(total_kernel, nshot),
        arr((mine, CBLK, samples), bf16),
        [],
        [VMEM] * (1 + nshot),
        "total",
        bytes_accessed=1 << 20,
    )(grad1, *gparts2)
    totals = gather(total, "shot", nshot)
    new_state = call(
        functools.partial(last_kernel, nshot),
        arr((cells, CBLK, samples), f32),
        [],
        [SMEM] + [VMEM] * (2 + nshot),
        "new_state",
        bytes_accessed=4 << 20,
    )(shot, state_b, prior_b, *totals)
    return new_state.reshape(state.shape), resid2


def solution(mesh):
    in_specs = (
        P(("shot", "band"), None, None),
        P(("shot", "band")),
        P(("shot", "band")),
        P("band", None),
        P("band", None),
        P(("shot", "band"), None),
        P(("shot", "band"), None),
    )
    out_specs = (P("band", None), P(("shot", "band"), None, None))
    return jax.shard_map(
        functools.partial(per_device, mesh.shape["shot"], mesh.shape["band"]),
        mesh=mesh,
        in_specs=in_specs,
        out_specs=out_specs,
        check_vma=False,
    )
```

```python
import functools

import jax
import jax.numpy as jnp
from jax import lax
from jax.experimental import pallas as pl
from jax.experimental.pallas import tpu as pltpu
from jax.sharding import PartitionSpec as P

CBLK = 128
GROUP = 16
CHUNKS = 4
FIRST_VMEM = 57 << 20

VMEM = pl.BlockSpec(memory_space=pltpu.VMEM)
SMEM = pl.BlockSpec(memory_space=pltpu.SMEM)
HBM = pl.BlockSpec(memory_space=pltpu.HBM)

bf16, f32 = jnp.bfloat16, jnp.float32
arr = jax.ShapeDtypeStruct


def call(body, outs, scratch, in_specs, name, flops=0, bytes_accessed=0, vmem=32 << 20):
    return pl.pallas_call(
        body,
        out_shape=outs,
        in_specs=in_specs,
        out_specs=jax.tree.map(lambda _: VMEM, outs),
        scratch_shapes=scratch,
        compiler_params=pltpu.CompilerParams(vmem_limit_bytes=vmem),
        cost_estimate=pl.CostEstimate(
            flops=flops, bytes_accessed=bytes_accessed, transcendentals=0
        ),
        name=name,
    )


def products(first, count, lhs_of, rhs_of, slot_of, acc_ref):
    def group(g, carry):
        ks = [first + g * GROUP + j for j in range(GROUP)]
        prods = [jnp.dot(lhs_of(k), rhs_of(k), preferred_element_type=f32) for k in ks]
        for k, prod in zip(ks, prods):
            acc_ref[slot_of(k)] += prod
        return carry

    if count == GROUP:
        group(0, 0)
    else:
        lax.fori_loop(0, count // GROUP, group, 0)


def first_forward_kernel(
    bund_hbm, cblk_hbm, sens_hbm, state_hbm, prior_hbm, out_ref, acc, probe, bund, cblk, sens, state, prior, sems
):
    nblk = sens.shape[0]
    step = nblk // CHUNKS
    half = state.shape[0] // 2
    small = [
        pltpu.make_async_copy(bund_hbm, bund, sems.at[0]),
        pltpu.make_async_copy(cblk_hbm, cblk, sems.at[1]),
    ]
    fields = []
    for h in range(2):
        part = pl.ds(h * half, half)
        fields.append(
            [
                pltpu.make_async_copy(state_hbm.at[part], state.at[part], sems.at[2 + 2 * h]),
                pltpu.make_async_copy(prior_hbm.at[part], prior.at[part], sems.at[3 + 2 * h]),
            ]
        )

    def block_copy(c):
        part = pl.ds(c * step, step)
        return pltpu.make_async_copy(sens_hbm.at[part], sens.at[part], sems.at[6 + c])

    for copy in small + fields[0] + fields[1] + [block_copy(c) for c in range(CHUNKS)]:
        copy.start()
    acc[...] = jnp.zeros_like(acc)
    for h in range(2):
        part = pl.ds(h * half, half)
        for copy in fields[h]:
            copy.wait()
        probe[part] = (state[part] + 0.5 * prior[part]).astype(bf16)
    for copy in small:
        copy.wait()

    def chunk(c, carry):
        block_copy(c).wait()
        products(
            c * step,
            step,
            lambda k: sens[k],
            lambda k: probe[cblk[k]],
            lambda k: bund[k],
            acc,
        )
        return carry

    lax.fori_loop(0, CHUNKS, chunk, 0)
    out_ref[...] = acc[...].astype(bf16)


def forward_kernel(shot_ref, bund, cblk, sens, own_ref, mate_ref, out_ref, acc, probe):
    half = own_ref.shape[0]
    core = shot_ref[0] % 2
    probe[pl.ds(core * half, half)] = own_ref[...]
    probe[pl.ds((1 - core) * half, half)] = mate_ref[...]
    acc[...] = jnp.zeros_like(acc)
    products(
        0,
        sens.shape[0],
        lambda k: sens[k],
        lambda k: probe[cblk[k]],
        lambda k: bund[k],
        acc,
    )
    out_ref[...] = acc[...].astype(bf16)


def adjoint_kernel(shot_ref, bund, cblk, sens, resid, keep_ref, give_ref, acc):
    acc[...] = jnp.zeros_like(acc)
    products(
        0,
        sens.shape[0],
        lambda k: resid[bund[k]],
        lambda k: sens[k],
        lambda k: cblk[k],
        acc,
    )
    half = keep_ref.shape[0]
    core = shot_ref[0] % 2
    keep_ref[...] = acc[pl.ds(core * half, half)]
    give_ref[...] = acc[pl.ds((1 - core) * half, half)].astype(bf16)


def pair_kernel(keep_ref, got_ref, out_ref):
    out_ref[...] = (keep_ref[...] + got_ref[...].astype(f32)).astype(bf16)


def residual_kernel(parts_ref, obs_ref, wt_ref, out_ref, *resid_ref):
    for i in range(parts_ref.shape[1]):
        total = parts_ref[0, i].astype(f32)
        for d in range(1, parts_ref.shape[0]):
            total += parts_ref[d, i].astype(f32)
        resid = wt_ref[pl.ds(i, 1), :] * (total.T - obs_ref[pl.ds(i, 1), :])
        if resid_ref:
            resid_ref[0][i] = resid
        rounded = resid.astype(bf16)
        for d in range(parts_ref.shape[0]):
            out_ref[d, i] = rounded


def turn_kernel(in_ref, out_ref):
    for i in range(in_ref.shape[0]):
        out_ref[i] = in_ref[i].T


def sum_over_y(chip_y, part_refs, order, i):
    if len(part_refs) > 2:
        for d, part_ref in enumerate(part_refs):
            order[chip_y ^ d] = part_ref[i]
        part_refs = [order.at[y] for y in range(len(part_refs))]
        read = lambda ref: ref[...]
    else:
        read = lambda ref: ref[i]
    total = read(part_refs[0]).astype(f32)
    for part_ref in part_refs[1:]:
        total += read(part_ref).astype(f32)
    return total


def probe_kernel(ny, shot_ref, state_hbm, prior_hbm, *rest):
    part_refs, (out_ref, grad_ref, state, prior, order, sems) = rest[:ny], rest[ny:]
    half = out_ref.shape[0]
    core = shot_ref[0] % 2
    part = pl.ds(core * half, half)
    copies = [
        pltpu.make_async_copy(state_hbm.at[part], state, sems.at[0]),
        pltpu.make_async_copy(prior_hbm.at[part], prior, sems.at[1]),
    ]
    for copy in copies:
        copy.start()
    for i in range(half):
        grad_ref[i] = sum_over_y(shot_ref[0] // 2, part_refs, order, i).T
    for copy in copies:
        copy.wait()
    middle = state[...] + 0.5 * (prior[...] - 0.5 * grad_ref[...])
    out_ref[...] = (middle + 0.5 * prior[...]).astype(bf16)


def total_kernel(ny, shot_ref, grad_ref, *rest):
    part_refs, (out_ref, order) = rest[:ny], rest[ny:]
    for i in range(out_ref.shape[0]):
        grad2 = sum_over_y(shot_ref[0] // 2, part_refs, order, i).T
        out_ref[i] = (grad_ref[i] + grad2).astype(bf16)


def last_kernel(shot_ref, state, prior, own_ref, mate_ref, out_ref):
    half = own_ref.shape[0]
    core = shot_ref[0] % 2
    for at, part_ref in ((core * half, own_ref), ((1 - core) * half, mate_ref)):
        part = pl.ds(at, half)
        out_ref[part] = state[part] + 0.5 * (prior[part] - 0.25 * part_ref[...].astype(f32))


def per_device(nshot, nband, sens, bund, cblk, state, prior, observed, pick_weight):
    nblk = sens.shape[0]
    samples = state.shape[1]
    owned, rays = observed.shape
    bundles = owned * nband
    cells = state.shape[0] // CBLK
    half = cells // 2
    ny = nshot // 2
    flops = 2 * nblk * rays * CBLK * samples
    sens_bytes = nblk * rays * CBLK * 2

    state_b = state.reshape(cells, CBLK, samples)
    prior_b = prior.reshape(cells, CBLK, samples)
    shot = lax.axis_index("shot").reshape(1)

    def other_core(array):
        return lax.ppermute(array, "shot", [(i, i ^ 1) for i in range(nshot)])

    def other_chips(array):
        return [array] + [
            lax.ppermute(array, "shot", [(i, i ^ (2 * d)) for i in range(nshot)])
            for d in range(1, ny)
        ]

    def over_band(array):
        return lax.all_to_all(array, "band", split_axis=0, concat_axis=0, tiled=True)

    part_out = arr((bundles, rays, samples), bf16)
    part_acc = pltpu.VMEM((bundles, rays, samples), f32)
    whole_field = pltpu.VMEM((cells, CBLK, samples), bf16)
    half_bf16 = arr((half, CBLK, samples), bf16)
    half_f32 = arr((half, CBLK, samples), f32)
    half_scratch = pltpu.VMEM((half, CBLK, samples), f32)
    order = pltpu.VMEM((ny, samples, CBLK), bf16)

    def residual(part, name, keep):
        parts = over_band(part).reshape(nband, owned, rays, samples)
        outs = (arr((nband, owned, samples, rays), bf16),)
        if keep:
            outs += (arr((owned, samples, rays), f32),)
        copies, *resid = call(
            residual_kernel, outs, [], [VMEM] * 3, name, bytes_accessed=1 << 20
        )(parts, observed, pick_weight)
        return resid, over_band(copies).reshape(bundles, samples, rays)

    def adjoint(resid_all, name):
        keep, give = call(
            adjoint_kernel,
            (half_f32, half_bf16),
            [pltpu.VMEM((cells, samples, CBLK), f32)],
            [SMEM] * 3 + [VMEM] * 2,
            name,
            flops,
            sens_bytes,
        )(shot, bund, cblk, sens, resid_all)
        pair = call(
            pair_kernel, half_bf16, [], [VMEM] * 2, name + "_pair", bytes_accessed=1 << 20
        )(keep, other_core(give))
        return other_chips(pair)

    part1 = call(
        first_forward_kernel,
        part_out,
        [
            part_acc,
            whole_field,
            pltpu.SMEM((nblk,), jnp.int32),
            pltpu.SMEM((nblk,), jnp.int32),
            pltpu.VMEM(sens.shape, bf16),
            pltpu.VMEM(state_b.shape, f32),
            pltpu.VMEM(state_b.shape, f32),
            pltpu.SemaphoreType.DMA((6 + CHUNKS,)),
        ],
        [HBM] * 5,
        "forward1",
        flops,
        sens_bytes,
        vmem=FIRST_VMEM,
    )(bund, cblk, sens, state_b, prior_b)
    _, resid_all1 = residual(part1, "residual1", False)
    gparts1 = adjoint(resid_all1, "adjoint1")
    probe_own, grad1 = call(
        functools.partial(probe_kernel, ny),
        (half_bf16, half_f32),
        [half_scratch, half_scratch, order, pltpu.SemaphoreType.DMA((2,))],
        [SMEM, HBM, HBM] + [VMEM] * ny,
        "probe2",
        bytes_accessed=1 << 20,
    )(shot, state_b, prior_b, *gparts1)
    part2 = call(
        forward_kernel,
        part_out,
        [part_acc, whole_field],
        [SMEM] * 3 + [VMEM] * 3,
        "forward2",
        flops,
        sens_bytes,
    )(shot, bund, cblk, sens, probe_own, other_core(probe_own))
    (resid2_t,), resid_all2 = residual(part2, "residual2", True)
    resid2 = call(
        turn_kernel,
        arr((owned, rays, samples), f32),
        [],
        [VMEM],
        "turn",
        bytes_accessed=1 << 20,
    )(resid2_t)
    gparts2 = adjoint(resid_all2, "adjoint2")
    total = call(
        functools.partial(total_kernel, ny),
        half_bf16,
        [order],
        [SMEM] + [VMEM] * (1 + ny),
        "total",
        bytes_accessed=1 << 20,
    )(shot, grad1, *gparts2)
    new_state = call(
        last_kernel,
        arr((cells, CBLK, samples), f32),
        [],
        [SMEM] + [VMEM] * 4,
        "new_state",
        bytes_accessed=4 << 20,
    )(shot, state_b, prior_b, total, other_core(total))
    return new_state.reshape(state.shape), resid2


def solution(mesh):
    in_specs = (
        P(("shot", "band"), None, None),
        P(("shot", "band")),
        P(("shot", "band")),
        P("band", None),
        P("band", None),
        P(("shot", "band"), None),
        P(("shot", "band"), None),
    )
    out_specs = (P("band", None), P(("shot", "band"), None, None))
    return jax.shard_map(
        functools.partial(per_device, mesh.shape["shot"], mesh.shape["band"]),
        mesh=mesh,
        in_specs=in_specs,
        out_specs=out_specs,
        check_vma=False,
    )
```

```python
import functools

import jax
import jax.numpy as jnp
from jax import lax
from jax.experimental import pallas as pl
from jax.experimental.pallas import tpu as pltpu
from jax.sharding import PartitionSpec as P

CBLK = 128
GROUP = 16
CHUNKS = 4
CHAINS = 2
FIRST_VMEM = 57 << 20

VMEM = pl.BlockSpec(memory_space=pltpu.VMEM)
SMEM = pl.BlockSpec(memory_space=pltpu.SMEM)
HBM = pl.BlockSpec(memory_space=pltpu.HBM)

bf16, f32 = jnp.bfloat16, jnp.float32
arr = jax.ShapeDtypeStruct


def call(body, outs, scratch, in_specs, name, flops=0, bytes_accessed=0, vmem=32 << 20):
    return pl.pallas_call(
        body,
        out_shape=outs,
        in_specs=in_specs,
        out_specs=jax.tree.map(lambda _: VMEM, outs),
        scratch_shapes=scratch,
        compiler_params=pltpu.CompilerParams(vmem_limit_bytes=vmem),
        cost_estimate=pl.CostEstimate(
            flops=flops, bytes_accessed=bytes_accessed, transcendentals=0
        ),
        name=name,
    )


def products(first, count, product_of, slot_of, acc_ref):
    def group(g, carry):
        ks = [first + g * GROUP + j for j in range(GROUP)]
        prods = [product_of(k) for k in ks]
        for k, prod in zip(ks, prods):
            acc_ref[slot_of(k)] += prod
        return carry

    if count == GROUP:
        group(0, 0)
    else:
        lax.fori_loop(0, count // GROUP, group, 0)


def first_forward_kernel(
    bund_hbm, cblk_hbm, sens_hbm, state_hbm, prior_hbm, *rest
):
    out_refs, (acc, probe, bund, cblk, sens, state, prior, sems) = rest[:CHAINS], rest[CHAINS:]
    nblk = sens.shape[0]
    step = nblk // CHUNKS
    half = state.shape[0] // 2
    small = [
        pltpu.make_async_copy(bund_hbm, bund, sems.at[0]),
        pltpu.make_async_copy(cblk_hbm, cblk, sems.at[1]),
    ]
    fields = []
    for h in range(2):
        part = pl.ds(h * half, half)
        fields.append(
            [
                pltpu.make_async_copy(state_hbm.at[part], state.at[part], sems.at[2 + 2 * h]),
                pltpu.make_async_copy(prior_hbm.at[part], prior.at[part], sems.at[3 + 2 * h]),
            ]
        )

    def block_copy(c):
        part = pl.ds(c * step, step)
        return pltpu.make_async_copy(sens_hbm.at[part], sens.at[part], sems.at[6 + c])

    for copy in small + fields[0] + fields[1] + [block_copy(c) for c in range(CHUNKS)]:
        copy.start()
    acc[...] = jnp.zeros_like(acc)
    for h in range(2):
        part = pl.ds(h * half, half)
        for copy in fields[h]:
            copy.wait()
        probe[part] = (state[part] + 0.5 * prior[part]).astype(bf16)
    for copy in small:
        copy.wait()

    def chunk(c, carry):
        block_copy(c).wait()
        products(
            c * step,
            step,
            lambda k: jnp.dot(sens[k], probe[cblk[k]], preferred_element_type=f32),
            lambda k: bund[k],
            acc,
        )
        return carry

    lax.fori_loop(0, CHUNKS, chunk, 0)
    for m in range(acc.shape[0]):
        turned = acc[m].T.astype(bf16)
        rows = turned.shape[0] // CHAINS
        for h, out_ref in enumerate(out_refs):
            out_ref[m] = turned[h * rows : (h + 1) * rows]


def turn_field_kernel(shot_ref, state_hbm, prior_hbm, *rest):
    out_refs, (state, prior, sems) = rest[:CHAINS], rest[CHAINS:]
    half = state.shape[0]
    part = pl.ds(shot_ref[0] % 2 * half, half)
    copies = [
        pltpu.make_async_copy(state_hbm.at[part], state, sems.at[0]),
        pltpu.make_async_copy(prior_hbm.at[part], prior, sems.at[1]),
    ]
    for copy in copies:
        copy.start()
    for copy in copies:
        copy.wait()
    for i in range(half):
        turned = (state[i] + prior[i]).T
        rows = turned.shape[0] // CHAINS
        for h, out_ref in enumerate(out_refs):
            out_ref[i] = turned[h * rows : (h + 1) * rows]


def forward_kernel(shot_ref, bund, cblk, sens, own_ref, mate_ref, out_ref, acc, probe):
    half = own_ref.shape[0]
    core = shot_ref[0] % 2
    probe[pl.ds(core * half, half)] = own_ref[...]
    probe[pl.ds((1 - core) * half, half)] = mate_ref[...]
    acc[...] = jnp.zeros_like(acc)
    products(
        0,
        sens.shape[0],
        lambda k: lax.dot_general(
            probe[cblk[k]], sens[k], (((1,), (1,)), ((), ())), preferred_element_type=f32
        ),
        lambda k: bund[k],
        acc,
    )
    out_ref[...] = acc[...].astype(bf16)


def adjoint_kernel(shot_ref, bund, cblk, sens, resid, keep_ref, give_ref, acc):
    acc[...] = jnp.zeros_like(acc)
    products(
        0,
        sens.shape[0],
        lambda k: jnp.dot(resid[bund[k]], sens[k], preferred_element_type=f32),
        lambda k: cblk[k],
        acc,
    )
    half = keep_ref.shape[0]
    core = shot_ref[0] % 2
    keep_ref[...] = acc[pl.ds(core * half, half)]
    give_ref[...] = acc[pl.ds((1 - core) * half, half)].astype(bf16)


def pair_kernel(keep_ref, got_ref, out_ref):
    out_ref[...] = (keep_ref[...] + got_ref[...].astype(f32)).astype(bf16)


def residual_kernel(parts_ref, obs_ref, wt_ref, out_ref, *resid_ref):
    for i in range(parts_ref.shape[1]):
        total = parts_ref[0, i].astype(f32)
        for d in range(1, parts_ref.shape[0]):
            total += parts_ref[d, i].astype(f32)
        resid = wt_ref[pl.ds(i, 1), :] * (total - obs_ref[pl.ds(i, 1), :])
        if resid_ref:
            resid_ref[0][i] = resid
        rounded = resid.astype(bf16)
        for d in range(parts_ref.shape[0]):
            out_ref[d, i] = rounded


def turn_residual_kernel(*refs):
    in_refs, out_ref = refs[:-1], refs[-1]
    for i in range(out_ref.shape[0]):
        out_ref[i] = jnp.concatenate([in_ref[i] for in_ref in in_refs], axis=0).T


def sum_over_y(chip_y, part_refs, order, i):
    if len(part_refs) > 2:
        for d, part_ref in enumerate(part_refs):
            order[chip_y ^ d] = part_ref[i]
        parts = [order[y] for y in range(len(part_refs))]
    else:
        parts = [part_ref[i] for part_ref in part_refs]
    total = parts[0].astype(f32)
    for part in parts[1:]:
        total += part.astype(f32)
    return total


def probe_kernel(ny, shot_ref, field_ref, *rest):
    part_refs, (out_ref, grad_ref, order) = rest[:ny], rest[ny:]
    for i in range(out_ref.shape[0]):
        grad = sum_over_y(shot_ref[0] // 2, part_refs, order, i)
        grad_ref[i] = grad
        out_ref[i] = (field_ref[i] - 0.25 * grad).astype(bf16)


def total_kernel(ny, shot_ref, grad_ref, *rest):
    part_refs, (out_ref, order) = rest[:ny], rest[ny:]
    for i in range(out_ref.shape[0]):
        grad2 = sum_over_y(shot_ref[0] // 2, part_refs, order, i)
        out_ref[i] = (grad_ref[i] + grad2).astype(bf16)


def last_kernel(shot_ref, state, prior, *rest):
    own_refs, mate_refs, out_ref = rest[:CHAINS], rest[CHAINS : 2 * CHAINS], rest[2 * CHAINS]
    half = own_refs[0].shape[0]
    core = shot_ref[0] % 2
    for at, part_refs in ((core * half, own_refs), ((1 - core) * half, mate_refs)):
        for i in range(half):
            both = jnp.concatenate([part_ref[i] for part_ref in part_refs], axis=0)
            both = both.astype(f32).T
            out_ref[at + i] = state[at + i] + 0.5 * (prior[at + i] - 0.25 * both)


def per_device(nshot, nband, sens, bund, cblk, state, prior, observed, pick_weight):
    nblk = sens.shape[0]
    samples = state.shape[1]
    rows = samples // CHAINS
    owned, rays = observed.shape
    bundles = owned * nband
    cells = state.shape[0] // CBLK
    half = cells // 2
    ny = nshot // 2
    flops = 2 * nblk * rays * CBLK * samples
    sens_bytes = nblk * rays * CBLK * 2

    state_b = state.reshape(cells, CBLK, samples)
    prior_b = prior.reshape(cells, CBLK, samples)
    shot = lax.axis_index("shot").reshape(1)

    def other_core(array):
        return lax.ppermute(array, "shot", [(i, i ^ 1) for i in range(nshot)])

    def other_chips(array):
        return [array] + [
            lax.ppermute(array, "shot", [(i, i ^ (2 * d)) for i in range(nshot)])
            for d in range(1, ny)
        ]

    def over_band(array):
        return lax.all_to_all(array, "band", split_axis=0, concat_axis=0, tiled=True)

    both = range(CHAINS)
    half_bf16 = arr((half, rows, CBLK), bf16)
    half_f32 = arr((half, rows, CBLK), f32)
    half_field = pltpu.VMEM((half, CBLK, samples), f32)
    order = pltpu.VMEM((ny, rows, CBLK), bf16)

    def residual(part, name, keep):
        parts = over_band(part).reshape(nband, owned, rows, rays)
        outs = (arr((nband, owned, rows, rays), bf16),)
        if keep:
            outs += (arr((owned, rows, rays), f32),)
        copies, *resid = call(
            residual_kernel, outs, [], [VMEM] * 3, name, bytes_accessed=1 << 19
        )(parts, observed, pick_weight)
        return resid, over_band(copies).reshape(bundles, rows, rays)

    def adjoint(resid_all, name):
        keep, give = call(
            adjoint_kernel,
            (half_f32, half_bf16),
            [pltpu.VMEM((cells, rows, CBLK), f32)],
            [SMEM] * 3 + [VMEM] * 2,
            name,
            flops,
            sens_bytes,
        )(shot, bund, cblk, sens, resid_all)
        pair = call(
            pair_kernel, half_bf16, [], [VMEM] * 2, name + "_pair", bytes_accessed=1 << 19
        )(keep, other_core(give))
        return other_chips(pair)

    part1 = call(
        first_forward_kernel,
        tuple(arr((bundles, rows, rays), bf16) for _ in both),
        [
            pltpu.VMEM((bundles, rays, samples), f32),
            pltpu.VMEM((cells, CBLK, samples), bf16),
            pltpu.SMEM((nblk,), jnp.int32),
            pltpu.SMEM((nblk,), jnp.int32),
            pltpu.VMEM(sens.shape, bf16),
            pltpu.VMEM(state_b.shape, f32),
            pltpu.VMEM(state_b.shape, f32),
            pltpu.SemaphoreType.DMA((6 + CHUNKS,)),
        ],
        [HBM] * 5,
        "forward1",
        flops,
        sens_bytes,
        vmem=FIRST_VMEM,
    )(bund, cblk, sens, state_b, prior_b)
    field = call(
        turn_field_kernel,
        tuple(half_f32 for _ in both),
        [half_field, half_field, pltpu.SemaphoreType.DMA((2,))],
        [SMEM, HBM, HBM],
        "turn_field",
        bytes_accessed=2 << 20,
    )(shot, state_b, prior_b)

    resid2, total, grad1, part2, resid_all2 = [], [], [], [], []
    gparts1 = [adjoint(residual(part1[h], "residual1", False)[1], "adjoint1") for h in both]
    for h in both:
        probe_own, grad = call(
            functools.partial(probe_kernel, ny),
            (half_bf16, half_f32),
            [order],
            [SMEM] + [VMEM] * (1 + ny),
            "probe2",
            bytes_accessed=1 << 19,
        )(shot, field[h], *gparts1[h])
        grad1.append(grad)
        part2.append(
            call(
                forward_kernel,
                arr((bundles, rows, rays), bf16),
                [
                    pltpu.VMEM((bundles, rows, rays), f32),
                    pltpu.VMEM((cells, rows, CBLK), bf16),
                ],
                [SMEM] * 3 + [VMEM] * 3,
                "forward2",
                flops,
                sens_bytes,
            )(shot, bund, cblk, sens, probe_own, other_core(probe_own))
        )
    for h in both:
        (resid,), resid_all = residual(part2[h], "residual2", True)
        resid2.append(resid)
        gparts2 = adjoint(resid_all, "adjoint2")
        total.append(
            call(
                functools.partial(total_kernel, ny),
                half_bf16,
                [order],
                [SMEM] + [VMEM] * (1 + ny),
                "total",
                bytes_accessed=1 << 19,
            )(shot, grad1[h], *gparts2)
        )
    resid2 = call(
        turn_residual_kernel,
        arr((owned, rays, samples), f32),
        [],
        [VMEM] * CHAINS,
        "turn_residual",
        bytes_accessed=1 << 20,
    )(*resid2)
    new_state = call(
        last_kernel,
        arr((cells, CBLK, samples), f32),
        [],
        [SMEM] + [VMEM] * (2 + 2 * CHAINS),
        "new_state",
        bytes_accessed=4 << 20,
    )(shot, state_b, prior_b, *total, *[other_core(t) for t in total])
    return new_state.reshape(state.shape), resid2


def solution(mesh):
    in_specs = (
        P(("shot", "band"), None, None),
        P(("shot", "band")),
        P(("shot", "band")),
        P("band", None),
        P("band", None),
        P(("shot", "band"), None),
        P(("shot", "band"), None),
    )
    out_specs = (P("band", None), P(("shot", "band"), None, None))
    return jax.shard_map(
        functools.partial(per_device, mesh.shape["shot"], mesh.shape["band"]),
        mesh=mesh,
        in_specs=in_specs,
        out_specs=out_specs,
        check_vma=False,
    )
```

```python
import functools

import jax
import jax.numpy as jnp
from jax import lax
from jax.experimental import pallas as pl
from jax.experimental.pallas import tpu as pltpu
from jax.sharding import PartitionSpec as P

CBLK = 128
GROUP = 16
PAIRS = 4
CHUNKS = 4
FIRST_VMEM = 57 << 20

VMEM = pl.BlockSpec(memory_space=pltpu.VMEM)
SMEM = pl.BlockSpec(memory_space=pltpu.SMEM)
HBM = pl.BlockSpec(memory_space=pltpu.HBM)
ANY = pl.BlockSpec(memory_space=pl.ANY)

bf16, f32, i32 = jnp.bfloat16, jnp.float32, jnp.int32
arr = jax.ShapeDtypeStruct

BLOCK, OPERAND, TARGET, STEPS = range(4)


def call(body, outs, scratch, in_specs, name, flops=0, bytes_accessed=0, vmem=32 << 20, **more):
    if "out_specs" not in more:
        more["out_specs"] = jax.tree.map(lambda _: VMEM, outs)
    return pl.pallas_call(
        body,
        out_shape=outs,
        in_specs=in_specs,
        scratch_shapes=scratch,
        compiler_params=pltpu.CompilerParams(vmem_limit_bytes=vmem),
        cost_estimate=pl.CostEstimate(
            flops=flops, bytes_accessed=bytes_accessed, transcendentals=0
        ),
        name=name,
        **more,
    )


def region_of(nblk, bins):
    step = 2 * PAIRS
    return -(-(nblk + bins) // step) * step


def column(row):
    n = row.shape[1]
    eye = lax.broadcasted_iota(i32, (n, n), 0) == lax.broadcasted_iota(i32, (n, n), 1)
    return jnp.sum(jnp.where(eye, row, 0.0), axis=1, keepdims=True)


def make_plan(cls, bins, target, operand, empty, region, plan_ref):
    n, classes = cls.shape[1], len(empty)
    key = cls * bins + target
    key_c, cls_c = column(key), column(cls)
    row = lax.broadcasted_iota(i32, (n, n), 0)
    col = lax.broadcasted_iota(i32, (n, n), 1)
    before = jnp.sum(
        jnp.where((key_c == key) & (col < row), 1.0, 0.0), axis=1, keepdims=True
    )
    bin_of = lax.broadcasted_iota(i32, (n, classes * bins), 1).astype(f32)
    count = jnp.sum(jnp.where(bin_of == key_c, 1.0, 0.0), axis=0, keepdims=True)
    padded = 2.0 * jnp.floor((count + 1.0) * 0.5)
    start = jnp.sum(
        jnp.where((bin_of < key_c) & (bin_of >= cls_c * bins), padded, 0.0),
        axis=1,
        keepdims=True,
    )
    position = cls_c * region + start + before
    width = plan_ref.shape[1]
    entry = lax.broadcasted_iota(i32, (n, width), 1).astype(f32)
    hit = entry == position

    def placed(values):
        return jnp.sum(jnp.where(hit, values, 0.0), axis=0, keepdims=True)

    block = lax.broadcasted_iota(i32, (n, 1), 0).astype(f32)
    at = entry[0:1]
    vacant = jnp.zeros((1, width), f32)
    steps = jnp.zeros((1, width), f32)
    for c in range(classes):
        mine = (bin_of[0:1] >= c * bins) & (bin_of[0:1] < (c + 1) * bins)
        size = jnp.sum(jnp.where(mine, padded, 0.0), axis=1, keepdims=True)
        step = 2 * PAIRS
        vacant += jnp.where((at >= c * region) & (at < (c + 1) * region), float(empty[c]), 0.0)
        steps += jnp.where(at == c, jnp.floor((size + (step - 1)) * (1.0 / step)), 0.0)
    filled = placed(1.0)
    plan_ref[BLOCK : BLOCK + 1, :] = placed(block).astype(i32)
    plan_ref[OPERAND : OPERAND + 1, :] = (
        placed(column(operand)) + (1.0 - filled) * vacant
    ).astype(i32)
    plan_ref[TARGET : TARGET + 1, :] = placed(column(target)).astype(i32)
    plan_ref[STEPS : STEPS + 1, :] = steps.astype(i32)


def paired_products(plan, c, region, product_of, acc_ref):
    def group(g, carry):
        first = c * region + g * (2 * PAIRS)
        at = [first + 2 * j for j in range(PAIRS)]
        prods = [
            product_of(
                plan[BLOCK, p], plan[BLOCK, p + 1], plan[OPERAND, p], plan[OPERAND, p + 1]
            )
            for p in at
        ]
        for p, prod in zip(at, prods):
            acc_ref[plan[TARGET, p]] += prod
        return carry

    lax.fori_loop(0, plan[STEPS, c], group, 0)


def first_forward_kernel(
    shot_ref,
    bund_row,
    cblk_row,
    bund_hbm,
    cblk_hbm,
    sens_hbm,
    state_hbm,
    prior_hbm,
    out_ref,
    adjoint_plan,
    forward_plan,
    acc,
    probe,
    bund,
    cblk,
    sens,
    state,
    prior,
    sems,
):
    nblk = sens.shape[0]
    step = nblk // CHUNKS
    cells = state.shape[0]
    half, quarter = cells // 2, cells // 4
    bundles = acc.shape[0]
    small = [
        pltpu.make_async_copy(bund_hbm, bund, sems.at[0]),
        pltpu.make_async_copy(cblk_hbm, cblk, sems.at[1]),
    ]
    fields = []
    for h in range(2):
        part = pl.ds(h * half, half)
        fields.append(
            [
                pltpu.make_async_copy(state_hbm.at[part], state.at[part], sems.at[2 + 2 * h]),
                pltpu.make_async_copy(prior_hbm.at[part], prior.at[part], sems.at[3 + 2 * h]),
            ]
        )

    def block_copy(c):
        part = pl.ds(c * step, step)
        return pltpu.make_async_copy(sens_hbm.at[part], sens.at[part], sems.at[6 + c])

    for copy in small + fields[0] + fields[1] + [block_copy(c) for c in range(CHUNKS)]:
        copy.start()
    acc[...] = jnp.zeros_like(acc)

    core = (shot_ref[0] % 2).astype(f32)
    bundle, cell = bund_row[...].astype(f32), cblk_row[...].astype(f32)
    upper = jnp.where(cell >= half, 1.0, 0.0)
    kept = jnp.where(upper == core, 1.0, 0.0)
    in_half = cell - upper * half
    second = jnp.where(in_half >= quarter, 1.0, 0.0)
    in_quarter = in_half - second * quarter
    make_plan(
        2.0 * second + kept,
        quarter,
        in_quarter,
        bundle,
        [bundles] * 4,
        region_of(nblk, quarter),
        adjoint_plan,
    )
    late = (1.0 - kept) * second
    make_plan(
        late,
        bundles,
        bundle,
        jnp.where(late > 0.5, in_quarter, cell),
        [cells, quarter],
        region_of(nblk, bundles),
        forward_plan,
    )

    for h in range(2):
        part = pl.ds(h * half, half)
        for copy in fields[h]:
            copy.wait()
        probe[part] = (state[part] + 0.5 * prior[part]).astype(bf16)
    for copy in small:
        copy.wait()

    def chunk(c, carry):
        block_copy(c).wait()
        for g in range(step // GROUP):
            ks = [c * step + g * GROUP + j for j in range(GROUP)]
            prods = [
                jnp.dot(sens[k], probe[cblk[k]], preferred_element_type=f32) for k in ks
            ]
            for k, prod in zip(ks, prods):
                acc[bund[k]] += prod
        return carry

    lax.fori_loop(0, CHUNKS, chunk, 0)
    out_ref[...] = acc[...].astype(bf16)


def forward_pair(sens, probe):
    def product(k1, k2, c1, c2):
        return jnp.dot(
            jnp.concatenate([sens[k1], sens[k2]], axis=1),
            jnp.concatenate([probe[c1], probe[c2]], axis=0),
            preferred_element_type=f32,
        )

    return product


def early_forward_kernel(shot_ref, plan, sens, own_a, own_b, mate_a, acc, probe):
    cells = probe.shape[0] - 1
    half, quarter = cells // 2, cells // 4
    core = shot_ref[0] % 2
    own, mate = core * half, (1 - core) * half
    probe[pl.ds(own, quarter)] = own_a[...]
    probe[pl.ds(own + quarter, quarter)] = own_b[...]
    probe[pl.ds(mate, quarter)] = mate_a[...]
    probe[cells] = jnp.zeros_like(probe[cells])
    acc[...] = jnp.zeros_like(acc)
    region = region_of(sens.shape[0], acc.shape[0])
    paired_products(plan, 0, region, forward_pair(sens, probe), acc)


def late_forward_kernel(plan, sens, mate_b, early, out_ref, acc, probe):
    quarter = mate_b.shape[0]
    probe[pl.ds(0, quarter)] = mate_b[...]
    probe[quarter] = jnp.zeros_like(probe[quarter])
    acc[...] = early[...]
    region = region_of(sens.shape[0], acc.shape[0])
    paired_products(plan, 1, region, forward_pair(sens, probe), acc)
    out_ref[...] = acc[...].astype(bf16)


def adjoint_kernel(classes, plan, sens, resid_ref, *rest):
    out_refs, (acc, resid) = rest[: len(classes)], rest[len(classes) :]
    bundles = resid_ref.shape[0]
    resid[pl.ds(0, bundles)] = resid_ref[...]
    resid[bundles] = jnp.zeros_like(resid[bundles])
    region = region_of(sens.shape[0], acc.shape[0])

    def product(k1, k2, b1, b2):
        return jnp.dot(
            jnp.concatenate([resid[b1], resid[b2]], axis=1),
            jnp.concatenate([sens[k1], sens[k2]], axis=0),
            preferred_element_type=f32,
        )

    for c, out_ref in zip(classes, out_refs):
        acc[...] = jnp.zeros_like(acc)
        paired_products(plan, c, region, product, acc)
        out_ref[...] = acc[...].astype(out_ref.dtype)


def pair_kernel(keep_ref, got_ref, out_ref):
    out_ref[...] = (keep_ref[...] + got_ref[...].astype(f32)).astype(bf16)


def residual_kernel(parts_ref, obs_ref, wt_ref, out_ref, *resid_ref):
    for i in range(parts_ref.shape[1]):
        total = parts_ref[0, i].astype(f32)
        for d in range(1, parts_ref.shape[0]):
            total += parts_ref[d, i].astype(f32)
        resid = wt_ref[pl.ds(i, 1), :] * (total.T - obs_ref[pl.ds(i, 1), :])
        if resid_ref:
            resid_ref[0][i] = resid
        rounded = resid.astype(bf16)
        for d in range(parts_ref.shape[0]):
            out_ref[d, i] = rounded


def turn_kernel(in_ref, out_ref):
    for i in range(in_ref.shape[0]):
        out_ref[i] = in_ref[i].T


def prepare_kernel(shot_ref, state, prior, after_ref, field_a, field_b, base_ref):
    quarter = field_a.shape[0]
    own = shot_ref[0] % 2 * (2 * quarter)
    for at, field_ref in ((own, field_a), (own + quarter, field_b)):
        part = pl.ds(at, quarter)
        field_ref[...] = state[part] + prior[part]
    base_ref[...] = state[...] + 0.5 * prior[...]


def sum_over_y(chip_y, part_refs, order, i):
    if len(part_refs) > 2:
        for d, part_ref in enumerate(part_refs):
            order[chip_y ^ d] = part_ref[i]
        parts = [order[y] for y in range(len(part_refs))]
    else:
        parts = [part_ref[i] for part_ref in part_refs]
    total = parts[0].astype(f32)
    for part in parts[1:]:
        total += part.astype(f32)
    return total.T


def probe_kernel(ny, shot_ref, field_ref, *rest):
    part_refs, (out_ref, grad_ref, order) = rest[:ny], rest[ny:]
    for i in range(out_ref.shape[0]):
        grad = sum_over_y(shot_ref[0] // 2, part_refs, order, i)
        grad_ref[i] = grad
        out_ref[i] = (field_ref[i] - 0.25 * grad).astype(bf16)


def total_kernel(ny, shot_ref, grad_ref, *rest):
    part_refs, (out_ref, order) = rest[:ny], rest[ny:]
    for i in range(out_ref.shape[0]):
        grad2 = sum_over_y(shot_ref[0] // 2, part_refs, order, i)
        out_ref[i] = (grad_ref[i] + grad2).astype(bf16)


def early_update_kernel(shot_ref, base, own_a, own_b, mate_a, out_hbm, rest_ref, new, sems):
    quarter = own_a.shape[0]
    core = shot_ref[0] % 2
    own, mate = core * (2 * quarter), (1 - core) * (2 * quarter)
    copies = []
    for n, (at, part_ref) in enumerate(((own, own_a), (own + quarter, own_b), (mate, mate_a))):
        new[n] = base[pl.ds(at, quarter)] - 0.125 * part_ref[...].astype(f32)
        copies.append(
            pltpu.make_async_copy(new.at[n], out_hbm.at[pl.ds(at, quarter)], sems.at[n])
        )
        copies[-1].start()
    rest_ref[...] = base[pl.ds(mate + quarter, quarter)]
    for copy in copies:
        copy.wait()


def late_update_kernel(shot_ref, rest_ref, mate_b, so_far_hbm, out_hbm, new, sem):
    quarter = mate_b.shape[0]
    at = (1 - shot_ref[0] % 2) * (2 * quarter) + quarter
    new[...] = rest_ref[...] - 0.125 * mate_b[...].astype(f32)
    copy = pltpu.make_async_copy(new, out_hbm.at[pl.ds(at, quarter)], sem)
    copy.start()
    copy.wait()


def per_device(nshot, nband, sens, bund, cblk, state, prior, observed, pick_weight):
    nblk = sens.shape[0]
    samples = state.shape[1]
    owned, rays = observed.shape
    bundles = owned * nband
    cells = state.shape[0] // CBLK
    quarter = cells // 4
    ny = nshot // 2
    flops = 2 * nblk * rays * CBLK * samples
    sens_bytes = nblk * rays * CBLK * 2

    state_b = state.reshape(cells, CBLK, samples)
    prior_b = prior.reshape(cells, CBLK, samples)
    shot = lax.axis_index("shot").reshape(1)

    def other_core(array):
        return lax.ppermute(array, "shot", [(i, i ^ 1) for i in range(nshot)])

    def other_chips(array):
        return [array] + [
            lax.ppermute(array, "shot", [(i, i ^ (2 * d)) for i in range(nshot)])
            for d in range(1, ny)
        ]

    def over_band(array):
        return lax.all_to_all(array, "band", split_axis=0, concat_axis=0, tiled=True)

    part_out = arr((bundles, rays, samples), bf16)
    part_f32 = arr((bundles, rays, samples), f32)
    part_acc = pltpu.VMEM((bundles, rays, samples), f32)
    quarter_bf16 = arr((quarter, CBLK, samples), bf16)
    quarter_f32 = arr((quarter, CBLK, samples), f32)
    order = pltpu.VMEM((ny, samples, CBLK), bf16)

    def residual(part, name, keep):
        parts = over_band(part).reshape(nband, owned, rays, samples)
        outs = (arr((nband, owned, samples, rays), bf16),)
        if keep:
            outs += (arr((owned, samples, rays), f32),)
        copies, *resid = call(
            residual_kernel, outs, [], [VMEM] * 3, name, bytes_accessed=1 << 20
        )(parts, observed, pick_weight)
        return resid, over_band(copies).reshape(bundles, samples, rays)

    def adjoint(plan, resid_all, name):
        def kernel(classes, part):
            return call(
                functools.partial(adjoint_kernel, classes),
                tuple(quarter_f32 if c % 2 else quarter_bf16 for c in classes),
                [
                    pltpu.VMEM((quarter, samples, CBLK), f32),
                    pltpu.VMEM((bundles + 1, samples, rays), bf16),
                ],
                [SMEM] + [VMEM] * 2,
                name + part,
                flops * len(classes) // 4,
                sens_bytes * len(classes) // 4,
            )(plan, sens, resid_all)

        def pair(keep, got, part):
            return call(
                pair_kernel,
                quarter_bf16,
                [],
                [VMEM] * 2,
                name + "_pair" + part,
                bytes_accessed=1 << 19,
            )(keep, got)

        (give_a,) = kernel((0,), "_give_a")
        got_a = other_core(give_a)
        keep_a, give_b = kernel((1, 2), "_keep_a")
        got_b = other_core(give_b)
        sums_a = other_chips(pair(keep_a, got_a, "_a"))
        (keep_b,) = kernel((3,), "_keep_b")
        sums_b = other_chips(pair(keep_b, got_b, "_b"))
        return sums_a, sums_b, keep_b

    part1, adjoint_plan, forward_plan = call(
        first_forward_kernel,
        (
            part_out,
            arr((4, 4 * region_of(nblk, quarter)), i32),
            arr((4, 2 * region_of(nblk, bundles)), i32),
        ),
        [
            part_acc,
            pltpu.VMEM((cells, CBLK, samples), bf16),
            pltpu.SMEM((nblk,), i32),
            pltpu.SMEM((nblk,), i32),
            pltpu.VMEM(sens.shape, bf16),
            pltpu.VMEM(state_b.shape, f32),
            pltpu.VMEM(state_b.shape, f32),
            pltpu.SemaphoreType.DMA((6 + CHUNKS,)),
        ],
        [SMEM, VMEM, VMEM] + [HBM] * 5,
        "forward1",
        flops,
        sens_bytes,
        vmem=FIRST_VMEM,
    )(shot, bund.reshape(1, nblk), cblk.reshape(1, nblk), bund, cblk, sens, state_b, prior_b)
    _, resid_all1 = residual(part1, "residual1", False)
    *sums1, after = adjoint(adjoint_plan, resid_all1, "adjoint1")

    *fields, base = call(
        prepare_kernel,
        (quarter_f32, quarter_f32, arr((cells, CBLK, samples), f32)),
        [],
        [SMEM, VMEM, VMEM, ANY],
        "prepare",
        bytes_accessed=4 << 20,
    )(shot, state_b, prior_b, after)
    own, grad1, mate = [], [], []
    for field, sums, part in zip(fields, sums1, "ab"):
        probe, grad = call(
            functools.partial(probe_kernel, ny),
            (quarter_bf16, quarter_f32),
            [order],
            [SMEM] + [VMEM] * (1 + ny),
            "probe2_" + part,
            bytes_accessed=1 << 19,
        )(shot, field, *sums)
        own.append(probe)
        grad1.append(grad)
        mate.append(other_core(probe))

    early = call(
        early_forward_kernel,
        part_f32,
        [pltpu.VMEM((cells + 1, CBLK, samples), bf16)],
        [SMEM] * 2 + [VMEM] * 4,
        "forward2_early",
        flops * 3 // 4,
        sens_bytes * 3 // 4,
    )(shot, forward_plan, sens, own[0], own[1], mate[0])
    part2 = call(
        late_forward_kernel,
        part_out,
        [part_acc, pltpu.VMEM((quarter + 1, CBLK, samples), bf16)],
        [SMEM] + [VMEM] * 3,
        "forward2_late",
        flops // 4,
        sens_bytes // 4,
    )(forward_plan, sens, mate[1], early)

    (resid2_t,), resid_all2 = residual(part2, "residual2", True)
    *sums2, _ = adjoint(adjoint_plan, resid_all2, "adjoint2")
    resid2 = call(
        turn_kernel,
        arr((owned, rays, samples), f32),
        [],
        [VMEM],
        "turn",
        bytes_accessed=1 << 20,
    )(resid2_t)
    own, mate = [], []
    for grad, sums, part in zip(grad1, sums2, "ab"):
        total = call(
            functools.partial(total_kernel, ny),
            quarter_bf16,
            [order],
            [SMEM] + [VMEM] * (1 + ny),
            "total_" + part,
            bytes_accessed=1 << 19,
        )(shot, grad, *sums)
        own.append(total)
        mate.append(other_core(total))
    whole = arr((cells, CBLK, samples), f32)
    so_far, rest = call(
        early_update_kernel,
        (whole, quarter_f32),
        [pltpu.VMEM((3, quarter, CBLK, samples), f32), pltpu.SemaphoreType.DMA((3,))],
        [SMEM] + [VMEM] * 4,
        "new_state_early",
        bytes_accessed=3 << 20,
        out_specs=(HBM, VMEM),
    )(shot, base, own[0], own[1], mate[0])
    new_state = call(
        late_update_kernel,
        whole,
        [pltpu.VMEM((quarter, CBLK, samples), f32), pltpu.SemaphoreType.DMA],
        [SMEM, VMEM, VMEM, HBM],
        "new_state_late",
        bytes_accessed=1 << 20,
        out_specs=HBM,
        input_output_aliases={3: 0},
    )(shot, rest, mate[1], so_far)
    return new_state.reshape(state.shape), resid2


def solution(mesh):
    in_specs = (
        P(("shot", "band"), None, None),
        P(("shot", "band")),
        P(("shot", "band")),
        P("band", None),
        P("band", None),
        P(("shot", "band"), None),
        P(("shot", "band"), None),
    )
    out_specs = (P("band", None), P(("shot", "band"), None, None))
    return jax.shard_map(
        functools.partial(per_device, mesh.shape["shot"], mesh.shape["band"]),
        mesh=mesh,
        in_specs=in_specs,
        out_specs=out_specs,
        check_vma=False,
    )
```

```python
import functools

import jax
import jax.numpy as jnp
from jax import lax
from jax.experimental import pallas as pl
from jax.experimental.pallas import tpu as pltpu
from jax.sharding import PartitionSpec as P

CBLK = 128
GROUP = 16
PAIRS = 16
CHUNKS = 4
FIRST_VMEM = 55 << 20

VMEM = pl.BlockSpec(memory_space=pltpu.VMEM)
SMEM = pl.BlockSpec(memory_space=pltpu.SMEM)
HBM = pl.BlockSpec(memory_space=pltpu.HBM)
ANY = pl.BlockSpec(memory_space=pl.ANY)

bf16, f32, i32 = jnp.bfloat16, jnp.float32, jnp.int32
arr = jax.ShapeDtypeStruct

BASE = 256


def call(body, outs, scratch, in_specs, name, flops=0, bytes_accessed=0, vmem=32 << 20, **more):
    if "out_specs" not in more:
        more["out_specs"] = jax.tree.map(lambda _: VMEM, outs)
    return pl.pallas_call(
        body,
        out_shape=outs,
        in_specs=in_specs,
        scratch_shapes=scratch,
        compiler_params=pltpu.CompilerParams(vmem_limit_bytes=vmem),
        cost_estimate=pl.CostEstimate(
            flops=flops, bytes_accessed=bytes_accessed, transcendentals=0
        ),
        name=name,
        **more,
    )


def region_of(nblk, bins):
    step = 2 * PAIRS
    return -(-(nblk + bins) // step) * step


def column(row):
    n = row.shape[1]
    eye = lax.broadcasted_iota(i32, (n, n), 0) == lax.broadcasted_iota(i32, (n, n), 1)
    return jnp.sum(jnp.where(eye, row, 0.0), axis=1, keepdims=True)


def make_plan(cls, bins, target, operand, empty, region, plan_ref):
    n, classes = cls.shape[1], len(empty)
    key = cls * bins + target
    key_c, cls_c = column(key), column(cls)
    row = lax.broadcasted_iota(i32, (n, n), 0)
    col = lax.broadcasted_iota(i32, (n, n), 1)
    before = jnp.sum(
        jnp.where((key_c == key) & (col < row), 1.0, 0.0), axis=1, keepdims=True
    )
    bin_of = lax.broadcasted_iota(i32, (n, classes * bins), 1).astype(f32)
    count = jnp.sum(jnp.where(bin_of == key_c, 1.0, 0.0), axis=0, keepdims=True)
    padded = 2.0 * jnp.floor((count + 1.0) * 0.5)
    start = jnp.sum(
        jnp.where((bin_of < key_c) & (bin_of >= cls_c * bins), padded, 0.0),
        axis=1,
        keepdims=True,
    )
    position = cls_c * region + start + before
    width = plan_ref.shape[1]
    entry = lax.broadcasted_iota(i32, (n, width), 1).astype(f32)
    hit = entry == position

    def placed(values):
        return jnp.sum(jnp.where(hit, values, 0.0), axis=0, keepdims=True)

    block = lax.broadcasted_iota(i32, (n, 1), 0).astype(f32)
    at = entry[0:1]
    vacant = jnp.zeros((1, width), f32)
    steps = jnp.zeros((1, width), f32)
    for c in range(classes):
        mine = (bin_of[0:1] >= c * bins) & (bin_of[0:1] < (c + 1) * bins)
        size = jnp.sum(jnp.where(mine, padded, 0.0), axis=1, keepdims=True)
        step = 2 * PAIRS
        vacant += jnp.where((at >= c * region) & (at < (c + 1) * region), float(empty[c]), 0.0)
        steps += jnp.where(at == classes * region + c, jnp.floor((size + (step - 1)) * (1.0 / step)), 0.0)
    word = block + BASE * (column(operand) + BASE * column(target))
    plan = placed(word) + (1.0 - placed(1.0)) * (BASE * vacant) + steps
    plan_ref[...] = plan.astype(i32)


def paired_products(plan, classes, c, region, product_of, acc_ref):
    def group(g, carry):
        first = c * region + g * (2 * PAIRS)
        prods, targets = [], []
        for j in range(PAIRS):
            one, two = plan[0, first + 2 * j], plan[0, first + 2 * j + 1]
            k1, k2 = one & (BASE - 1), two & (BASE - 1)
            rest1, rest2 = one // BASE, two // BASE
            prods.append(product_of(k1, k2, rest1 & (BASE - 1), rest2 & (BASE - 1)))
            targets.append(rest1 // BASE)
        for target, prod in zip(targets, prods):
            acc_ref[target] += prod
        return carry

    lax.fori_loop(0, plan[0, classes * region + c], group, 0)


def first_forward_kernel(
    bund_row_hbm,
    cblk_row_hbm,
    bund_hbm,
    cblk_hbm,
    sens_hbm,
    state_hbm,
    prior_hbm,
    out_ref,
    adjoint_plan,
    forward_plan,
    acc,
    probe,
    bund,
    cblk,
    sens,
    state,
    prior,
    bund_row,
    cblk_row,
    sems,
):
    nblk = sens.shape[0]
    step = nblk // CHUNKS
    cells = state.shape[0]
    half, quarter = cells // 2, cells // 4
    bundles = acc.shape[0]
    small = [
        pltpu.make_async_copy(bund_hbm, bund, sems.at[0]),
        pltpu.make_async_copy(cblk_hbm, cblk, sems.at[1]),
    ]
    rows = [
        pltpu.make_async_copy(bund_row_hbm, bund_row, sems.at[6 + CHUNKS]),
        pltpu.make_async_copy(cblk_row_hbm, cblk_row, sems.at[7 + CHUNKS]),
    ]
    fields = []
    for h in range(2):
        part = pl.ds(h * half, half)
        fields.append(
            [
                pltpu.make_async_copy(state_hbm.at[part], state.at[part], sems.at[2 + 2 * h]),
                pltpu.make_async_copy(prior_hbm.at[part], prior.at[part], sems.at[3 + 2 * h]),
            ]
        )

    def block_copy(c):
        part = pl.ds(c * step, step)
        return pltpu.make_async_copy(sens_hbm.at[part], sens.at[part], sems.at[6 + c])

    for copy in rows + small + fields[0] + fields[1] + [block_copy(c) for c in range(CHUNKS)]:
        copy.start()
    acc[...] = jnp.zeros_like(acc)

    for copy in rows:
        copy.wait()
    core = (lax.axis_index("shot") % 2).astype(f32)
    bundle, cell = bund_row[...].astype(f32), cblk_row[...].astype(f32)
    upper = jnp.where(cell >= half, 1.0, 0.0)
    kept = jnp.where(upper == core, 1.0, 0.0)
    in_half = cell - upper * half
    second = jnp.where(in_half >= quarter, 1.0, 0.0)
    in_quarter = in_half - second * quarter
    make_plan(
        2.0 * second + kept,
        quarter,
        in_quarter,
        bundle,
        [bundles] * 4,
        region_of(nblk, quarter),
        adjoint_plan,
    )
    late = (1.0 - kept) * second
    make_plan(
        late,
        bundles,
        bundle,
        jnp.where(late > 0.5, in_quarter, cell),
        [cells, quarter],
        region_of(nblk, bundles),
        forward_plan,
    )

    for h in range(2):
        part = pl.ds(h * half, half)
        for copy in fields[h]:
            copy.wait()
        probe[part] = (state[part] + 0.5 * prior[part]).astype(bf16)
    for copy in small:
        copy.wait()

    def chunk(c, carry):
        block_copy(c).wait()
        for g in range(step // GROUP):
            ks = [c * step + g * GROUP + j for j in range(GROUP)]
            prods = [
                jnp.dot(sens[k], probe[cblk[k]], preferred_element_type=f32) for k in ks
            ]
            for k, prod in zip(ks, prods):
                acc[bund[k]] += prod
        return carry

    lax.fori_loop(0, CHUNKS, chunk, 0)
    out_ref[...] = acc[...].astype(bf16)


def forward_pair(sens, probe):
    def product(k1, k2, c1, c2):
        return jnp.dot(
            jnp.concatenate([sens[k1], sens[k2]], axis=1),
            jnp.concatenate([probe[c1], probe[c2]], axis=0),
            preferred_element_type=f32,
        )

    return product


def early_forward_kernel(plan, sens, own_a, own_b, mate_a, acc, probe):
    cells = probe.shape[0] - 1
    half, quarter = cells // 2, cells // 4
    core = lax.axis_index("shot") % 2
    own, mate = core * half, (1 - core) * half
    probe[pl.ds(own, quarter)] = own_a[...]
    probe[pl.ds(own + quarter, quarter)] = own_b[...]
    probe[pl.ds(mate, quarter)] = mate_a[...]
    probe[cells] = jnp.zeros_like(probe[cells])
    acc[...] = jnp.zeros_like(acc)
    region = region_of(sens.shape[0], acc.shape[0])
    paired_products(plan, 2, 0, region, forward_pair(sens, probe), acc)


def late_forward_kernel(plan, sens, mate_b, early, out_ref, acc, probe):
    quarter = mate_b.shape[0]
    probe[pl.ds(0, quarter)] = mate_b[...]
    probe[quarter] = jnp.zeros_like(probe[quarter])
    acc[...] = early[...]
    region = region_of(sens.shape[0], acc.shape[0])
    paired_products(plan, 2, 1, region, forward_pair(sens, probe), acc)
    out_ref[...] = acc[...].astype(bf16)


def adjoint_kernel(classes, plan, sens, resid_ref, *rest):
    out_refs, (acc, resid) = rest[: len(classes)], rest[len(classes) :]
    bundles = resid_ref.shape[0]
    resid[pl.ds(0, bundles)] = resid_ref[...]
    resid[bundles] = jnp.zeros_like(resid[bundles])
    region = region_of(sens.shape[0], acc.shape[0])

    def product(k1, k2, b1, b2):
        return jnp.dot(
            jnp.concatenate([resid[b1], resid[b2]], axis=1),
            jnp.concatenate([sens[k1], sens[k2]], axis=0),
            preferred_element_type=f32,
        )

    for c, out_ref in zip(classes, out_refs):
        acc[...] = jnp.zeros_like(acc)
        paired_products(plan, 4, c, region, product, acc)
        out_ref[...] = acc[...].astype(out_ref.dtype)


def pair_kernel(keep_ref, got_ref, out_ref):
    out_ref[...] = (keep_ref[...] + got_ref[...].astype(f32)).astype(bf16)


def residual_kernel(parts_ref, obs_ref, wt_ref, out_ref, *resid_ref):
    for i in range(parts_ref.shape[1]):
        total = parts_ref[0, i].astype(f32)
        for d in range(1, parts_ref.shape[0]):
            total += parts_ref[d, i].astype(f32)
        resid = wt_ref[pl.ds(i, 1), :] * (total.T - obs_ref[pl.ds(i, 1), :])
        if resid_ref:
            resid_ref[0][i] = resid
        rounded = resid.astype(bf16)
        for d in range(parts_ref.shape[0]):
            out_ref[d, i] = rounded


def turn_kernel(in_ref, out_ref):
    for i in range(in_ref.shape[0]):
        out_ref[i] = in_ref[i].T


def prepare_kernel(state, prior, after_ref, field_a, field_b, base_ref):
    quarter = field_a.shape[0]
    own = lax.axis_index("shot") % 2 * (2 * quarter)
    for at, field_ref in ((own, field_a), (own + quarter, field_b)):
        part = pl.ds(at, quarter)
        field_ref[...] = state[part] + prior[part]
    base_ref[...] = state[...] + 0.5 * prior[...]


def sum_over_y(chip_y, part_refs, order, i):
    if len(part_refs) > 2:
        for d, part_ref in enumerate(part_refs):
            order[chip_y ^ d] = part_ref[i]
        parts = [order[y] for y in range(len(part_refs))]
    else:
        parts = [part_ref[i] for part_ref in part_refs]
    total = parts[0].astype(f32)
    for part in parts[1:]:
        total += part.astype(f32)
    return total.T


def probe_kernel(ny, field_ref, *rest):
    part_refs, (out_ref, grad_ref, order) = rest[:ny], rest[ny:]
    for i in range(out_ref.shape[0]):
        grad = sum_over_y(lax.axis_index("shot") // 2, part_refs, order, i)
        grad_ref[i] = grad
        out_ref[i] = (field_ref[i] - 0.25 * grad).astype(bf16)


def total_kernel(ny, grad_ref, after_ref, *rest):
    part_refs, (out_ref, order) = rest[:ny], rest[ny:]
    for i in range(out_ref.shape[0]):
        grad2 = sum_over_y(lax.axis_index("shot") // 2, part_refs, order, i)
        out_ref[i] = (grad_ref[i] + grad2).astype(bf16)


def early_update_kernel(base, own_a, own_b, mate_a, out_hbm, rest_ref, new, sems):
    quarter = own_a.shape[0]
    core = lax.axis_index("shot") % 2
    own, mate = core * (2 * quarter), (1 - core) * (2 * quarter)
    copies = []
    for n, (at, part_ref) in enumerate(((own, own_a), (own + quarter, own_b), (mate, mate_a))):
        new[n] = base[pl.ds(at, quarter)] - 0.125 * part_ref[...].astype(f32)
        copies.append(
            pltpu.make_async_copy(new.at[n], out_hbm.at[pl.ds(at, quarter)], sems.at[n])
        )
        copies[-1].start()
    rest_ref[...] = base[pl.ds(mate + quarter, quarter)]
    for copy in copies:
        copy.wait()


def late_update_kernel(rest_ref, mate_b, so_far_hbm, out_hbm, new, sem):
    quarter = mate_b.shape[0]
    at = (1 - lax.axis_index("shot") % 2) * (2 * quarter) + quarter
    new[...] = rest_ref[...] - 0.125 * mate_b[...].astype(f32)
    copy = pltpu.make_async_copy(new, out_hbm.at[pl.ds(at, quarter)], sem)
    copy.start()
    copy.wait()


def per_device(nshot, nband, sens, bund, cblk, state, prior, observed, pick_weight):
    nblk = sens.shape[0]
    samples = state.shape[1]
    owned, rays = observed.shape
    bundles = owned * nband
    cells = state.shape[0] // CBLK
    quarter = cells // 4
    ny = nshot // 2
    flops = 2 * nblk * rays * CBLK * samples
    sens_bytes = nblk * rays * CBLK * 2

    state_b = state.reshape(cells, CBLK, samples)
    prior_b = prior.reshape(cells, CBLK, samples)

    def other_core(array):
        return lax.ppermute(array, "shot", [(i, i ^ 1) for i in range(nshot)])

    def other_chips(array):
        return [array] + [
            lax.ppermute(array, "shot", [(i, i ^ (2 * d)) for i in range(nshot)])
            for d in range(1, ny)
        ]

    def over_band(array):
        return lax.all_to_all(array, "band", split_axis=0, concat_axis=0, tiled=True)

    part_out = arr((bundles, rays, samples), bf16)
    part_f32 = arr((bundles, rays, samples), f32)
    part_acc = pltpu.VMEM((bundles, rays, samples), f32)
    quarter_bf16 = arr((quarter, CBLK, samples), bf16)
    quarter_f32 = arr((quarter, CBLK, samples), f32)
    order = pltpu.VMEM((ny, samples, CBLK), bf16)

    def residual(part, name, keep):
        parts = over_band(part).reshape(nband, owned, rays, samples)
        outs = (arr((nband, owned, samples, rays), bf16),)
        if keep:
            outs += (arr((owned, samples, rays), f32),)
        copies, *resid = call(
            residual_kernel, outs, [], [VMEM] * 3, name, bytes_accessed=1 << 20
        )(parts, observed, pick_weight)
        return resid, over_band(copies).reshape(bundles, samples, rays)

    def adjoint(plan, resid_all, name):
        def kernel(classes, part):
            return call(
                functools.partial(adjoint_kernel, classes),
                tuple(quarter_f32 if c % 2 else quarter_bf16 for c in classes),
                [
                    pltpu.VMEM((quarter, samples, CBLK), f32),
                    pltpu.VMEM((bundles + 1, samples, rays), bf16),
                ],
                [SMEM] + [VMEM] * 2,
                name + part,
                flops * len(classes) // 4,
                sens_bytes * len(classes) // 4,
            )(plan, sens, resid_all)

        def pair(keep, got, part):
            return call(
                pair_kernel,
                quarter_bf16,
                [],
                [VMEM] * 2,
                name + "_pair" + part,
                bytes_accessed=1 << 19,
            )(keep, got)

        (give_a,) = kernel((0,), "_give_a")
        got_a = other_core(give_a)
        keep_a, give_b = kernel((1, 2), "_keep_a")
        got_b = other_core(give_b)
        sums_a = other_chips(pair(keep_a, got_a, "_a"))
        (keep_b,) = kernel((3,), "_keep_b")
        sums_b = other_chips(pair(keep_b, got_b, "_b"))
        return sums_a, sums_b, keep_b

    part1, adjoint_plan, forward_plan = call(
        first_forward_kernel,
        (
            part_out,
            arr((1, 4 * region_of(nblk, quarter) + 4), i32),
            arr((1, 2 * region_of(nblk, bundles) + 2), i32),
        ),
        [
            part_acc,
            pltpu.VMEM((cells, CBLK, samples), bf16),
            pltpu.SMEM((nblk,), i32),
            pltpu.SMEM((nblk,), i32),
            pltpu.VMEM(sens.shape, bf16),
            pltpu.VMEM(state_b.shape, f32),
            pltpu.VMEM(state_b.shape, f32),
            pltpu.VMEM((1, nblk), i32),
            pltpu.VMEM((1, nblk), i32),
            pltpu.SemaphoreType.DMA((8 + CHUNKS,)),
        ],
        [HBM] * 7,
        "forward1",
        flops,
        sens_bytes,
        vmem=FIRST_VMEM,
    )(bund.reshape(1, nblk), cblk.reshape(1, nblk), bund, cblk, sens, state_b, prior_b)
    _, resid_all1 = residual(part1, "residual1", False)
    *sums1, after = adjoint(adjoint_plan, resid_all1, "adjoint1")

    *fields, base = call(
        prepare_kernel,
        (quarter_f32, quarter_f32, arr((cells, CBLK, samples), f32)),
        [],
        [VMEM, VMEM, ANY],
        "prepare",
        bytes_accessed=4 << 20,
    )(state_b, prior_b, after)
    own, grad1, mate = [], [], []
    for field, sums, part in zip(fields, sums1, "ab"):
        probe, grad = call(
            functools.partial(probe_kernel, ny),
            (quarter_bf16, quarter_f32),
            [order],
            [VMEM] * (1 + ny),
            "probe2_" + part,
            bytes_accessed=1 << 19,
        )(field, *sums)
        own.append(probe)
        grad1.append(grad)
        mate.append(other_core(probe))

    early = call(
        early_forward_kernel,
        part_f32,
        [pltpu.VMEM((cells + 1, CBLK, samples), bf16)],
        [SMEM] + [VMEM] * 4,
        "forward2_early",
        flops * 3 // 4,
        sens_bytes * 3 // 4,
    )(forward_plan, sens, own[0], own[1], mate[0])
    part2 = call(
        late_forward_kernel,
        part_out,
        [part_acc, pltpu.VMEM((quarter + 1, CBLK, samples), bf16)],
        [SMEM] + [VMEM] * 3,
        "forward2_late",
        flops // 4,
        sens_bytes // 4,
    )(forward_plan, sens, mate[1], early)

    (resid2_t,), resid_all2 = residual(part2, "residual2", True)
    *sums2, _ = adjoint(adjoint_plan, resid_all2, "adjoint2")
    resid2 = call(
        turn_kernel,
        arr((owned, rays, samples), f32),
        [],
        [VMEM],
        "turn",
        bytes_accessed=1 << 20,
    )(resid2_t)
    own, mate, after = [], [], resid2
    for grad, sums, part in zip(grad1, sums2, "ab"):
        total = call(
            functools.partial(total_kernel, ny),
            quarter_bf16,
            [order],
            [VMEM, ANY] + [VMEM] * ny,
            "total_" + part,
            bytes_accessed=1 << 19,
        )(grad, after, *sums)
        own.append(total)
        after = grad
        mate.append(other_core(total))
    whole = arr((cells, CBLK, samples), f32)
    so_far, rest = call(
        early_update_kernel,
        (whole, quarter_f32),
        [pltpu.VMEM((3, quarter, CBLK, samples), f32), pltpu.SemaphoreType.DMA((3,))],
        [VMEM] * 4,
        "new_state_early",
        bytes_accessed=3 << 20,
        out_specs=(HBM, VMEM),
    )(base, own[0], own[1], mate[0])
    new_state = call(
        late_update_kernel,
        whole,
        [pltpu.VMEM((quarter, CBLK, samples), f32), pltpu.SemaphoreType.DMA],
        [VMEM, VMEM, HBM],
        "new_state_late",
        bytes_accessed=1 << 20,
        out_specs=HBM,
        input_output_aliases={2: 0},
    )(rest, mate[1], so_far)
    return new_state.reshape(state.shape), resid2


def solution(mesh):
    in_specs = (
        P(("shot", "band"), None, None),
        P(("shot", "band")),
        P(("shot", "band")),
        P("band", None),
        P("band", None),
        P(("shot", "band"), None),
        P(("shot", "band"), None),
    )
    out_specs = (P("band", None), P(("shot", "band"), None, None))
    return jax.shard_map(
        functools.partial(per_device, mesh.shape["shot"], mesh.shape["band"]),
        mesh=mesh,
        in_specs=in_specs,
        out_specs=out_specs,
        check_vma=False,
    )
```

```python
import functools

import jax
import jax.numpy as jnp
from jax import lax
from jax.experimental import pallas as pl
from jax.experimental.pallas import tpu as pltpu
from jax.sharding import PartitionSpec as P

CBLK = 128
GROUP = 16
CHUNKS = 4
FIRST_VMEM = 55 << 20

VMEM = pl.BlockSpec(memory_space=pltpu.VMEM)
SMEM = pl.BlockSpec(memory_space=pltpu.SMEM)
HBM = pl.BlockSpec(memory_space=pltpu.HBM)
ANY = pl.BlockSpec(memory_space=pl.ANY)

bf16, f32, i32 = jnp.bfloat16, jnp.float32, jnp.int32
arr = jax.ShapeDtypeStruct

def call(body, outs, scratch, in_specs, name, flops=0, bytes_accessed=0, vmem=32 << 20, **more):
    if "out_specs" not in more:
        more["out_specs"] = jax.tree.map(lambda _: VMEM, outs)
    return pl.pallas_call(
        body,
        out_shape=outs,
        in_specs=in_specs,
        scratch_shapes=scratch,
        compiler_params=pltpu.CompilerParams(vmem_limit_bytes=vmem),
        cost_estimate=pl.CostEstimate(
            flops=flops, bytes_accessed=bytes_accessed, transcendentals=0
        ),
        name=name,
        **more,
    )


def first_forward_kernel(
    bund_hbm,
    cblk_hbm,
    sens_hbm,
    state_hbm,
    prior_hbm,
    out_ref,
    acc,
    probe,
    bund,
    cblk,
    sens,
    state,
    prior,
    sems,
):
    nblk = sens.shape[0]
    step = nblk // CHUNKS
    cells = state.shape[0]
    half = cells // 2
    small = [
        pltpu.make_async_copy(bund_hbm, bund, sems.at[0]),
        pltpu.make_async_copy(cblk_hbm, cblk, sems.at[1]),
    ]
    fields = []
    for h in range(2):
        part = pl.ds(h * half, half)
        fields.append(
            [
                pltpu.make_async_copy(state_hbm.at[part], state.at[part], sems.at[2 + 2 * h]),
                pltpu.make_async_copy(prior_hbm.at[part], prior.at[part], sems.at[3 + 2 * h]),
            ]
        )

    def block_copy(c):
        part = pl.ds(c * step, step)
        return pltpu.make_async_copy(sens_hbm.at[part], sens.at[part], sems.at[6 + c])

    for copy in small + fields[0] + fields[1] + [block_copy(c) for c in range(CHUNKS)]:
        copy.start()
    acc[...] = jnp.zeros_like(acc)

    for h in range(2):
        part = pl.ds(h * half, half)
        for copy in fields[h]:
            copy.wait()
        probe[part] = (state[part] + 0.5 * prior[part]).astype(bf16)
    for copy in small:
        copy.wait()

    def chunk(c, carry):
        block_copy(c).wait()
        for g in range(step // GROUP):
            ks = [c * step + g * GROUP + j for j in range(GROUP)]
            prods = [
                jnp.dot(sens[k], probe[cblk[k]], preferred_element_type=f32) for k in ks
            ]
            for k, prod in zip(ks, prods):
                acc[bund[k]] += prod
        return carry

    lax.fori_loop(0, CHUNKS, chunk, 0)
    out_ref[...] = acc[...].astype(bf16)


def dense_kernel(bund, cblk, sens, after_ref, out_ref, token_ref, total):
    rays = sens.shape[1]
    total[...] = jnp.zeros_like(total)

    def place(k, carry):
        rows = pl.ds(pl.multiple_of(bund[k] * rays, rays), rays)
        lanes = pl.ds(pl.multiple_of(cblk[k] % 2 * CBLK, CBLK), CBLK)
        total[cblk[k] // 2, rows, lanes] += sens[k].astype(f32)
        return carry

    lax.fori_loop(0, sens.shape[0], place, 0)
    for i in range(total.shape[0]):
        out_ref[i] = total[i].astype(bf16)
    token_ref[...] = jnp.zeros_like(token_ref)


def dense_forward(dense, columns, start_of, store):
    step = 2 * CBLK
    probe = jnp.concatenate([part for _, part in columns], axis=0)
    for m in range(dense.shape[1] // step):
        rows = pl.ds(m * step, step)
        lhs = jnp.concatenate([dense[pair, rows, :] for pair, _ in columns], axis=1)
        total = jnp.dot(lhs, probe, preferred_element_type=f32)
        store(m, start_of(m, total.reshape(2, CBLK, -1)))


def columns_of(first, part_ref):
    return [
        (first + j, part_ref[pl.ds(2 * j, 2)].reshape(2 * CBLK, -1))
        for j in range(part_ref.shape[0] // 2)
    ]


def early_forward_kernel(dense, own_a, own_b, mate_a, acc):
    half, quarter = dense.shape[0] // 2, dense.shape[0] // 4
    core = lax.axis_index("shot") % 2
    own, mate = core * half, (1 - core) * half
    columns = columns_of(own, own_a) + columns_of(own + quarter, own_b) + columns_of(mate, mate_a)

    def store(m, value):
        acc[pl.ds(2 * m, 2)] = value

    dense_forward(dense, columns, lambda m, value: value, store)


def late_forward_kernel(dense, mate_b, early, out_ref):
    half, quarter = dense.shape[0] // 2, dense.shape[0] // 4
    core = lax.axis_index("shot") % 2

    def store(m, value):
        out_ref[pl.ds(2 * m, 2)] = value.astype(bf16)

    dense_forward(
        dense,
        columns_of((1 - core) * half + quarter, mate_b),
        lambda m, value: early[pl.ds(2 * m, 2)] + value,
        store,
    )


def adjoint_kernel(parts, dense, resid, *out_refs):
    half, quarter = dense.shape[0] // 2, dense.shape[0] // 4
    core = lax.axis_index("shot") % 2
    lhs = jnp.concatenate([resid[m] for m in range(resid.shape[0])], axis=1)
    for (keep, second), out_ref in zip(parts, out_refs):
        first = (core if keep else 1 - core) * half + second * quarter
        for j in range(quarter):
            both = jnp.dot(lhs, dense[first + j], preferred_element_type=f32)
            both = both.astype(out_ref.dtype)
            out_ref[2 * j] = both[:, :CBLK]
            out_ref[2 * j + 1] = both[:, CBLK:]


def pair_kernel(keep_ref, got_ref, out_ref):
    out_ref[...] = (keep_ref[...] + got_ref[...].astype(f32)).astype(bf16)


def residual_kernel(parts_ref, obs_ref, wt_ref, after_ref, out_ref, *resid_ref):
    for i in range(parts_ref.shape[1]):
        total = parts_ref[0, i].astype(f32)
        for d in range(1, parts_ref.shape[0]):
            total += parts_ref[d, i].astype(f32)
        resid = wt_ref[pl.ds(i, 1), :] * (total.T - obs_ref[pl.ds(i, 1), :])
        if resid_ref:
            resid_ref[0][i] = resid
        rounded = resid.astype(bf16)
        for d in range(parts_ref.shape[0]):
            out_ref[d, i] = rounded


def turn_kernel(in_ref, out_ref):
    for i in range(in_ref.shape[0]):
        out_ref[i] = in_ref[i].T


def prepare_kernel(state, prior, after_ref, field_a, field_b, base_ref):
    quarter = field_a.shape[0]
    own = lax.axis_index("shot") % 2 * (2 * quarter)
    for at, field_ref in ((own, field_a), (own + quarter, field_b)):
        part = pl.ds(at, quarter)
        field_ref[...] = state[part] + prior[part]
    base_ref[...] = state[...] + 0.5 * prior[...]


def sum_over_y(chip_y, part_refs, order, i):
    if len(part_refs) > 2:
        for d, part_ref in enumerate(part_refs):
            order[chip_y ^ d] = part_ref[i]
        parts = [order[y] for y in range(len(part_refs))]
    else:
        parts = [part_ref[i] for part_ref in part_refs]
    total = parts[0].astype(f32)
    for part in parts[1:]:
        total += part.astype(f32)
    return total.T


def probe_kernel(ny, field_ref, *rest):
    part_refs, (out_ref, grad_ref, order) = rest[:ny], rest[ny:]
    for i in range(out_ref.shape[0]):
        grad = sum_over_y(lax.axis_index("shot") // 2, part_refs, order, i)
        grad_ref[i] = grad
        out_ref[i] = (field_ref[i] - 0.25 * grad).astype(bf16)


def total_kernel(ny, grad_ref, after_ref, *rest):
    part_refs, (out_ref, order) = rest[:ny], rest[ny:]
    for i in range(out_ref.shape[0]):
        grad2 = sum_over_y(lax.axis_index("shot") // 2, part_refs, order, i)
        out_ref[i] = (grad_ref[i] + grad2).astype(bf16)


def early_update_kernel(base, own_a, own_b, mate_a, out_hbm, rest_ref, new, sems):
    quarter = own_a.shape[0]
    core = lax.axis_index("shot") % 2
    own, mate = core * (2 * quarter), (1 - core) * (2 * quarter)
    copies = []
    for n, (at, part_ref) in enumerate(((own, own_a), (own + quarter, own_b), (mate, mate_a))):
        new[n] = base[pl.ds(at, quarter)] - 0.125 * part_ref[...].astype(f32)
        copies.append(
            pltpu.make_async_copy(new.at[n], out_hbm.at[pl.ds(at, quarter)], sems.at[n])
        )
        copies[-1].start()
    rest_ref[...] = base[pl.ds(mate + quarter, quarter)]
    for copy in copies:
        copy.wait()


def late_update_kernel(rest_ref, mate_b, so_far_hbm, out_hbm, new, sem):
    quarter = mate_b.shape[0]
    at = (1 - lax.axis_index("shot") % 2) * (2 * quarter) + quarter
    new[...] = rest_ref[...] - 0.125 * mate_b[...].astype(f32)
    copy = pltpu.make_async_copy(new, out_hbm.at[pl.ds(at, quarter)], sem)
    copy.start()
    copy.wait()


def per_device(nshot, nband, sens, bund, cblk, state, prior, observed, pick_weight):
    nblk = sens.shape[0]
    samples = state.shape[1]
    owned, rays = observed.shape
    bundles = owned * nband
    cells = state.shape[0] // CBLK
    quarter = cells // 4
    ny = nshot // 2
    flops = 2 * nblk * rays * CBLK * samples
    sens_bytes = nblk * rays * CBLK * 2

    state_b = state.reshape(cells, CBLK, samples)
    prior_b = prior.reshape(cells, CBLK, samples)

    def other_core(array):
        return lax.ppermute(array, "shot", [(i, i ^ 1) for i in range(nshot)])

    def other_chips(array):
        return [array] + [
            lax.ppermute(array, "shot", [(i, i ^ (2 * d)) for i in range(nshot)])
            for d in range(1, ny)
        ]

    def over_band(array):
        return lax.all_to_all(array, "band", split_axis=0, concat_axis=0, tiled=True)

    part_out = arr((bundles, rays, samples), bf16)
    dense_shape = (cells // 2, bundles * rays, 2 * CBLK)
    dense_flops = 2 * bundles * rays * cells * CBLK * samples
    dense_bytes = 2 * bundles * rays * cells * CBLK
    quarter_bf16 = arr((quarter, CBLK, samples), bf16)
    quarter_f32 = arr((quarter, CBLK, samples), f32)
    order = pltpu.VMEM((ny, samples, CBLK), bf16)

    def residual(part, after, name, keep):
        parts = over_band(part).reshape(nband, owned, rays, samples)
        outs = (arr((nband, owned, samples, rays), bf16),)
        if keep:
            outs += (arr((owned, samples, rays), f32),)
        copies, *resid = call(
            residual_kernel, outs, [], [VMEM] * 3 + [ANY], name, bytes_accessed=1 << 20
        )(parts, observed, pick_weight, after)
        return resid, over_band(copies).reshape(bundles, samples, rays)

    def adjoint(dense, resid_all, name):
        def kernel(parts, part):
            return call(
                functools.partial(adjoint_kernel, parts),
                tuple(quarter_f32 if keep else quarter_bf16 for keep, _ in parts),
                [],
                [VMEM] * 2,
                name + part,
                dense_flops * len(parts) // 4,
                dense_bytes * len(parts) // 4,
            )(dense, resid_all)

        def pair(keep, got, part):
            return call(
                pair_kernel,
                quarter_bf16,
                [],
                [VMEM] * 2,
                name + "_pair" + part,
                bytes_accessed=1 << 19,
            )(keep, got)

        (give_a,) = kernel(((False, 0),), "_give_a")
        got_a = other_core(give_a)
        keep_a, give_b = kernel(((True, 0), (False, 1)), "_keep_a")
        got_b = other_core(give_b)
        sums_a = other_chips(pair(keep_a, got_a, "_a"))
        (keep_b,) = kernel(((True, 1),), "_keep_b")
        sums_b = other_chips(pair(keep_b, got_b, "_b"))
        return sums_a, sums_b, keep_b

    part1 = call(
        first_forward_kernel,
        part_out,
        [
            pltpu.VMEM((bundles, rays, samples), f32),
            pltpu.VMEM((cells, CBLK, samples), bf16),
            pltpu.SMEM((nblk,), i32),
            pltpu.SMEM((nblk,), i32),
            pltpu.VMEM(sens.shape, bf16),
            pltpu.VMEM(state_b.shape, f32),
            pltpu.VMEM(state_b.shape, f32),
            pltpu.SemaphoreType.DMA((6 + CHUNKS,)),
        ],
        [HBM] * 5,
        "forward1",
        flops,
        sens_bytes,
        vmem=FIRST_VMEM,
    )(bund, cblk, sens, state_b, prior_b)
    dense, token = call(
        dense_kernel,
        (arr(dense_shape, bf16), arr((8, CBLK), f32)),
        [pltpu.VMEM(dense_shape, f32)],
        [SMEM, SMEM, VMEM, ANY],
        "dense",
        0,
        16 << 20,
        vmem=3 * dense_bytes + 2 * sens_bytes + (2 << 20),
    )(bund, cblk, sens, part1)
    _, resid_all1 = residual(part1, token, "residual1", False)
    *sums1, after = adjoint(dense, resid_all1, "adjoint1")

    *fields, base = call(
        prepare_kernel,
        (quarter_f32, quarter_f32, arr((cells, CBLK, samples), f32)),
        [],
        [VMEM, VMEM, ANY],
        "prepare",
        bytes_accessed=4 << 20,
    )(state_b, prior_b, after)
    own, grad1, mate = [], [], []
    for field, sums, part in zip(fields, sums1, "ab"):
        probe, grad = call(
            functools.partial(probe_kernel, ny),
            (quarter_bf16, quarter_f32),
            [order],
            [VMEM] * (1 + ny),
            "probe2_" + part,
            bytes_accessed=1 << 19,
        )(field, *sums)
        own.append(probe)
        grad1.append(grad)
        mate.append(other_core(probe))

    early = call(
        early_forward_kernel,
        arr((bundles, rays, samples), f32),
        [],
        [VMEM] * 4,
        "forward2_early",
        dense_flops * 3 // 4,
        dense_bytes * 3 // 4,
    )(dense, own[0], own[1], mate[0])
    part2 = call(
        late_forward_kernel,
        part_out,
        [],
        [VMEM] * 3,
        "forward2_late",
        dense_flops // 4,
        dense_bytes // 4,
    )(dense, mate[1], early)

    (resid2_t,), resid_all2 = residual(part2, token, "residual2", True)
    *sums2, _ = adjoint(dense, resid_all2, "adjoint2")
    resid2 = call(
        turn_kernel,
        arr((owned, rays, samples), f32),
        [],
        [VMEM],
        "turn",
        bytes_accessed=1 << 20,
    )(resid2_t)
    own, mate, after = [], [], resid2
    for grad, sums, part in zip(grad1, sums2, "ab"):
        total = call(
            functools.partial(total_kernel, ny),
            quarter_bf16,
            [order],
            [VMEM, ANY] + [VMEM] * ny,
            "total_" + part,
            bytes_accessed=1 << 19,
        )(grad, after, *sums)
        own.append(total)
        after = grad
        mate.append(other_core(total))
    whole = arr((cells, CBLK, samples), f32)
    so_far, rest = call(
        early_update_kernel,
        (whole, quarter_f32),
        [pltpu.VMEM((3, quarter, CBLK, samples), f32), pltpu.SemaphoreType.DMA((3,))],
        [VMEM] * 4,
        "new_state_early",
        bytes_accessed=3 << 20,
        out_specs=(HBM, VMEM),
    )(base, own[0], own[1], mate[0])
    new_state = call(
        late_update_kernel,
        whole,
        [pltpu.VMEM((quarter, CBLK, samples), f32), pltpu.SemaphoreType.DMA],
        [VMEM, VMEM, HBM],
        "new_state_late",
        bytes_accessed=1 << 20,
        out_specs=HBM,
        input_output_aliases={2: 0},
    )(rest, mate[1], so_far)
    return new_state.reshape(state.shape), resid2


def solution(mesh):
    in_specs = (
        P(("shot", "band"), None, None),
        P(("shot", "band")),
        P(("shot", "band")),
        P("band", None),
        P("band", None),
        P(("shot", "band"), None),
        P(("shot", "band"), None),
    )
    out_specs = (P("band", None), P(("shot", "band"), None, None))
    return jax.shard_map(
        functools.partial(per_device, mesh.shape["shot"], mesh.shape["band"]),
        mesh=mesh,
        in_specs=in_specs,
        out_specs=out_specs,
        check_vma=False,
    )
```

```python
import functools

import jax
import jax.numpy as jnp
from jax import lax
from jax.experimental import pallas as pl
from jax.experimental.pallas import tpu as pltpu
from jax.sharding import PartitionSpec as P

CBLK = 128
GROUP = 32
CHUNKS = 2
FIRST_VMEM = 55 << 20
GIVE_A, KEEP_A, GIVE_B, KEEP_B = range(4)

VMEM = pl.BlockSpec(memory_space=pltpu.VMEM)
SMEM = pl.BlockSpec(memory_space=pltpu.SMEM)
HBM = pl.BlockSpec(memory_space=pltpu.HBM)
ANY = pl.BlockSpec(memory_space=pl.ANY)

bf16, f32, i32 = jnp.bfloat16, jnp.float32, jnp.int32
arr = jax.ShapeDtypeStruct

def call(body, outs, scratch, in_specs, name, flops=0, bytes_accessed=0, vmem=32 << 20, **more):
    if "out_specs" not in more:
        more["out_specs"] = jax.tree.map(lambda _: VMEM, outs)
    return pl.pallas_call(
        body,
        out_shape=outs,
        in_specs=in_specs,
        scratch_shapes=scratch,
        compiler_params=pltpu.CompilerParams(vmem_limit_bytes=vmem),
        cost_estimate=pl.CostEstimate(
            flops=flops, bytes_accessed=bytes_accessed, transcendentals=0
        ),
        name=name,
        **more,
    )


def first_forward_kernel(
    bund_hbm,
    cblk_hbm,
    sens_hbm,
    state_hbm,
    prior_hbm,
    out_ref,
    acc,
    probe,
    bund,
    cblk,
    sens,
    state,
    prior,
    sems,
):
    nblk = sens.shape[0]
    step = nblk // CHUNKS
    cells = state.shape[0]
    half = cells // 2
    small = [
        pltpu.make_async_copy(bund_hbm, bund, sems.at[0]),
        pltpu.make_async_copy(cblk_hbm, cblk, sems.at[1]),
    ]
    fields = []
    for h in range(2):
        part = pl.ds(h * half, half)
        fields.append(
            [
                pltpu.make_async_copy(state_hbm.at[part], state.at[part], sems.at[2 + 2 * h]),
                pltpu.make_async_copy(prior_hbm.at[part], prior.at[part], sems.at[3 + 2 * h]),
            ]
        )

    def block_copy(c):
        part = pl.ds(c * step, step)
        return pltpu.make_async_copy(sens_hbm.at[part], sens.at[part], sems.at[6 + c])

    for copy in small + fields[0] + fields[1] + [block_copy(c) for c in range(CHUNKS)]:
        copy.start()
    acc[...] = jnp.zeros_like(acc)

    for h in range(2):
        part = pl.ds(h * half, half)
        for copy in fields[h]:
            copy.wait()
        probe[part] = (state[part] + 0.5 * prior[part]).astype(bf16)
    for copy in small:
        copy.wait()

    def chunk(c, carry):
        block_copy(c).wait()
        for g in range(step // GROUP):
            ks = [c * step + g * GROUP + j for j in range(GROUP)]
            prods = [
                jnp.dot(sens[k], probe[cblk[k]], preferred_element_type=f32) for k in ks
            ]
            for k, prod in zip(ks, prods):
                acc[bund[k]] += prod
        return carry

    lax.fori_loop(0, CHUNKS, chunk, 0)
    out_ref[...] = acc[...].astype(bf16)


def dense_kernel(bund, cblk, sens, after_ref, *rest):
    out_refs, (token_ref, total) = rest[:4], rest[4:]
    rays = sens.shape[1]
    quarter = 2 * total.shape[1]
    core = lax.axis_index("shot") % 2
    total[...] = jnp.zeros_like(total)

    def place(k, carry):
        cell = cblk[k]
        kept = jnp.where(cell // (2 * quarter) == core, 1, 0)
        part = 2 * (cell // quarter % 2) + kept
        rows = pl.ds(pl.multiple_of(bund[k] * rays, rays), rays)
        lanes = pl.ds(pl.multiple_of(cell % 2 * CBLK, CBLK), CBLK)
        total[part, cell % quarter // 2, rows, lanes] += sens[k].astype(f32)
        return carry

    lax.fori_loop(0, sens.shape[0], place, 0)
    for part, out_ref in enumerate(out_refs):
        out_ref[...] = total[part].astype(bf16)
    token_ref[...] = jnp.zeros_like(token_ref)


def dense_forward(columns, store):
    step = 2 * CBLK
    pairs = columns[0][0].shape[0]
    probe = jnp.concatenate(
        [part[...].reshape(2 * CBLK * pairs, -1) for _, part in columns], axis=0
    )
    for m in range(columns[0][0].shape[1] // step):
        rows = pl.ds(m * step, step)
        lhs = jnp.concatenate(
            [dense[pair, rows, :] for dense, _ in columns for pair in range(pairs)], axis=1
        )
        total = jnp.dot(lhs, probe, preferred_element_type=f32)
        store(pl.ds(2 * m, 2), total.reshape(2, CBLK, -1))


def early_forward_kernel(dense_own_a, dense_own_b, dense_mate_a, own_a, own_b, mate_a, acc):
    def store(rows, value):
        acc[rows] = value

    columns = [(dense_own_a, own_a), (dense_own_b, own_b), (dense_mate_a, mate_a)]
    dense_forward(columns, store)


def late_forward_kernel(dense_mate_b, mate_b, early, out_ref):
    def store(rows, value):
        out_ref[rows] = (early[rows] + value).astype(bf16)

    dense_forward([(dense_mate_b, mate_b)], store)


def adjoint_kernel(resid, *refs):
    lhs = jnp.concatenate([resid[m] for m in range(resid.shape[0])], axis=1)
    count = len(refs) // 2
    for dense, out_ref in zip(refs[:count], refs[count:]):
        for pair in range(dense.shape[0]):
            both = jnp.dot(lhs, dense[pair], preferred_element_type=f32)
            both = both.astype(out_ref.dtype)
            out_ref[2 * pair] = both[:, :CBLK]
            out_ref[2 * pair + 1] = both[:, CBLK:]


def pair_kernel(keep_ref, got_ref, out_ref):
    out_ref[...] = (keep_ref[...] + got_ref[...].astype(f32)).astype(bf16)


def residual_kernel(parts_ref, obs_ref, wt_ref, after_ref, out_ref, *resid_ref):
    for i in range(parts_ref.shape[1]):
        total = parts_ref[0, i].astype(f32)
        for d in range(1, parts_ref.shape[0]):
            total += parts_ref[d, i].astype(f32)
        resid = wt_ref[pl.ds(i, 1), :] * (total.T - obs_ref[pl.ds(i, 1), :])
        if resid_ref:
            resid_ref[0][i] = resid
        rounded = resid.astype(bf16)
        for d in range(parts_ref.shape[0]):
            out_ref[d, i] = rounded


def turn_kernel(in_ref, out_ref, token_ref):
    for i in range(in_ref.shape[0]):
        out_ref[i] = in_ref[i].T
    token_ref[...] = jnp.zeros_like(token_ref)


def prepare_kernel(state, prior, after_ref, field_a, field_b, base_ref):
    quarter = field_a.shape[0]
    own = lax.axis_index("shot") % 2 * (2 * quarter)
    for at, field_ref in ((own, field_a), (own + quarter, field_b)):
        part = pl.ds(at, quarter)
        field_ref[...] = state[part] + prior[part]
    base_ref[...] = state[...] + 0.5 * prior[...]


def sum_over_y(chip_y, part_refs, order, i):
    if len(part_refs) > 2:
        for d, part_ref in enumerate(part_refs):
            order[chip_y ^ d] = part_ref[i]
        parts = [order[y] for y in range(len(part_refs))]
    else:
        parts = [part_ref[i] for part_ref in part_refs]
    total = parts[0].astype(f32)
    for part in parts[1:]:
        total += part.astype(f32)
    return total.T


def probe_kernel(ny, field_ref, *rest):
    part_refs, (out_ref, grad_ref, order) = rest[:ny], rest[ny:]
    for i in range(out_ref.shape[0]):
        grad = sum_over_y(lax.axis_index("shot") // 2, part_refs, order, i)
        grad_ref[i] = grad
        out_ref[i] = (field_ref[i] - 0.25 * grad).astype(bf16)


def total_kernel(ny, grad_ref, after_ref, *rest):
    part_refs, (out_ref, order) = rest[:ny], rest[ny:]
    for i in range(out_ref.shape[0]):
        grad2 = sum_over_y(lax.axis_index("shot") // 2, part_refs, order, i)
        out_ref[i] = (grad_ref[i] + grad2).astype(bf16)


def early_update_kernel(base, own_a, own_b, mate_a, out_hbm, rest_ref, new, sems):
    quarter = own_a.shape[0]
    core = lax.axis_index("shot") % 2
    own, mate = core * (2 * quarter), (1 - core) * (2 * quarter)
    copies = []
    for n, (at, part_ref) in enumerate(((own, own_a), (own + quarter, own_b), (mate, mate_a))):
        new[n] = base[pl.ds(at, quarter)] - 0.125 * part_ref[...].astype(f32)
        copies.append(
            pltpu.make_async_copy(new.at[n], out_hbm.at[pl.ds(at, quarter)], sems.at[n])
        )
        copies[-1].start()
    rest_ref[...] = base[pl.ds(mate + quarter, quarter)]
    for copy in copies:
        copy.wait()


def late_update_kernel(rest_ref, mate_b, so_far_hbm, out_hbm, new, sem):
    quarter = mate_b.shape[0]
    at = (1 - lax.axis_index("shot") % 2) * (2 * quarter) + quarter
    new[...] = rest_ref[...] - 0.125 * mate_b[...].astype(f32)
    copy = pltpu.make_async_copy(new, out_hbm.at[pl.ds(at, quarter)], sem)
    copy.start()
    copy.wait()


def per_device(nshot, nband, sens, bund, cblk, state, prior, observed, pick_weight):
    nblk = sens.shape[0]
    samples = state.shape[1]
    owned, rays = observed.shape
    bundles = owned * nband
    cells = state.shape[0] // CBLK
    quarter = cells // 4
    ny = nshot // 2
    flops = 2 * nblk * rays * CBLK * samples
    sens_bytes = nblk * rays * CBLK * 2

    state_b = state.reshape(cells, CBLK, samples)
    prior_b = prior.reshape(cells, CBLK, samples)

    def other_core(array):
        return lax.ppermute(array, "shot", [(i, i ^ 1) for i in range(nshot)])

    def other_chips(array):
        return [array] + [
            lax.ppermute(array, "shot", [(i, i ^ (2 * d)) for i in range(nshot)])
            for d in range(1, ny)
        ]

    def over_band(array):
        return lax.all_to_all(array, "band", split_axis=0, concat_axis=0, tiled=True)

    part_out = arr((bundles, rays, samples), bf16)
    dense_shape = (quarter // 2, bundles * rays, 2 * CBLK)
    small_token = arr((8, CBLK), f32)
    dense_flops = 2 * bundles * rays * cells * CBLK * samples
    dense_bytes = 2 * bundles * rays * cells * CBLK
    quarter_bf16 = arr((quarter, CBLK, samples), bf16)
    quarter_f32 = arr((quarter, CBLK, samples), f32)
    order = pltpu.VMEM((ny, samples, CBLK), bf16)

    def residual(part, after, name, keep):
        parts = over_band(part).reshape(nband, owned, rays, samples)
        outs = (arr((nband, owned, samples, rays), bf16),)
        if keep:
            outs += (arr((owned, samples, rays), f32),)
        copies, *resid = call(
            residual_kernel, outs, [], [VMEM] * 3 + [ANY], name, bytes_accessed=1 << 20
        )(parts, observed, pick_weight, after)
        return resid, over_band(copies).reshape(bundles, samples, rays)

    def adjoint(dense, resid_all, name):
        def kernel(parts, part):
            return call(
                adjoint_kernel,
                tuple(quarter_f32 if p % 2 else quarter_bf16 for p in parts),
                [],
                [VMEM] * (1 + len(parts)),
                name + part,
                dense_flops * len(parts) // 4,
                dense_bytes * len(parts) // 4,
            )(resid_all, *[dense[p] for p in parts])

        def pair(keep, got, part):
            return call(
                pair_kernel,
                quarter_bf16,
                [],
                [VMEM] * 2,
                name + "_pair" + part,
                bytes_accessed=1 << 19,
            )(keep, got)

        (give_a,) = kernel((GIVE_A,), "_give_a")
        got_a = other_core(give_a)
        keep_a, give_b = kernel((KEEP_A, GIVE_B), "_keep_a")
        got_b = other_core(give_b)
        sums_a = other_chips(pair(keep_a, got_a, "_a"))
        (keep_b,) = kernel((KEEP_B,), "_keep_b")
        sums_b = other_chips(pair(keep_b, got_b, "_b"))
        return sums_a, sums_b, keep_b

    part1 = call(
        first_forward_kernel,
        part_out,
        [
            pltpu.VMEM((bundles, rays, samples), f32),
            pltpu.VMEM((cells, CBLK, samples), bf16),
            pltpu.SMEM((nblk,), i32),
            pltpu.SMEM((nblk,), i32),
            pltpu.VMEM(sens.shape, bf16),
            pltpu.VMEM(state_b.shape, f32),
            pltpu.VMEM(state_b.shape, f32),
            pltpu.SemaphoreType.DMA((6 + CHUNKS,)),
        ],
        [HBM] * 5,
        "forward1",
        flops,
        sens_bytes,
        vmem=FIRST_VMEM,
    )(bund, cblk, sens, state_b, prior_b)
    *dense, token = call(
        dense_kernel,
        (arr(dense_shape, bf16),) * 4 + (small_token,),
        [pltpu.VMEM((4,) + dense_shape, f32)],
        [SMEM, SMEM, VMEM, ANY],
        "dense",
        0,
        16 << 20,
        vmem=3 * dense_bytes + 2 * sens_bytes + (2 << 20),
    )(bund, cblk, sens, part1)
    _, resid_all1 = residual(part1, token, "residual1", False)
    *sums1, after = adjoint(dense, resid_all1, "adjoint1")

    *fields, base = call(
        prepare_kernel,
        (quarter_f32, quarter_f32, arr((cells, CBLK, samples), f32)),
        [],
        [VMEM, VMEM, ANY],
        "prepare",
        bytes_accessed=4 << 20,
    )(state_b, prior_b, after)
    own, grad1, mate = [], [], []
    for field, sums, part in zip(fields, sums1, "ab"):
        probe, grad = call(
            functools.partial(probe_kernel, ny),
            (quarter_bf16, quarter_f32),
            [order],
            [VMEM] * (1 + ny),
            "probe2_" + part,
            bytes_accessed=1 << 19,
        )(field, *sums)
        own.append(probe)
        grad1.append(grad)
        mate.append(other_core(probe))

    early = call(
        early_forward_kernel,
        arr((bundles, rays, samples), f32),
        [],
        [VMEM] * 6,
        "forward2_early",
        dense_flops * 3 // 4,
        dense_bytes * 3 // 4,
    )(dense[KEEP_A], dense[KEEP_B], dense[GIVE_A], own[0], own[1], mate[0])
    part2 = call(
        late_forward_kernel,
        part_out,
        [],
        [VMEM] * 3,
        "forward2_late",
        dense_flops // 4,
        dense_bytes // 4,
    )(dense[GIVE_B], mate[1], early)

    (resid2_t,), resid_all2 = residual(part2, token, "residual2", True)
    *sums2, _ = adjoint(dense, resid_all2, "adjoint2")
    resid2, after = call(
        turn_kernel,
        (arr((owned, rays, samples), f32), small_token),
        [],
        [VMEM],
        "turn",
        bytes_accessed=1 << 20,
    )(resid2_t)
    own, mate = [], []
    for grad, sums, part in zip(grad1, sums2, "ab"):
        total = call(
            functools.partial(total_kernel, ny),
            quarter_bf16,
            [order],
            [VMEM, ANY] + [VMEM] * ny,
            "total_" + part,
            bytes_accessed=1 << 19,
        )(grad, after, *sums)
        own.append(total)
        mate.append(other_core(total))
    whole = arr((cells, CBLK, samples), f32)
    so_far, rest = call(
        early_update_kernel,
        (whole, quarter_f32),
        [pltpu.VMEM((3, quarter, CBLK, samples), f32), pltpu.SemaphoreType.DMA((3,))],
        [VMEM] * 4,
        "new_state_early",
        bytes_accessed=3 << 20,
        out_specs=(HBM, VMEM),
    )(base, own[0], own[1], mate[0])
    new_state = call(
        late_update_kernel,
        whole,
        [pltpu.VMEM((quarter, CBLK, samples), f32), pltpu.SemaphoreType.DMA],
        [VMEM, VMEM, HBM],
        "new_state_late",
        bytes_accessed=1 << 20,
        out_specs=HBM,
        input_output_aliases={2: 0},
    )(rest, mate[1], so_far)
    return new_state.reshape(state.shape), resid2


def solution(mesh):
    in_specs = (
        P(("shot", "band"), None, None),
        P(("shot", "band")),
        P(("shot", "band")),
        P("band", None),
        P("band", None),
        P(("shot", "band"), None),
        P(("shot", "band"), None),
    )
    out_specs = (P("band", None), P(("shot", "band"), None, None))
    return jax.shard_map(
        functools.partial(per_device, mesh.shape["shot"], mesh.shape["band"]),
        mesh=mesh,
        in_specs=in_specs,
        out_specs=out_specs,
        check_vma=False,
    )
```

```python
import functools

import jax
import jax.numpy as jnp
from jax import lax
from jax.experimental import pallas as pl
from jax.experimental.pallas import tpu as pltpu
from jax.sharding import PartitionSpec as P

CBLK = 128
GROUP = 32
CHUNKS = 2
FIRST_VMEM = 55 << 20
GIVE_A, KEEP_A, GIVE_B, KEEP_B = range(4)

VMEM = pl.BlockSpec(memory_space=pltpu.VMEM)
SMEM = pl.BlockSpec(memory_space=pltpu.SMEM)
HBM = pl.BlockSpec(memory_space=pltpu.HBM)
ANY = pl.BlockSpec(memory_space=pl.ANY)

bf16, f32, i32 = jnp.bfloat16, jnp.float32, jnp.int32
arr = jax.ShapeDtypeStruct

def call(body, outs, scratch, in_specs, name, flops=0, bytes_accessed=0, vmem=32 << 20, **more):
    if "out_specs" not in more:
        more["out_specs"] = jax.tree.map(lambda _: VMEM, outs)
    return pl.pallas_call(
        body,
        out_shape=outs,
        in_specs=in_specs,
        scratch_shapes=scratch,
        compiler_params=pltpu.CompilerParams(vmem_limit_bytes=vmem),
        cost_estimate=pl.CostEstimate(
            flops=flops, bytes_accessed=bytes_accessed, transcendentals=0
        ),
        name=name,
        **more,
    )


def first_forward_kernel(
    bund_hbm,
    cblk_hbm,
    sens_hbm,
    state_hbm,
    prior_hbm,
    out_ref,
    acc,
    probe,
    bund,
    cblk,
    sens,
    state,
    prior,
    sems,
):
    nblk = sens.shape[0]
    step = nblk // CHUNKS
    cells = state.shape[0]
    half = cells // 2
    small = [
        pltpu.make_async_copy(bund_hbm, bund, sems.at[0]),
        pltpu.make_async_copy(cblk_hbm, cblk, sems.at[1]),
    ]
    fields = []
    for h in range(2):
        part = pl.ds(h * half, half)
        fields.append(
            [
                pltpu.make_async_copy(state_hbm.at[part], state.at[part], sems.at[2 + 2 * h]),
                pltpu.make_async_copy(prior_hbm.at[part], prior.at[part], sems.at[3 + 2 * h]),
            ]
        )

    def block_copy(c):
        part = pl.ds(c * step, step)
        return pltpu.make_async_copy(sens_hbm.at[part], sens.at[part], sems.at[6 + c])

    for copy in small + fields[0] + fields[1] + [block_copy(c) for c in range(CHUNKS)]:
        copy.start()
    acc[...] = jnp.zeros_like(acc)

    for h in range(2):
        part = pl.ds(h * half, half)
        for copy in fields[h]:
            copy.wait()
        probe[part] = (state[part] + 0.5 * prior[part]).astype(bf16)
    for copy in small:
        copy.wait()

    def chunk(c, carry):
        block_copy(c).wait()
        for g in range(step // GROUP):
            ks = [c * step + g * GROUP + j for j in range(GROUP)]
            prods = [
                jnp.dot(sens[k], probe[cblk[k]], preferred_element_type=f32) for k in ks
            ]
            for k, prod in zip(ks, prods):
                acc[bund[k]] += prod
        return carry

    lax.fori_loop(0, CHUNKS, chunk, 0)
    out_ref[...] = acc[...].astype(bf16)


def dense_kernel(bund, cblk, sens, after_ref, *rest):
    out_refs, (token_ref, total, last, sem) = rest[:4], rest[4:]
    rays = sens.shape[1]
    quarter = 2 * total.shape[1]
    core = lax.axis_index("shot") % 2
    total[...] = jnp.zeros_like(total)

    def place(k, carry):
        cell = cblk[k]
        kept = jnp.where(cell // (2 * quarter) == core, 1, 0)
        part = 2 * (cell // quarter % 2) + kept
        rows = pl.ds(pl.multiple_of(bund[k] * rays, rays), rays)
        lanes = pl.ds(pl.multiple_of(cell % 2 * CBLK, CBLK), CBLK)
        total[part, cell % quarter // 2, rows, lanes] += sens[k].astype(f32)
        return carry

    lax.fori_loop(0, sens.shape[0], place, 0)
    last[...] = total[KEEP_B].astype(bf16)
    copy = pltpu.make_async_copy(last, out_refs[KEEP_B], sem)
    copy.start()
    for part in (GIVE_A, KEEP_A, GIVE_B):
        out_refs[part][...] = total[part].astype(bf16)
    copy.wait()
    token_ref[...] = jnp.zeros_like(token_ref)


def dense_forward(columns, store):
    step = 2 * CBLK
    pairs = columns[0][0].shape[0]
    probe = jnp.concatenate(
        [part[...].reshape(2 * CBLK * pairs, -1) for _, part in columns], axis=0
    )
    for m in range(columns[0][0].shape[1] // step):
        rows = pl.ds(m * step, step)
        lhs = jnp.concatenate(
            [dense[pair, rows, :] for dense, _ in columns for pair in range(pairs)], axis=1
        )
        total = jnp.dot(lhs, probe, preferred_element_type=f32)
        store(pl.ds(2 * m, 2), total.reshape(2, CBLK, -1))


def early_forward_kernel(dense_own_a, dense_own_b, dense_mate_a, own_a, own_b, mate_a, acc):
    def store(rows, value):
        acc[rows] = value

    columns = [(dense_own_a, own_a), (dense_own_b, own_b), (dense_mate_a, mate_a)]
    dense_forward(columns, store)


def late_forward_kernel(dense_mate_b, mate_b, early, out_ref):
    def store(rows, value):
        out_ref[rows] = (early[rows] + value).astype(bf16)

    dense_forward([(dense_mate_b, mate_b)], store)


def adjoint_kernel(resid, *refs):
    lhs = jnp.concatenate([resid[m] for m in range(resid.shape[0])], axis=1)
    count = len(refs) // 2
    for dense, out_ref in zip(refs[:count], refs[count:]):
        for pair in range(dense.shape[0]):
            both = jnp.dot(lhs, dense[pair], preferred_element_type=f32)
            both = both.astype(out_ref.dtype)
            out_ref[2 * pair] = both[:, :CBLK]
            out_ref[2 * pair + 1] = both[:, CBLK:]


def pair_kernel(keep_ref, got_ref, out_ref):
    out_ref[...] = (keep_ref[...] + got_ref[...].astype(f32)).astype(bf16)


def residual_kernel(parts_ref, obs_ref, wt_ref, after_ref, out_ref, *resid_ref):
    for i in range(parts_ref.shape[1]):
        total = parts_ref[0, i].astype(f32)
        for d in range(1, parts_ref.shape[0]):
            total += parts_ref[d, i].astype(f32)
        resid = wt_ref[pl.ds(i, 1), :] * (total.T - obs_ref[pl.ds(i, 1), :])
        if resid_ref:
            resid_ref[0][i] = resid
        rounded = resid.astype(bf16)
        for d in range(parts_ref.shape[0]):
            out_ref[d, i] = rounded


def turn_kernel(in_ref, out_ref, token_ref):
    for i in range(in_ref.shape[0]):
        out_ref[i] = in_ref[i].T
    token_ref[...] = jnp.zeros_like(token_ref)


def prepare_kernel(state, prior, after_ref, field_a, field_b, base_ref):
    quarter = field_a.shape[0]
    own = lax.axis_index("shot") % 2 * (2 * quarter)
    for at, field_ref in ((own, field_a), (own + quarter, field_b)):
        part = pl.ds(at, quarter)
        field_ref[...] = state[part] + prior[part]
    base_ref[...] = state[...] + 0.5 * prior[...]


def sum_over_y(chip_y, part_refs, order, i):
    if len(part_refs) > 2:
        for d, part_ref in enumerate(part_refs):
            order[chip_y ^ d] = part_ref[i]
        parts = [order[y] for y in range(len(part_refs))]
    else:
        parts = [part_ref[i] for part_ref in part_refs]
    total = parts[0].astype(f32)
    for part in parts[1:]:
        total += part.astype(f32)
    return total.T


def probe_kernel(ny, field_ref, *rest):
    part_refs, (out_ref, grad_ref, order) = rest[:ny], rest[ny:]
    for i in range(out_ref.shape[0]):
        grad = sum_over_y(lax.axis_index("shot") // 2, part_refs, order, i)
        grad_ref[i] = grad
        out_ref[i] = (field_ref[i] - 0.25 * grad).astype(bf16)


def total_kernel(ny, grad_ref, after_ref, *rest):
    part_refs, (out_ref, order) = rest[:ny], rest[ny:]
    for i in range(out_ref.shape[0]):
        grad2 = sum_over_y(lax.axis_index("shot") // 2, part_refs, order, i)
        out_ref[i] = (grad_ref[i] + grad2).astype(bf16)


def early_update_kernel(base, own_a, own_b, mate_a, out_hbm, rest_ref, new, sems):
    quarter = own_a.shape[0]
    core = lax.axis_index("shot") % 2
    own, mate = core * (2 * quarter), (1 - core) * (2 * quarter)
    copies = []
    for n, (at, part_ref) in enumerate(((own, own_a), (own + quarter, own_b), (mate, mate_a))):
        new[n] = base[pl.ds(at, quarter)] - 0.125 * part_ref[...].astype(f32)
        copies.append(
            pltpu.make_async_copy(new.at[n], out_hbm.at[pl.ds(at, quarter)], sems.at[n])
        )
        copies[-1].start()
    rest_ref[...] = base[pl.ds(mate + quarter, quarter)]
    for copy in copies:
        copy.wait()


def late_update_kernel(rest_ref, mate_b, so_far_hbm, out_hbm, new, sem):
    quarter = mate_b.shape[0]
    at = (1 - lax.axis_index("shot") % 2) * (2 * quarter) + quarter
    new[...] = rest_ref[...] - 0.125 * mate_b[...].astype(f32)
    copy = pltpu.make_async_copy(new, out_hbm.at[pl.ds(at, quarter)], sem)
    copy.start()
    copy.wait()


def per_device(nshot, nband, sens, bund, cblk, state, prior, observed, pick_weight):
    nblk = sens.shape[0]
    samples = state.shape[1]
    owned, rays = observed.shape
    bundles = owned * nband
    cells = state.shape[0] // CBLK
    quarter = cells // 4
    ny = nshot // 2
    flops = 2 * nblk * rays * CBLK * samples
    sens_bytes = nblk * rays * CBLK * 2

    state_b = state.reshape(cells, CBLK, samples)
    prior_b = prior.reshape(cells, CBLK, samples)

    def other_core(array):
        return lax.ppermute(array, "shot", [(i, i ^ 1) for i in range(nshot)])

    def other_chips(array):
        return [array] + [
            lax.ppermute(array, "shot", [(i, i ^ (2 * d)) for i in range(nshot)])
            for d in range(1, ny)
        ]

    def over_band(array):
        return lax.all_to_all(array, "band", split_axis=0, concat_axis=0, tiled=True)

    part_out = arr((bundles, rays, samples), bf16)
    dense_shape = (quarter // 2, bundles * rays, 2 * CBLK)
    small_token = arr((8, CBLK), f32)
    dense_flops = 2 * bundles * rays * cells * CBLK * samples
    dense_bytes = 2 * bundles * rays * cells * CBLK
    quarter_bf16 = arr((quarter, CBLK, samples), bf16)
    quarter_f32 = arr((quarter, CBLK, samples), f32)
    order = pltpu.VMEM((ny, samples, CBLK), bf16)

    def residual(part, after, name, keep):
        parts = over_band(part).reshape(nband, owned, rays, samples)
        outs = (arr((nband, owned, samples, rays), bf16),)
        if keep:
            outs += (arr((owned, samples, rays), f32),)
        copies, *resid = call(
            residual_kernel, outs, [], [VMEM] * 3 + [ANY], name, bytes_accessed=1 << 20
        )(parts, observed, pick_weight, after)
        return resid, over_band(copies).reshape(bundles, samples, rays)

    def adjoint(dense, resid_all, name):
        def kernel(parts, part):
            return call(
                adjoint_kernel,
                tuple(quarter_f32 if p % 2 else quarter_bf16 for p in parts),
                [],
                [VMEM] * (1 + len(parts)),
                name + part,
                dense_flops * len(parts) // 4,
                dense_bytes * len(parts) // 4,
            )(resid_all, *[dense[p] for p in parts])

        def pair(keep, got, part):
            return call(
                pair_kernel,
                quarter_bf16,
                [],
                [VMEM] * 2,
                name + "_pair" + part,
                bytes_accessed=1 << 19,
            )(keep, got)

        (give_a,) = kernel((GIVE_A,), "_give_a")
        got_a = other_core(give_a)
        keep_a, give_b = kernel((KEEP_A, GIVE_B), "_keep_a")
        got_b = other_core(give_b)
        sums_a = other_chips(pair(keep_a, got_a, "_a"))
        (keep_b,) = kernel((KEEP_B,), "_keep_b")
        sums_b = other_chips(pair(keep_b, got_b, "_b"))
        return sums_a, sums_b, keep_b

    part1 = call(
        first_forward_kernel,
        part_out,
        [
            pltpu.VMEM((bundles, rays, samples), f32),
            pltpu.VMEM((cells, CBLK, samples), bf16),
            pltpu.SMEM((nblk,), i32),
            pltpu.SMEM((nblk,), i32),
            pltpu.VMEM(sens.shape, bf16),
            pltpu.VMEM(state_b.shape, f32),
            pltpu.VMEM(state_b.shape, f32),
            pltpu.SemaphoreType.DMA((6 + CHUNKS,)),
        ],
        [HBM] * 5,
        "forward1",
        flops,
        sens_bytes,
        vmem=FIRST_VMEM,
    )(bund, cblk, sens, state_b, prior_b)
    *dense, token = call(
        dense_kernel,
        (arr(dense_shape, bf16),) * 4 + (small_token,),
        [
            pltpu.VMEM((4,) + dense_shape, f32),
            pltpu.VMEM(dense_shape, bf16),
            pltpu.SemaphoreType.DMA,
        ],
        [SMEM, SMEM, VMEM, ANY],
        "dense",
        0,
        16 << 20,
        vmem=3 * dense_bytes + 2 * sens_bytes + (2 << 20),
        out_specs=(VMEM, VMEM, VMEM, HBM, VMEM),
    )(bund, cblk, sens, part1)
    _, resid_all1 = residual(part1, token, "residual1", False)
    *sums1, after = adjoint(dense, resid_all1, "adjoint1")

    *fields, base = call(
        prepare_kernel,
        (quarter_f32, quarter_f32, arr((cells, CBLK, samples), f32)),
        [],
        [VMEM, VMEM, ANY],
        "prepare",
        bytes_accessed=4 << 20,
    )(state_b, prior_b, after)
    own, grad1, mate = [], [], []
    for field, sums, part in zip(fields, sums1, "ab"):
        probe, grad = call(
            functools.partial(probe_kernel, ny),
            (quarter_bf16, quarter_f32),
            [order],
            [VMEM] * (1 + ny),
            "probe2_" + part,
            bytes_accessed=1 << 19,
        )(field, *sums)
        own.append(probe)
        grad1.append(grad)
        mate.append(other_core(probe))

    early = call(
        early_forward_kernel,
        arr((bundles, rays, samples), f32),
        [],
        [VMEM] * 6,
        "forward2_early",
        dense_flops * 3 // 4,
        dense_bytes * 3 // 4,
    )(dense[KEEP_A], dense[KEEP_B], dense[GIVE_A], own[0], own[1], mate[0])
    part2 = call(
        late_forward_kernel,
        part_out,
        [],
        [VMEM] * 3,
        "forward2_late",
        dense_flops // 4,
        dense_bytes // 4,
    )(dense[GIVE_B], mate[1], early)

    (resid2_t,), resid_all2 = residual(part2, token, "residual2", True)
    *sums2, _ = adjoint(dense, resid_all2, "adjoint2")
    resid2, after = call(
        turn_kernel,
        (arr((owned, rays, samples), f32), small_token),
        [],
        [VMEM],
        "turn",
        bytes_accessed=1 << 20,
    )(resid2_t)
    own, mate = [], []
    for grad, sums, part in zip(grad1, sums2, "ab"):
        total = call(
            functools.partial(total_kernel, ny),
            quarter_bf16,
            [order],
            [VMEM, ANY] + [VMEM] * ny,
            "total_" + part,
            bytes_accessed=1 << 19,
        )(grad, after, *sums)
        own.append(total)
        mate.append(other_core(total))
    whole = arr((cells, CBLK, samples), f32)
    so_far, rest = call(
        early_update_kernel,
        (whole, quarter_f32),
        [pltpu.VMEM((3, quarter, CBLK, samples), f32), pltpu.SemaphoreType.DMA((3,))],
        [VMEM] * 4,
        "new_state_early",
        bytes_accessed=3 << 20,
        out_specs=(HBM, VMEM),
    )(base, own[0], own[1], mate[0])
    new_state = call(
        late_update_kernel,
        whole,
        [pltpu.VMEM((quarter, CBLK, samples), f32), pltpu.SemaphoreType.DMA],
        [VMEM, VMEM, HBM],
        "new_state_late",
        bytes_accessed=1 << 20,
        out_specs=HBM,
        input_output_aliases={2: 0},
    )(rest, mate[1], so_far)
    return new_state.reshape(state.shape), resid2


def solution(mesh):
    in_specs = (
        P(("shot", "band"), None, None),
        P(("shot", "band")),
        P(("shot", "band")),
        P("band", None),
        P("band", None),
        P(("shot", "band"), None),
        P(("shot", "band"), None),
    )
    out_specs = (P("band", None), P(("shot", "band"), None, None))
    return jax.shard_map(
        functools.partial(per_device, mesh.shape["shot"], mesh.shape["band"]),
        mesh=mesh,
        in_specs=in_specs,
        out_specs=out_specs,
        check_vma=False,
    )
```

```python
import functools

import jax
import jax.numpy as jnp
from jax import lax
from jax.experimental import pallas as pl
from jax.experimental.pallas import tpu as pltpu
from jax.sharding import PartitionSpec as P

CBLK = 128
GROUP = 64
CHUNKS = 1
FIRST_VMEM = 55 << 20
GIVE_A, KEEP_A, GIVE_B, KEEP_B = range(4)

VMEM = pl.BlockSpec(memory_space=pltpu.VMEM)
SMEM = pl.BlockSpec(memory_space=pltpu.SMEM)
HBM = pl.BlockSpec(memory_space=pltpu.HBM)
ANY = pl.BlockSpec(memory_space=pl.ANY)

bf16, f32, i32 = jnp.bfloat16, jnp.float32, jnp.int32
arr = jax.ShapeDtypeStruct

def call(body, outs, scratch, in_specs, name, flops=0, bytes_accessed=0, vmem=32 << 20, **more):
    if "out_specs" not in more:
        more["out_specs"] = jax.tree.map(lambda _: VMEM, outs)
    return pl.pallas_call(
        body,
        out_shape=outs,
        in_specs=in_specs,
        scratch_shapes=scratch,
        compiler_params=pltpu.CompilerParams(vmem_limit_bytes=vmem),
        cost_estimate=pl.CostEstimate(
            flops=flops, bytes_accessed=bytes_accessed, transcendentals=0
        ),
        name=name,
        **more,
    )


def first_forward_kernel(
    bund_hbm,
    cblk_hbm,
    sens_hbm,
    state_hbm,
    prior_hbm,
    out_ref,
    acc,
    probe,
    bund,
    cblk,
    sens,
    state,
    prior,
    sems,
):
    nblk = sens.shape[0]
    step = nblk // CHUNKS
    cells = state.shape[0]
    half = cells // 2
    small = [
        pltpu.make_async_copy(bund_hbm, bund, sems.at[0]),
        pltpu.make_async_copy(cblk_hbm, cblk, sems.at[1]),
    ]
    fields = []
    for h in range(2):
        part = pl.ds(h * half, half)
        fields.append(
            [
                pltpu.make_async_copy(state_hbm.at[part], state.at[part], sems.at[2 + 2 * h]),
                pltpu.make_async_copy(prior_hbm.at[part], prior.at[part], sems.at[3 + 2 * h]),
            ]
        )

    def block_copy(c):
        part = pl.ds(c * step, step)
        return pltpu.make_async_copy(sens_hbm.at[part], sens.at[part], sems.at[6 + c])

    for copy in small + fields[0] + fields[1] + [block_copy(c) for c in range(CHUNKS)]:
        copy.start()
    acc[...] = jnp.zeros_like(acc)

    for h in range(2):
        part = pl.ds(h * half, half)
        for copy in fields[h]:
            copy.wait()
        probe[part] = (state[part] + 0.5 * prior[part]).astype(bf16)
    for copy in small:
        copy.wait()

    def chunk(c, carry):
        block_copy(c).wait()
        for g in range(step // GROUP):
            ks = [c * step + g * GROUP + j for j in range(GROUP)]
            prods = [
                jnp.dot(sens[k], probe[cblk[k]], preferred_element_type=f32) for k in ks
            ]
            for k, prod in zip(ks, prods):
                acc[bund[k]] += prod
        return carry

    lax.fori_loop(0, CHUNKS, chunk, 0)
    out_ref[...] = acc[...].astype(bf16)


def dense_kernel(bund, cblk, sens, *rest):
    out_refs, (token_ref, total) = rest[:4], rest[4:]
    rays = sens.shape[1]
    quarter = 2 * total.shape[1]
    core = lax.axis_index("shot") % 2
    total[...] = jnp.zeros_like(total)

    def place(k, carry):
        cell = cblk[k]
        kept = jnp.where(cell // (2 * quarter) == core, 1, 0)
        part = 2 * (cell // quarter % 2) + kept
        rows = pl.ds(pl.multiple_of(bund[k] * rays, rays), rays)
        lanes = pl.ds(pl.multiple_of(cell % 2 * CBLK, CBLK), CBLK)
        total[part, cell % quarter // 2, rows, lanes] += sens[k].astype(f32)
        return carry

    lax.fori_loop(0, sens.shape[0], place, 0)
    for part, out_ref in zip((KEEP_B, GIVE_A, KEEP_A, GIVE_B), out_refs):
        out_ref[...] = total[part].astype(bf16)
    token_ref[...] = jnp.zeros_like(token_ref)


def dense_forward(columns, store):
    step = 2 * CBLK
    pairs = columns[0][0].shape[0]
    probe = jnp.concatenate(
        [part[...].reshape(2 * CBLK * pairs, -1) for _, part in columns], axis=0
    )
    for m in range(columns[0][0].shape[1] // step):
        rows = pl.ds(m * step, step)
        lhs = jnp.concatenate(
            [dense[pair, rows, :] for dense, _ in columns for pair in range(pairs)], axis=1
        )
        total = jnp.dot(lhs, probe, preferred_element_type=f32)
        store(pl.ds(2 * m, 2), total.reshape(2, CBLK, -1))


def early_forward_kernel(dense_own_a, dense_own_b, dense_mate_a, own_a, own_b, mate_a, acc):
    def store(rows, value):
        acc[rows] = value

    columns = [(dense_own_a, own_a), (dense_own_b, own_b), (dense_mate_a, mate_a)]
    dense_forward(columns, store)


def late_forward_kernel(dense_mate_b, mate_b, early, out_ref):
    def store(rows, value):
        out_ref[rows] = (early[rows] + value).astype(bf16)

    dense_forward([(dense_mate_b, mate_b)], store)


def adjoint_kernel(resid, *refs):
    lhs = jnp.concatenate([resid[m] for m in range(resid.shape[0])], axis=1)
    count = len(refs) // 2
    for dense, out_ref in zip(refs[:count], refs[count:]):
        for pair in range(dense.shape[0]):
            both = jnp.dot(lhs, dense[pair], preferred_element_type=f32)
            both = both.astype(out_ref.dtype)
            out_ref[2 * pair] = both[:, :CBLK]
            out_ref[2 * pair + 1] = both[:, CBLK:]


def pair_kernel(keep_ref, got_ref, out_ref):
    out_ref[...] = (keep_ref[...] + got_ref[...].astype(f32)).astype(bf16)


def residual_kernel(parts_ref, obs_ref, wt_ref, after_ref, out_ref, *resid_ref):
    for i in range(parts_ref.shape[1]):
        total = parts_ref[0, i].astype(f32)
        for d in range(1, parts_ref.shape[0]):
            total += parts_ref[d, i].astype(f32)
        resid = wt_ref[pl.ds(i, 1), :] * (total.T - obs_ref[pl.ds(i, 1), :])
        if resid_ref:
            resid_ref[0][i] = resid
        rounded = resid.astype(bf16)
        for d in range(parts_ref.shape[0]):
            out_ref[d, i] = rounded


def turn_kernel(in_ref, out_ref, token_ref):
    for i in range(in_ref.shape[0]):
        out_ref[i] = in_ref[i].T
    token_ref[...] = jnp.zeros_like(token_ref)


def prepare_kernel(state, prior, after_ref, field_a, field_b, base_ref):
    quarter = field_a.shape[0]
    own = lax.axis_index("shot") % 2 * (2 * quarter)
    for at, field_ref in ((own, field_a), (own + quarter, field_b)):
        part = pl.ds(at, quarter)
        field_ref[...] = state[part] + prior[part]
    base_ref[...] = state[...] + 0.5 * prior[...]


def sum_over_y(chip_y, part_refs, order, i):
    if len(part_refs) > 2:
        for d, part_ref in enumerate(part_refs):
            order[chip_y ^ d] = part_ref[i]
        parts = [order[y] for y in range(len(part_refs))]
    else:
        parts = [part_ref[i] for part_ref in part_refs]
    total = parts[0].astype(f32)
    for part in parts[1:]:
        total += part.astype(f32)
    return total.T


def probe_kernel(ny, field_ref, *rest):
    part_refs, (out_ref, grad_ref, order) = rest[:ny], rest[ny:]
    for i in range(out_ref.shape[0]):
        grad = sum_over_y(lax.axis_index("shot") // 2, part_refs, order, i)
        grad_ref[i] = grad
        out_ref[i] = (field_ref[i] - 0.25 * grad).astype(bf16)


def total_kernel(ny, grad_ref, after_ref, *rest):
    part_refs, (out_ref, order) = rest[:ny], rest[ny:]
    for i in range(out_ref.shape[0]):
        grad2 = sum_over_y(lax.axis_index("shot") // 2, part_refs, order, i)
        out_ref[i] = (grad_ref[i] + grad2).astype(bf16)


def early_update_kernel(base, own_a, own_b, mate_a, out_hbm, rest_ref, new, sems):
    quarter = own_a.shape[0]
    core = lax.axis_index("shot") % 2
    own, mate = core * (2 * quarter), (1 - core) * (2 * quarter)
    copies = []
    for n, (at, part_ref) in enumerate(((own, own_a), (own + quarter, own_b), (mate, mate_a))):
        new[n] = base[pl.ds(at, quarter)] - 0.125 * part_ref[...].astype(f32)
        copies.append(
            pltpu.make_async_copy(new.at[n], out_hbm.at[pl.ds(at, quarter)], sems.at[n])
        )
        copies[-1].start()
    rest_ref[...] = base[pl.ds(mate + quarter, quarter)]
    for copy in copies:
        copy.wait()


def late_update_kernel(rest_ref, mate_b, so_far_hbm, out_hbm, new, sem):
    quarter = mate_b.shape[0]
    at = (1 - lax.axis_index("shot") % 2) * (2 * quarter) + quarter
    new[...] = rest_ref[...] - 0.125 * mate_b[...].astype(f32)
    copy = pltpu.make_async_copy(new, out_hbm.at[pl.ds(at, quarter)], sem)
    copy.start()
    copy.wait()


def per_device(nshot, nband, sens, bund, cblk, state, prior, observed, pick_weight):
    nblk = sens.shape[0]
    samples = state.shape[1]
    owned, rays = observed.shape
    bundles = owned * nband
    cells = state.shape[0] // CBLK
    quarter = cells // 4
    ny = nshot // 2
    flops = 2 * nblk * rays * CBLK * samples
    sens_bytes = nblk * rays * CBLK * 2

    state_b = state.reshape(cells, CBLK, samples)
    prior_b = prior.reshape(cells, CBLK, samples)

    def other_core(array):
        return lax.ppermute(array, "shot", [(i, i ^ 1) for i in range(nshot)])

    def other_chips(array):
        return [array] + [
            lax.ppermute(array, "shot", [(i, i ^ (2 * d)) for i in range(nshot)])
            for d in range(1, ny)
        ]

    def over_band(array):
        return lax.all_to_all(array, "band", split_axis=0, concat_axis=0, tiled=True)

    part_out = arr((bundles, rays, samples), bf16)
    dense_shape = (quarter // 2, bundles * rays, 2 * CBLK)
    small_token = arr((8, CBLK), f32)
    dense_flops = 2 * bundles * rays * cells * CBLK * samples
    dense_bytes = 2 * bundles * rays * cells * CBLK
    quarter_bf16 = arr((quarter, CBLK, samples), bf16)
    quarter_f32 = arr((quarter, CBLK, samples), f32)
    order = pltpu.VMEM((ny, samples, CBLK), bf16)

    def residual(part, after, name, keep):
        parts = over_band(part).reshape(nband, owned, rays, samples)
        outs = (arr((nband, owned, samples, rays), bf16),)
        if keep:
            outs += (arr((owned, samples, rays), f32),)
        copies, *resid = call(
            residual_kernel, outs, [], [VMEM] * 3 + [ANY], name, bytes_accessed=1 << 20
        )(parts, observed, pick_weight, after)
        return resid, over_band(copies).reshape(bundles, samples, rays)

    def adjoint(dense, resid_all, name):
        def kernel(parts, part):
            return call(
                adjoint_kernel,
                tuple(quarter_f32 if p % 2 else quarter_bf16 for p in parts),
                [],
                [VMEM] * (1 + len(parts)),
                name + part,
                dense_flops * len(parts) // 4,
                dense_bytes * len(parts) // 4,
            )(resid_all, *[dense[p] for p in parts])

        def pair(keep, got, part):
            return call(
                pair_kernel,
                quarter_bf16,
                [],
                [VMEM] * 2,
                name + "_pair" + part,
                bytes_accessed=1 << 19,
            )(keep, got)

        (give_a,) = kernel((GIVE_A,), "_give_a")
        got_a = other_core(give_a)
        keep_a, give_b = kernel((KEEP_A, GIVE_B), "_keep_a")
        got_b = other_core(give_b)
        sums_a = other_chips(pair(keep_a, got_a, "_a"))
        (keep_b,) = kernel((KEEP_B,), "_keep_b")
        sums_b = other_chips(pair(keep_b, got_b, "_b"))
        return sums_a, sums_b, keep_b

    part1 = call(
        first_forward_kernel,
        part_out,
        [
            pltpu.VMEM((bundles, rays, samples), f32),
            pltpu.VMEM((cells, CBLK, samples), bf16),
            pltpu.SMEM((nblk,), i32),
            pltpu.SMEM((nblk,), i32),
            pltpu.VMEM(sens.shape, bf16),
            pltpu.VMEM(state_b.shape, f32),
            pltpu.VMEM(state_b.shape, f32),
            pltpu.SemaphoreType.DMA((6 + CHUNKS,)),
        ],
        [HBM] * 5,
        "forward1",
        flops,
        sens_bytes,
        vmem=FIRST_VMEM,
    )(bund, cblk, sens, state_b, prior_b)
    dense_keep_b, *dense, token = call(
        dense_kernel,
        (arr(dense_shape, bf16),) * 4 + (small_token,),
        [pltpu.VMEM((4,) + dense_shape, f32)],
        [SMEM, SMEM, VMEM],
        "dense",
        0,
        16 << 20,
        vmem=3 * dense_bytes + 2 * sens_bytes + (2 << 20),
    )(bund, cblk, sens)
    dense.append(dense_keep_b)
    _, resid_all1 = residual(part1, token, "residual1", False)
    *sums1, after = adjoint(dense, resid_all1, "adjoint1")

    *fields, base = call(
        prepare_kernel,
        (quarter_f32, quarter_f32, arr((cells, CBLK, samples), f32)),
        [],
        [VMEM, VMEM, ANY],
        "prepare",
        bytes_accessed=4 << 20,
    )(state_b, prior_b, after)
    own, grad1, mate = [], [], []
    for field, sums, part in zip(fields, sums1, "ab"):
        probe, grad = call(
            functools.partial(probe_kernel, ny),
            (quarter_bf16, quarter_f32),
            [order],
            [VMEM] * (1 + ny),
            "probe2_" + part,
            bytes_accessed=1 << 19,
        )(field, *sums)
        own.append(probe)
        grad1.append(grad)
        mate.append(other_core(probe))

    early = call(
        early_forward_kernel,
        arr((bundles, rays, samples), f32),
        [],
        [VMEM] * 6,
        "forward2_early",
        dense_flops * 3 // 4,
        dense_bytes * 3 // 4,
    )(dense[KEEP_A], dense[KEEP_B], dense[GIVE_A], own[0], own[1], mate[0])
    part2 = call(
        late_forward_kernel,
        part_out,
        [],
        [VMEM] * 3,
        "forward2_late",
        dense_flops // 4,
        dense_bytes // 4,
    )(dense[GIVE_B], mate[1], early)

    (resid2_t,), resid_all2 = residual(part2, token, "residual2", True)
    *sums2, _ = adjoint(dense, resid_all2, "adjoint2")
    resid2, after = call(
        turn_kernel,
        (arr((owned, rays, samples), f32), small_token),
        [],
        [VMEM],
        "turn",
        bytes_accessed=1 << 20,
    )(resid2_t)
    own, mate = [], []
    for grad, sums, part in zip(grad1, sums2, "ab"):
        total = call(
            functools.partial(total_kernel, ny),
            quarter_bf16,
            [order],
            [VMEM, ANY] + [VMEM] * ny,
            "total_" + part,
            bytes_accessed=1 << 19,
        )(grad, after, *sums)
        own.append(total)
        mate.append(other_core(total))
    whole = arr((cells, CBLK, samples), f32)
    so_far, rest = call(
        early_update_kernel,
        (whole, quarter_f32),
        [pltpu.VMEM((3, quarter, CBLK, samples), f32), pltpu.SemaphoreType.DMA((3,))],
        [VMEM] * 4,
        "new_state_early",
        bytes_accessed=3 << 20,
        out_specs=(HBM, VMEM),
    )(base, own[0], own[1], mate[0])
    new_state = call(
        late_update_kernel,
        whole,
        [pltpu.VMEM((quarter, CBLK, samples), f32), pltpu.SemaphoreType.DMA],
        [VMEM, VMEM, HBM],
        "new_state_late",
        bytes_accessed=1 << 20,
        out_specs=HBM,
        input_output_aliases={2: 0},
    )(rest, mate[1], so_far)
    return new_state.reshape(state.shape), resid2


def solution(mesh):
    in_specs = (
        P(("shot", "band"), None, None),
        P(("shot", "band")),
        P(("shot", "band")),
        P("band", None),
        P("band", None),
        P(("shot", "band"), None),
        P(("shot", "band"), None),
    )
    out_specs = (P("band", None), P(("shot", "band"), None, None))
    return jax.shard_map(
        functools.partial(per_device, mesh.shape["shot"], mesh.shape["band"]),
        mesh=mesh,
        in_specs=in_specs,
        out_specs=out_specs,
        check_vma=False,
    )
```

```python
import functools

import jax
import jax.numpy as jnp
from jax import lax
from jax.experimental import pallas as pl
from jax.experimental.pallas import tpu as pltpu
from jax.sharding import PartitionSpec as P

CBLK = 128
GROUP = 32
CHUNKS = 2
FIRST_VMEM = 55 << 20
GIVE_A, KEEP_A, GIVE_B, KEEP_B = range(4)

VMEM = pl.BlockSpec(memory_space=pltpu.VMEM)
SMEM = pl.BlockSpec(memory_space=pltpu.SMEM)
HBM = pl.BlockSpec(memory_space=pltpu.HBM)
ANY = pl.BlockSpec(memory_space=pl.ANY)

bf16, f32, i32 = jnp.bfloat16, jnp.float32, jnp.int32
arr = jax.ShapeDtypeStruct

def call(body, outs, scratch, in_specs, name, flops=0, bytes_accessed=0, vmem=32 << 20, **more):
    if "out_specs" not in more:
        more["out_specs"] = jax.tree.map(lambda _: VMEM, outs)
    return pl.pallas_call(
        body,
        out_shape=outs,
        in_specs=in_specs,
        scratch_shapes=scratch,
        compiler_params=pltpu.CompilerParams(vmem_limit_bytes=vmem),
        cost_estimate=pl.CostEstimate(
            flops=flops, bytes_accessed=bytes_accessed, transcendentals=0
        ),
        name=name,
        **more,
    )


def first_forward_kernel(
    bund_hbm,
    cblk_hbm,
    sens_hbm,
    state_hbm,
    prior_hbm,
    out_ref,
    acc,
    probe,
    bund,
    cblk,
    sens,
    state,
    prior,
    sems,
):
    nblk = sens.shape[0]
    step = nblk // CHUNKS
    cells = state.shape[0]
    half = cells // 2
    small = [
        pltpu.make_async_copy(bund_hbm, bund, sems.at[0]),
        pltpu.make_async_copy(cblk_hbm, cblk, sems.at[1]),
    ]
    fields = []
    for h in range(2):
        part = pl.ds(h * half, half)
        fields.append(
            [
                pltpu.make_async_copy(state_hbm.at[part], state.at[part], sems.at[2 + 2 * h]),
                pltpu.make_async_copy(prior_hbm.at[part], prior.at[part], sems.at[3 + 2 * h]),
            ]
        )

    def block_copy(c):
        part = pl.ds(c * step, step)
        return pltpu.make_async_copy(sens_hbm.at[part], sens.at[part], sems.at[6 + c])

    for copy in small + fields[0] + fields[1] + [block_copy(c) for c in range(CHUNKS)]:
        copy.start()
    acc[...] = jnp.zeros_like(acc)

    for h in range(2):
        part = pl.ds(h * half, half)
        for copy in fields[h]:
            copy.wait()
        probe[part] = (state[part] + 0.5 * prior[part]).astype(bf16)
    for copy in small:
        copy.wait()

    def chunk(c, carry):
        block_copy(c).wait()
        for g in range(step // GROUP):
            ks = [c * step + g * GROUP + j for j in range(GROUP)]
            prods = [
                jnp.dot(sens[k], probe[cblk[k]], preferred_element_type=f32) for k in ks
            ]
            for k, prod in zip(ks, prods):
                acc[bund[k]] += prod
        return carry

    lax.fori_loop(0, CHUNKS, chunk, 0)
    out_ref[...] = acc[...].astype(bf16)


def dense_kernel(bund, cblk, sens, *rest):
    out_refs, (token_ref, total) = rest[:4], rest[4:]
    rays = sens.shape[1]
    quarter = 2 * total.shape[1]
    core = lax.axis_index("shot") % 2
    total[...] = jnp.zeros_like(total)

    def place(k, carry):
        cell = cblk[k]
        kept = jnp.where(cell // (2 * quarter) == core, 1, 0)
        part = 2 * (cell // quarter % 2) + kept
        rows = pl.ds(pl.multiple_of(bund[k] * rays, rays), rays)
        lanes = pl.ds(pl.multiple_of(cell % 2 * CBLK, CBLK), CBLK)
        total[part, cell % quarter // 2, rows, lanes] += sens[k].astype(f32)
        return carry

    lax.fori_loop(0, sens.shape[0], place, 0)
    for part, out_ref in zip((KEEP_B, GIVE_A, KEEP_A, GIVE_B), out_refs):
        out_ref[...] = total[part].astype(bf16)
    token_ref[...] = jnp.zeros_like(token_ref)


def dense_forward(columns, store):
    step = 2 * CBLK
    pairs = columns[0][0].shape[0]
    probe = jnp.concatenate(
        [part[...].reshape(2 * CBLK * pairs, -1) for _, part in columns], axis=0
    )
    for m in range(columns[0][0].shape[1] // step):
        rows = pl.ds(m * step, step)
        lhs = jnp.concatenate(
            [dense[pair, rows, :] for dense, _ in columns for pair in range(pairs)], axis=1
        )
        total = jnp.dot(lhs, probe, preferred_element_type=f32)
        store(pl.ds(2 * m, 2), total.reshape(2, CBLK, -1))


def early_forward_kernel(dense_own_a, dense_own_b, dense_mate_a, own_a, own_b, mate_a, acc):
    def store(rows, value):
        acc[rows] = value

    columns = [(dense_own_a, own_a), (dense_own_b, own_b), (dense_mate_a, mate_a)]
    dense_forward(columns, store)


def late_forward_kernel(dense_mate_b, mate_b, early, out_ref):
    def store(rows, value):
        out_ref[rows] = (early[rows] + value).astype(bf16)

    dense_forward([(dense_mate_b, mate_b)], store)


def adjoint_kernel(resid, *refs):
    lhs = jnp.concatenate([resid[m] for m in range(resid.shape[0])], axis=1)
    count = len(refs) // 2
    for dense, out_ref in zip(refs[:count], refs[count:]):
        for pair in range(dense.shape[0]):
            both = jnp.dot(lhs, dense[pair], preferred_element_type=f32)
            both = both.astype(out_ref.dtype)
            out_ref[2 * pair] = both[:, :CBLK]
            out_ref[2 * pair + 1] = both[:, CBLK:]


def pair_kernel(keep_ref, got_ref, out_ref):
    out_ref[...] = (keep_ref[...] + got_ref[...].astype(f32)).astype(bf16)


def residual_kernel(parts_ref, obs_ref, wt_ref, after_ref, out_ref, *resid_ref):
    for i in range(parts_ref.shape[1]):
        total = parts_ref[0, i].astype(f32)
        for d in range(1, parts_ref.shape[0]):
            total += parts_ref[d, i].astype(f32)
        resid = wt_ref[pl.ds(i, 1), :] * (total.T - obs_ref[pl.ds(i, 1), :])
        if resid_ref:
            resid_ref[0][i] = resid
        rounded = resid.astype(bf16)
        for d in range(parts_ref.shape[0]):
            out_ref[d, i] = rounded


def turn_kernel(in_ref, out_ref, token_ref):
    for i in range(in_ref.shape[0]):
        out_ref[i] = in_ref[i].T
    token_ref[...] = jnp.zeros_like(token_ref)


def prepare_kernel(state, prior, after_ref, field_a, field_b, base_ref):
    quarter = field_a.shape[0]
    own = lax.axis_index("shot") % 2 * (2 * quarter)
    for at, field_ref in ((own, field_a), (own + quarter, field_b)):
        part = pl.ds(at, quarter)
        field_ref[...] = state[part] + prior[part]
    base_ref[...] = state[...] + 0.5 * prior[...]


def sum_over_y(chip_y, part_refs, order, i):
    if len(part_refs) > 2:
        for d, part_ref in enumerate(part_refs):
            order[chip_y ^ d] = part_ref[i]
        parts = [order[y] for y in range(len(part_refs))]
    else:
        parts = [part_ref[i] for part_ref in part_refs]
    total = parts[0].astype(f32)
    for part in parts[1:]:
        total += part.astype(f32)
    return total.T


def probe_kernel(ny, field_ref, *rest):
    part_refs, (out_ref, grad_ref, order) = rest[:ny], rest[ny:]
    for i in range(out_ref.shape[0]):
        grad = sum_over_y(lax.axis_index("shot") // 2, part_refs, order, i)
        grad_ref[i] = grad
        out_ref[i] = (field_ref[i] - 0.25 * grad).astype(bf16)


def total_kernel(ny, grad_ref, after_ref, *rest):
    part_refs, (out_ref, order) = rest[:ny], rest[ny:]
    for i in range(out_ref.shape[0]):
        grad2 = sum_over_y(lax.axis_index("shot") // 2, part_refs, order, i)
        out_ref[i] = (grad_ref[i] + grad2).astype(bf16)


def early_update_kernel(base, own_a, own_b, mate_a, out_hbm, rest_ref, new, sems):
    quarter = own_a.shape[0]
    core = lax.axis_index("shot") % 2
    own, mate = core * (2 * quarter), (1 - core) * (2 * quarter)
    copies = []
    for n, (at, part_ref) in enumerate(((own, own_a), (own + quarter, own_b), (mate, mate_a))):
        new[n] = base[pl.ds(at, quarter)] - 0.125 * part_ref[...].astype(f32)
        copies.append(
            pltpu.make_async_copy(new.at[n], out_hbm.at[pl.ds(at, quarter)], sems.at[n])
        )
        copies[-1].start()
    rest_ref[...] = base[pl.ds(mate + quarter, quarter)]
    for copy in copies:
        copy.wait()


def late_update_kernel(rest_ref, mate_b, so_far_hbm, out_hbm, new, sem):
    quarter = mate_b.shape[0]
    at = (1 - lax.axis_index("shot") % 2) * (2 * quarter) + quarter
    new[...] = rest_ref[...] - 0.125 * mate_b[...].astype(f32)
    copy = pltpu.make_async_copy(new, out_hbm.at[pl.ds(at, quarter)], sem)
    copy.start()
    copy.wait()


def per_device(nshot, nband, sens, bund, cblk, state, prior, observed, pick_weight):
    nblk = sens.shape[0]
    samples = state.shape[1]
    owned, rays = observed.shape
    bundles = owned * nband
    cells = state.shape[0] // CBLK
    quarter = cells // 4
    ny = nshot // 2
    flops = 2 * nblk * rays * CBLK * samples
    sens_bytes = nblk * rays * CBLK * 2

    state_b = state.reshape(cells, CBLK, samples)
    prior_b = prior.reshape(cells, CBLK, samples)

    def other_core(array):
        return lax.ppermute(array, "shot", [(i, i ^ 1) for i in range(nshot)])

    def other_chips(array):
        return [array] + [
            lax.ppermute(array, "shot", [(i, i ^ (2 * d)) for i in range(nshot)])
            for d in range(1, ny)
        ]

    def over_band(array):
        return lax.all_to_all(array, "band", split_axis=0, concat_axis=0, tiled=True)

    part_out = arr((bundles, rays, samples), bf16)
    dense_shape = (quarter // 2, bundles * rays, 2 * CBLK)
    small_token = arr((8, CBLK), f32)
    dense_flops = 2 * bundles * rays * cells * CBLK * samples
    dense_bytes = 2 * bundles * rays * cells * CBLK
    quarter_bf16 = arr((quarter, CBLK, samples), bf16)
    quarter_f32 = arr((quarter, CBLK, samples), f32)
    order = pltpu.VMEM((ny, samples, CBLK), bf16)

    def residual(part, after, name, keep):
        parts = over_band(part).reshape(nband, owned, rays, samples)
        outs = (arr((nband, owned, samples, rays), bf16),)
        if keep:
            outs += (arr((owned, samples, rays), f32),)
        copies, *resid = call(
            residual_kernel, outs, [], [VMEM] * 3 + [ANY], name, bytes_accessed=64 << 20
        )(parts, observed, pick_weight, after)
        return resid, over_band(copies).reshape(bundles, samples, rays)

    def adjoint(dense, resid_all, name):
        def kernel(parts, part):
            return call(
                adjoint_kernel,
                tuple(quarter_f32 if p % 2 else quarter_bf16 for p in parts),
                [],
                [VMEM] * (1 + len(parts)),
                name + part,
                dense_flops * len(parts) // 4,
                dense_bytes * len(parts) // 4,
            )(resid_all, *[dense[p] for p in parts])

        def pair(keep, got, part):
            return call(
                pair_kernel,
                quarter_bf16,
                [],
                [VMEM] * 2,
                name + "_pair" + part,
                bytes_accessed=1 << 19,
            )(keep, got)

        (give_a,) = kernel((GIVE_A,), "_give_a")
        got_a = other_core(give_a)
        keep_a, give_b = kernel((KEEP_A, GIVE_B), "_keep_a")
        got_b = other_core(give_b)
        sums_a = other_chips(pair(keep_a, got_a, "_a"))
        (keep_b,) = kernel((KEEP_B,), "_keep_b")
        sums_b = other_chips(pair(keep_b, got_b, "_b"))
        return sums_a, sums_b, keep_b

    part1 = call(
        first_forward_kernel,
        part_out,
        [
            pltpu.VMEM((bundles, rays, samples), f32),
            pltpu.VMEM((cells, CBLK, samples), bf16),
            pltpu.SMEM((nblk,), i32),
            pltpu.SMEM((nblk,), i32),
            pltpu.VMEM(sens.shape, bf16),
            pltpu.VMEM(state_b.shape, f32),
            pltpu.VMEM(state_b.shape, f32),
            pltpu.SemaphoreType.DMA((6 + CHUNKS,)),
        ],
        [HBM] * 5,
        "forward1",
        flops,
        sens_bytes,
        vmem=FIRST_VMEM,
    )(bund, cblk, sens, state_b, prior_b)
    dense_keep_b, *dense, token = call(
        dense_kernel,
        (arr(dense_shape, bf16),) * 4 + (small_token,),
        [pltpu.VMEM((4,) + dense_shape, f32)],
        [SMEM, SMEM, VMEM],
        "dense",
        0,
        16 << 20,
        vmem=3 * dense_bytes + 2 * sens_bytes + (2 << 20),
    )(bund, cblk, sens)
    dense.append(dense_keep_b)
    _, resid_all1 = residual(part1, token, "residual1", False)
    *sums1, after = adjoint(dense, resid_all1, "adjoint1")

    *fields, base = call(
        prepare_kernel,
        (quarter_f32, quarter_f32, arr((cells, CBLK, samples), f32)),
        [],
        [VMEM, VMEM, ANY],
        "prepare",
        bytes_accessed=4 << 20,
    )(state_b, prior_b, after)
    own, grad1, mate = [], [], []
    for field, sums, part in zip(fields, sums1, "ab"):
        probe, grad = call(
            functools.partial(probe_kernel, ny),
            (quarter_bf16, quarter_f32),
            [order],
            [VMEM] * (1 + ny),
            "probe2_" + part,
            bytes_accessed=1 << 19,
        )(field, *sums)
        own.append(probe)
        grad1.append(grad)
        mate.append(other_core(probe))

    early = call(
        early_forward_kernel,
        arr((bundles, rays, samples), f32),
        [],
        [VMEM] * 6,
        "forward2_early",
        dense_flops * 3 // 4,
        dense_bytes * 3 // 4,
    )(dense[KEEP_A], dense[KEEP_B], dense[GIVE_A], own[0], own[1], mate[0])
    part2 = call(
        late_forward_kernel,
        part_out,
        [],
        [VMEM] * 3,
        "forward2_late",
        dense_flops // 4,
        dense_bytes // 4,
    )(dense[GIVE_B], mate[1], early)

    (resid2_t,), resid_all2 = residual(part2, token, "residual2", True)
    *sums2, _ = adjoint(dense, resid_all2, "adjoint2")
    resid2, after = call(
        turn_kernel,
        (arr((owned, rays, samples), f32), small_token),
        [],
        [VMEM],
        "turn",
        bytes_accessed=1 << 20,
    )(resid2_t)
    own, mate = [], []
    for grad, sums, part in zip(grad1, sums2, "ab"):
        total = call(
            functools.partial(total_kernel, ny),
            quarter_bf16,
            [order],
            [VMEM, ANY] + [VMEM] * ny,
            "total_" + part,
            bytes_accessed=1 << 19,
        )(grad, after, *sums)
        own.append(total)
        mate.append(other_core(total))
    whole = arr((cells, CBLK, samples), f32)
    so_far, rest = call(
        early_update_kernel,
        (whole, quarter_f32),
        [pltpu.VMEM((3, quarter, CBLK, samples), f32), pltpu.SemaphoreType.DMA((3,))],
        [VMEM] * 4,
        "new_state_early",
        bytes_accessed=3 << 20,
        out_specs=(HBM, VMEM),
    )(base, own[0], own[1], mate[0])
    new_state = call(
        late_update_kernel,
        whole,
        [pltpu.VMEM((quarter, CBLK, samples), f32), pltpu.SemaphoreType.DMA],
        [VMEM, VMEM, HBM],
        "new_state_late",
        bytes_accessed=1 << 20,
        out_specs=HBM,
        input_output_aliases={2: 0},
    )(rest, mate[1], so_far)
    return new_state.reshape(state.shape), resid2


def solution(mesh):
    in_specs = (
        P(("shot", "band"), None, None),
        P(("shot", "band")),
        P(("shot", "band")),
        P("band", None),
        P("band", None),
        P(("shot", "band"), None),
        P(("shot", "band"), None),
    )
    out_specs = (P("band", None), P(("shot", "band"), None, None))
    return jax.shard_map(
        functools.partial(per_device, mesh.shape["shot"], mesh.shape["band"]),
        mesh=mesh,
        in_specs=in_specs,
        out_specs=out_specs,
        check_vma=False,
    )
```

```python
import functools

import jax
import jax.numpy as jnp
from jax import lax
from jax.experimental import pallas as pl
from jax.experimental.pallas import tpu as pltpu
from jax.sharding import PartitionSpec as P

CBLK = 128
GROUP = 32
CHUNKS = 2
FIRST_VMEM = 55 << 20
GIVE_A, KEEP_A, GIVE_B, KEEP_B = range(4)

VMEM = pl.BlockSpec(memory_space=pltpu.VMEM)
SMEM = pl.BlockSpec(memory_space=pltpu.SMEM)
HBM = pl.BlockSpec(memory_space=pltpu.HBM)
ANY = pl.BlockSpec(memory_space=pl.ANY)

bf16, f32, i32 = jnp.bfloat16, jnp.float32, jnp.int32
arr = jax.ShapeDtypeStruct

def call(body, outs, scratch, in_specs, name, flops=0, bytes_accessed=0, vmem=32 << 20, **more):
    if "out_specs" not in more:
        more["out_specs"] = jax.tree.map(lambda _: VMEM, outs)
    return pl.pallas_call(
        body,
        out_shape=outs,
        in_specs=in_specs,
        scratch_shapes=scratch,
        compiler_params=pltpu.CompilerParams(vmem_limit_bytes=vmem),
        cost_estimate=pl.CostEstimate(
            flops=flops, bytes_accessed=bytes_accessed, transcendentals=0
        ),
        name=name,
        **more,
    )


def first_forward_kernel(
    bund_hbm,
    cblk_hbm,
    sens_hbm,
    state_hbm,
    prior_hbm,
    out_ref,
    acc,
    probe,
    bund,
    cblk,
    sens,
    state,
    prior,
    sems,
):
    nblk = sens.shape[0]
    step = nblk // CHUNKS
    cells = state.shape[0]
    half = cells // 2
    small = [
        pltpu.make_async_copy(bund_hbm, bund, sems.at[0]),
        pltpu.make_async_copy(cblk_hbm, cblk, sems.at[1]),
    ]
    fields = []
    for h in range(2):
        part = pl.ds(h * half, half)
        fields.append(
            [
                pltpu.make_async_copy(state_hbm.at[part], state.at[part], sems.at[2 + 2 * h]),
                pltpu.make_async_copy(prior_hbm.at[part], prior.at[part], sems.at[3 + 2 * h]),
            ]
        )

    def block_copy(c):
        part = pl.ds(c * step, step)
        return pltpu.make_async_copy(sens_hbm.at[part], sens.at[part], sems.at[6 + c])

    for copy in small + fields[0] + fields[1] + [block_copy(c) for c in range(CHUNKS)]:
        copy.start()
    acc[...] = jnp.zeros_like(acc)

    for h in range(2):
        part = pl.ds(h * half, half)
        for copy in fields[h]:
            copy.wait()
        probe[part] = (state[part] + 0.5 * prior[part]).astype(bf16)
    for copy in small:
        copy.wait()

    def chunk(c, carry):
        block_copy(c).wait()
        for g in range(step // GROUP):
            ks = [c * step + g * GROUP + j for j in range(GROUP)]
            prods = [
                jnp.dot(sens[k], probe[cblk[k]], preferred_element_type=f32) for k in ks
            ]
            for k, prod in zip(ks, prods):
                acc[bund[k]] += prod
        return carry

    lax.fori_loop(0, CHUNKS, chunk, 0)
    out_ref[...] = acc[...].astype(bf16)


def dense_kernel(bund, cblk, sens, *rest):
    out_refs, (token_ref, total) = rest[:4], rest[4:]
    rays = sens.shape[1]
    quarter = 2 * total.shape[1]
    core = lax.axis_index("shot") % 2
    total[...] = jnp.zeros_like(total)

    def place(k, carry):
        cell = cblk[k]
        kept = jnp.where(cell // (2 * quarter) == core, 1, 0)
        part = 2 * (cell // quarter % 2) + kept
        rows = pl.ds(pl.multiple_of(bund[k] * rays, rays), rays)
        lanes = pl.ds(pl.multiple_of(cell % 2 * CBLK, CBLK), CBLK)
        total[part, cell % quarter // 2, rows, lanes] += sens[k].astype(f32)
        return carry

    lax.fori_loop(0, sens.shape[0], place, 0)
    for part, out_ref in zip((KEEP_B, GIVE_A, KEEP_A, GIVE_B), out_refs):
        out_ref[...] = total[part].astype(bf16)
    token_ref[...] = jnp.zeros_like(token_ref)


def dense_forward(columns, store):
    step = 2 * CBLK
    pairs = columns[0][0].shape[0]
    probe = jnp.concatenate(
        [part[...].reshape(2 * CBLK * pairs, -1) for _, part in columns], axis=0
    )
    for m in range(columns[0][0].shape[1] // step):
        rows = pl.ds(m * step, step)
        lhs = jnp.concatenate(
            [dense[pair, rows, :] for dense, _ in columns for pair in range(pairs)], axis=1
        )
        total = jnp.dot(lhs, probe, preferred_element_type=f32)
        store(pl.ds(2 * m, 2), total.reshape(2, CBLK, -1))


def early_forward_kernel(dense_own_a, dense_own_b, dense_mate_a, own_a, own_b, mate_a, acc):
    def store(rows, value):
        acc[rows] = value

    columns = [(dense_own_a, own_a), (dense_own_b, own_b), (dense_mate_a, mate_a)]
    dense_forward(columns, store)


def late_forward_kernel(dense_mate_b, mate_b, early, out_ref):
    def store(rows, value):
        out_ref[rows] = (early[rows] + value).astype(bf16)

    dense_forward([(dense_mate_b, mate_b)], store)


def adjoint_kernel(resid, *refs):
    lhs = jnp.concatenate([resid[m] for m in range(resid.shape[0])], axis=1)
    count = len(refs) // 2
    for dense, out_ref in zip(refs[:count], refs[count:]):
        for pair in range(dense.shape[0]):
            both = jnp.dot(lhs, dense[pair], preferred_element_type=f32)
            both = both.astype(out_ref.dtype)
            out_ref[2 * pair] = both[:, :CBLK]
            out_ref[2 * pair + 1] = both[:, CBLK:]


def pair_kernel(keep_ref, got_ref, out_ref):
    out_ref[...] = (keep_ref[...] + got_ref[...].astype(f32)).astype(bf16)


def residual_kernel(parts_ref, obs_ref, wt_ref, after_ref, out_ref, *resid_ref):
    for i in range(parts_ref.shape[1]):
        total = parts_ref[0, i].astype(f32)
        for d in range(1, parts_ref.shape[0]):
            total += parts_ref[d, i].astype(f32)
        resid = wt_ref[pl.ds(i, 1), :] * (total.T - obs_ref[pl.ds(i, 1), :])
        if resid_ref:
            resid_ref[0][i] = resid
        rounded = resid.astype(bf16)
        for d in range(parts_ref.shape[0]):
            out_ref[d, i] = rounded


def turn_kernel(in_ref, out_ref, token_ref):
    for i in range(in_ref.shape[0]):
        out_ref[i] = in_ref[i].T
    token_ref[...] = jnp.zeros_like(token_ref)


def prepare_kernel(state, prior, after_ref, field_a, field_b, base_ref):
    quarter = field_a.shape[0]
    own = lax.axis_index("shot") % 2 * (2 * quarter)
    for at, field_ref in ((own, field_a), (own + quarter, field_b)):
        part = pl.ds(at, quarter)
        field_ref[...] = state[part] + prior[part]
    base_ref[...] = state[...] + 0.5 * prior[...]


def sum_over_y(chip_y, part_refs, order, i):
    if len(part_refs) > 2:
        for d, part_ref in enumerate(part_refs):
            order[chip_y ^ d] = part_ref[i]
        parts = [order[y] for y in range(len(part_refs))]
    else:
        parts = [part_ref[i] for part_ref in part_refs]
    total = parts[0].astype(f32)
    for part in parts[1:]:
        total += part.astype(f32)
    return total.T


def probe_kernel(ny, field_ref, *rest):
    part_refs, (out_ref, grad_ref, order) = rest[:ny], rest[ny:]
    for i in range(out_ref.shape[0]):
        grad = sum_over_y(lax.axis_index("shot") // 2, part_refs, order, i)
        grad_ref[i] = grad
        out_ref[i] = (field_ref[i] - 0.25 * grad).astype(bf16)


def total_kernel(ny, after, grad_ref, *rest):
    rest = rest[after:]
    part_refs, (out_ref, order) = rest[:ny], rest[ny:]
    for i in range(out_ref.shape[0]):
        grad2 = sum_over_y(lax.axis_index("shot") // 2, part_refs, order, i)
        out_ref[i] = (grad_ref[i] + grad2).astype(bf16)


def early_update_kernel(base, own_a, own_b, mate_a, out_hbm, rest_ref, new, sems):
    quarter = own_a.shape[0]
    core = lax.axis_index("shot") % 2
    own, mate = core * (2 * quarter), (1 - core) * (2 * quarter)
    copies = []
    for n, (at, part_ref) in enumerate(((own, own_a), (own + quarter, own_b), (mate, mate_a))):
        new[n] = base[pl.ds(at, quarter)] - 0.125 * part_ref[...].astype(f32)
        copies.append(
            pltpu.make_async_copy(new.at[n], out_hbm.at[pl.ds(at, quarter)], sems.at[n])
        )
        copies[-1].start()
    rest_ref[...] = base[pl.ds(mate + quarter, quarter)]
    for copy in copies:
        copy.wait()


def late_update_kernel(rest_ref, mate_b, so_far_hbm, out_hbm, new, sem):
    quarter = mate_b.shape[0]
    at = (1 - lax.axis_index("shot") % 2) * (2 * quarter) + quarter
    new[...] = rest_ref[...] - 0.125 * mate_b[...].astype(f32)
    copy = pltpu.make_async_copy(new, out_hbm.at[pl.ds(at, quarter)], sem)
    copy.start()
    copy.wait()


def per_device(nshot, nband, sens, bund, cblk, state, prior, observed, pick_weight):
    nblk = sens.shape[0]
    samples = state.shape[1]
    owned, rays = observed.shape
    bundles = owned * nband
    cells = state.shape[0] // CBLK
    quarter = cells // 4
    ny = nshot // 2
    flops = 2 * nblk * rays * CBLK * samples
    sens_bytes = nblk * rays * CBLK * 2

    state_b = state.reshape(cells, CBLK, samples)
    prior_b = prior.reshape(cells, CBLK, samples)

    def other_core(array):
        return lax.ppermute(array, "shot", [(i, i ^ 1) for i in range(nshot)])

    def other_chips(array):
        return [array] + [
            lax.ppermute(array, "shot", [(i, i ^ (2 * d)) for i in range(nshot)])
            for d in range(1, ny)
        ]

    def over_band(array):
        return lax.all_to_all(array, "band", split_axis=0, concat_axis=0, tiled=True)

    part_out = arr((bundles, rays, samples), bf16)
    dense_shape = (quarter // 2, bundles * rays, 2 * CBLK)
    small_token = arr((8, CBLK), f32)
    dense_flops = 2 * bundles * rays * cells * CBLK * samples
    dense_bytes = 2 * bundles * rays * cells * CBLK
    quarter_bf16 = arr((quarter, CBLK, samples), bf16)
    quarter_f32 = arr((quarter, CBLK, samples), f32)
    order = pltpu.VMEM((ny, samples, CBLK), bf16)

    def residual(part, after, name, keep):
        parts = over_band(part).reshape(nband, owned, rays, samples)
        outs = (arr((nband, owned, samples, rays), bf16),)
        if keep:
            outs += (arr((owned, samples, rays), f32),)
        copies, *resid = call(
            residual_kernel, outs, [], [VMEM] * 3 + [ANY], name, bytes_accessed=1 << 20
        )(parts, observed, pick_weight, after)
        return resid, over_band(copies).reshape(bundles, samples, rays)

    def adjoint(dense, resid_all, name):
        def kernel(parts, part):
            return call(
                adjoint_kernel,
                tuple(quarter_f32 if p % 2 else quarter_bf16 for p in parts),
                [],
                [VMEM] * (1 + len(parts)),
                name + part,
                dense_flops * len(parts) // 4,
                dense_bytes * len(parts) // 4,
            )(resid_all, *[dense[p] for p in parts])

        def pair(keep, got, part):
            return call(
                pair_kernel,
                quarter_bf16,
                [],
                [VMEM] * 2,
                name + "_pair" + part,
                bytes_accessed=1 << 19,
            )(keep, got)

        (give_a,) = kernel((GIVE_A,), "_give_a")
        got_a = other_core(give_a)
        keep_a, give_b = kernel((KEEP_A, GIVE_B), "_keep_a")
        got_b = other_core(give_b)
        sums_a = other_chips(pair(keep_a, got_a, "_a"))
        (keep_b,) = kernel((KEEP_B,), "_keep_b")
        sums_b = other_chips(pair(keep_b, got_b, "_b"))
        return sums_a, sums_b, keep_b

    part1 = call(
        first_forward_kernel,
        part_out,
        [
            pltpu.VMEM((bundles, rays, samples), f32),
            pltpu.VMEM((cells, CBLK, samples), bf16),
            pltpu.SMEM((nblk,), i32),
            pltpu.SMEM((nblk,), i32),
            pltpu.VMEM(sens.shape, bf16),
            pltpu.VMEM(state_b.shape, f32),
            pltpu.VMEM(state_b.shape, f32),
            pltpu.SemaphoreType.DMA((6 + CHUNKS,)),
        ],
        [HBM] * 5,
        "forward1",
        flops,
        sens_bytes,
        vmem=FIRST_VMEM,
    )(bund, cblk, sens, state_b, prior_b)
    dense_keep_b, *dense, token = call(
        dense_kernel,
        (arr(dense_shape, bf16),) * 4 + (small_token,),
        [pltpu.VMEM((4,) + dense_shape, f32)],
        [SMEM, SMEM, VMEM],
        "dense",
        0,
        16 << 20,
        vmem=3 * dense_bytes + 2 * sens_bytes + (2 << 20),
    )(bund, cblk, sens)
    dense.append(dense_keep_b)
    _, resid_all1 = residual(part1, token, "residual1", False)
    *sums1, after = adjoint(dense, resid_all1, "adjoint1")

    *fields, base = call(
        prepare_kernel,
        (quarter_f32, quarter_f32, arr((cells, CBLK, samples), f32)),
        [],
        [VMEM, VMEM, ANY],
        "prepare",
        bytes_accessed=4 << 20,
    )(state_b, prior_b, after)
    own, grad1, mate = [], [], []
    for field, sums, part in zip(fields, sums1, "ab"):
        probe, grad = call(
            functools.partial(probe_kernel, ny),
            (quarter_bf16, quarter_f32),
            [order],
            [VMEM] * (1 + ny),
            "probe2_" + part,
            bytes_accessed=1 << 19,
        )(field, *sums)
        own.append(probe)
        grad1.append(grad)
        mate.append(other_core(probe))

    early = call(
        early_forward_kernel,
        arr((bundles, rays, samples), f32),
        [],
        [VMEM] * 6,
        "forward2_early",
        dense_flops * 3 // 4,
        dense_bytes * 3 // 4,
    )(dense[KEEP_A], dense[KEEP_B], dense[GIVE_A], own[0], own[1], mate[0])
    part2 = call(
        late_forward_kernel,
        part_out,
        [],
        [VMEM] * 3,
        "forward2_late",
        dense_flops // 4,
        dense_bytes // 4,
    )(dense[GIVE_B], mate[1], early)

    (resid2_t,), resid_all2 = residual(part2, token, "residual2", True)
    *sums2, _ = adjoint(dense, resid_all2, "adjoint2")
    resid2, turned = call(
        turn_kernel,
        (arr((owned, rays, samples), f32), small_token),
        [],
        [VMEM],
        "turn",
        bytes_accessed=1 << 20,
    )(resid2_t)
    own, mate, after = [], [], [turned, dense[GIVE_A], dense[KEEP_A], dense[GIVE_B]]
    for grad, sums, part in zip(grad1, sums2, "ab"):
        total = call(
            functools.partial(total_kernel, ny, len(after)),
            quarter_bf16,
            [order],
            [VMEM] + [ANY] * len(after) + [VMEM] * ny,
            "total_" + part,
            bytes_accessed=1 << 19,
        )(grad, *after, *sums)
        own.append(total)
        after = []
        mate.append(other_core(total))
    whole = arr((cells, CBLK, samples), f32)
    so_far, rest = call(
        early_update_kernel,
        (whole, quarter_f32),
        [pltpu.VMEM((3, quarter, CBLK, samples), f32), pltpu.SemaphoreType.DMA((3,))],
        [VMEM] * 4,
        "new_state_early",
        bytes_accessed=3 << 20,
        out_specs=(HBM, VMEM),
    )(base, own[0], own[1], mate[0])
    new_state = call(
        late_update_kernel,
        whole,
        [pltpu.VMEM((quarter, CBLK, samples), f32), pltpu.SemaphoreType.DMA],
        [VMEM, VMEM, HBM],
        "new_state_late",
        bytes_accessed=1 << 20,
        out_specs=HBM,
        input_output_aliases={2: 0},
    )(rest, mate[1], so_far)
    return new_state.reshape(state.shape), resid2


def solution(mesh):
    in_specs = (
        P(("shot", "band"), None, None),
        P(("shot", "band")),
        P(("shot", "band")),
        P("band", None),
        P("band", None),
        P(("shot", "band"), None),
        P(("shot", "band"), None),
    )
    out_specs = (P("band", None), P(("shot", "band"), None, None))
    return jax.shard_map(
        functools.partial(per_device, mesh.shape["shot"], mesh.shape["band"]),
        mesh=mesh,
        in_specs=in_specs,
        out_specs=out_specs,
        check_vma=False,
    )
```

```python
import functools

import jax
import jax.numpy as jnp
from jax import lax
from jax.experimental import pallas as pl
from jax.experimental.pallas import tpu as pltpu
from jax.sharding import PartitionSpec as P

CBLK = 128
GROUP = 32
CHUNKS = 2
FIRST_VMEM = 55 << 20

VMEM = pl.BlockSpec(memory_space=pltpu.VMEM)
SMEM = pl.BlockSpec(memory_space=pltpu.SMEM)
HBM = pl.BlockSpec(memory_space=pltpu.HBM)
ANY = pl.BlockSpec(memory_space=pl.ANY)

bf16, f32, i32 = jnp.bfloat16, jnp.float32, jnp.int32
arr = jax.ShapeDtypeStruct

def call(body, outs, scratch, in_specs, name, flops=0, bytes_accessed=0, vmem=32 << 20, **more):
    if "out_specs" not in more:
        more["out_specs"] = jax.tree.map(lambda _: VMEM, outs)
    return pl.pallas_call(
        body,
        out_shape=outs,
        in_specs=in_specs,
        scratch_shapes=scratch,
        compiler_params=pltpu.CompilerParams(vmem_limit_bytes=vmem),
        cost_estimate=pl.CostEstimate(
            flops=flops, bytes_accessed=bytes_accessed, transcendentals=0
        ),
        name=name,
        **more,
    )


def first_forward_kernel(
    bund_hbm,
    cblk_hbm,
    sens_hbm,
    state_hbm,
    prior_hbm,
    out_ref,
    acc,
    probe,
    bund,
    cblk,
    sens,
    state,
    prior,
    sems,
):
    nblk = sens.shape[0]
    step = nblk // CHUNKS
    cells = state.shape[0]
    half = cells // 2
    small = [
        pltpu.make_async_copy(bund_hbm, bund, sems.at[0]),
        pltpu.make_async_copy(cblk_hbm, cblk, sems.at[1]),
    ]
    fields = []
    for h in range(2):
        part = pl.ds(h * half, half)
        fields.append(
            [
                pltpu.make_async_copy(state_hbm.at[part], state.at[part], sems.at[2 + 2 * h]),
                pltpu.make_async_copy(prior_hbm.at[part], prior.at[part], sems.at[3 + 2 * h]),
            ]
        )

    def block_copy(c):
        part = pl.ds(c * step, step)
        return pltpu.make_async_copy(sens_hbm.at[part], sens.at[part], sems.at[6 + c])

    for copy in small + fields[0] + fields[1] + [block_copy(c) for c in range(CHUNKS)]:
        copy.start()
    acc[...] = jnp.zeros_like(acc)

    for h in range(2):
        part = pl.ds(h * half, half)
        for copy in fields[h]:
            copy.wait()
        probe[part] = (state[part] + 0.5 * prior[part]).astype(bf16)
    for copy in small:
        copy.wait()

    def chunk(c, carry):
        block_copy(c).wait()
        for g in range(step // GROUP):
            ks = [c * step + g * GROUP + j for j in range(GROUP)]
            prods = [
                jnp.dot(sens[k], probe[cblk[k]], preferred_element_type=f32) for k in ks
            ]
            for k, prod in zip(ks, prods):
                acc[bund[k]] += prod
        return carry

    lax.fori_loop(0, CHUNKS, chunk, 0)
    out_ref[...] = acc[...].astype(bf16)


def sizes_of(pairs):
    return (pairs // 4,) * 4


def dense_kernel(bund, cblk, sens, *rest):
    out_refs, (token_ref, total) = rest[:-2], rest[-2:]
    rays = sens.shape[1]
    pairs = total.shape[1]
    core = lax.axis_index("shot") % 2
    total[...] = jnp.zeros_like(total)

    def place(k, carry):
        pair = cblk[k] // 2
        kept = jnp.where(pair // pairs == core, 1, 0)
        rows = pl.ds(pl.multiple_of(bund[k] * rays, rays), rays)
        lanes = pl.ds(pl.multiple_of(cblk[k] % 2 * CBLK, CBLK), CBLK)
        total[kept, pair % pairs, rows, lanes] += sens[k].astype(f32)
        return carry

    lax.fori_loop(0, sens.shape[0], place, 0)
    at = 0
    for p in range(len(out_refs) // 2):
        size = out_refs[2 * p].shape[0]
        for kept in range(2):
            out_refs[2 * p + kept][...] = total[kept, at : at + size].astype(bf16)
        at += size
    token_ref[...] = jnp.zeros_like(token_ref)


def dense_forward(columns, store):
    step = 2 * CBLK
    probe = jnp.concatenate(
        [part[...].reshape(CBLK * part.shape[0], -1) for _, part in columns], axis=0
    )
    for m in range(columns[0][0].shape[1] // step):
        rows = pl.ds(m * step, step)
        lhs = jnp.concatenate(
            [dense[pair, rows, :] for dense, _ in columns for pair in range(dense.shape[0])],
            axis=1,
        )
        total = jnp.dot(lhs, probe, preferred_element_type=f32)
        store(pl.ds(2 * m, 2), total.reshape(2, CBLK, -1))


def early_forward_kernel(*refs):
    acc = refs[-1]
    count = len(refs) // 2

    def store(rows, value):
        acc[rows] = value

    dense_forward(list(zip(refs[:count], refs[count : 2 * count])), store)


def late_forward_kernel(dense_last, mate_last, early, out_ref):
    def store(rows, value):
        out_ref[rows] = (early[rows] + value).astype(bf16)

    dense_forward([(dense_last, mate_last)], store)


def adjoint_kernel(resid, after_ref, *refs):
    lhs = jnp.concatenate([resid[m] for m in range(resid.shape[0])], axis=1)
    count = len(refs) // 2
    for dense, out_ref in zip(refs[:count], refs[count:]):
        for pair in range(dense.shape[0]):
            both = jnp.dot(lhs, dense[pair], preferred_element_type=f32)
            both = both.astype(out_ref.dtype)
            out_ref[2 * pair] = both[:, :CBLK]
            out_ref[2 * pair + 1] = both[:, CBLK:]


def pair_kernel(keep_ref, got_ref, after_ref, out_ref):
    out_ref[...] = (keep_ref[...] + got_ref[...].astype(f32)).astype(bf16)


def residual_kernel(parts_ref, obs_ref, wt_ref, after_ref, out_ref, *resid_ref):
    for i in range(parts_ref.shape[1]):
        total = parts_ref[0, i].astype(f32)
        for d in range(1, parts_ref.shape[0]):
            total += parts_ref[d, i].astype(f32)
        resid = wt_ref[pl.ds(i, 1), :] * (total.T - obs_ref[pl.ds(i, 1), :])
        if resid_ref:
            resid_ref[0][i] = resid
        rounded = resid.astype(bf16)
        for d in range(parts_ref.shape[0]):
            out_ref[d, i] = rounded


def turn_kernel(in_ref, out_ref, token_ref):
    for i in range(in_ref.shape[0]):
        out_ref[i] = in_ref[i].T
    token_ref[...] = jnp.zeros_like(token_ref)


def prepare_kernel(state, prior, after_ref, *rest):
    field_refs, base_ref = rest[:-1], rest[-1]
    at = lax.axis_index("shot") % 2 * (state.shape[0] // 2)
    for field_ref in field_refs:
        part = pl.ds(at, field_ref.shape[0])
        field_ref[...] = state[part] + prior[part]
        at += field_ref.shape[0]
    base_ref[...] = state[...] + 0.5 * prior[...]


def sum_over_y(chip_y, part_refs, order, i):
    if len(part_refs) > 2:
        for d, part_ref in enumerate(part_refs):
            order[chip_y ^ d] = part_ref[i]
        parts = [order[y] for y in range(len(part_refs))]
    else:
        parts = [part_ref[i] for part_ref in part_refs]
    total = parts[0].astype(f32)
    for part in parts[1:]:
        total += part.astype(f32)
    return total.T


def probe_kernel(ny, field_ref, after_ref, *rest):
    part_refs, (out_ref, grad_ref, order) = rest[:ny], rest[ny:]
    for i in range(out_ref.shape[0]):
        grad = sum_over_y(lax.axis_index("shot") // 2, part_refs, order, i)
        grad_ref[i] = grad
        out_ref[i] = (field_ref[i] - 0.25 * grad).astype(bf16)


def total_kernel(ny, after, grad_ref, *rest):
    rest = rest[after:]
    part_refs, (out_ref, order) = rest[:ny], rest[ny:]
    for i in range(out_ref.shape[0]):
        grad2 = sum_over_y(lax.axis_index("shot") // 2, part_refs, order, i)
        out_ref[i] = (grad_ref[i] + grad2).astype(bf16)


def early_update_kernel(parts, base, *refs):
    part_refs, (out_hbm, rest_ref, new, sems) = refs[:-4], refs[-4:]
    half = base.shape[0] // 2
    core = lax.axis_index("shot") % 2
    own, mate = core * half, (1 - core) * half
    done, copies = 0, []
    for n, part_ref in enumerate(part_refs):
        size = part_ref.shape[0]
        at = own + done if n < parts else mate + done - half
        new[done : done + size] = base[pl.ds(at, size)] - 0.125 * part_ref[...].astype(f32)
        copies.append(
            pltpu.make_async_copy(
                new.at[pl.ds(done, size)], out_hbm.at[pl.ds(at, size)], sems.at[n]
            )
        )
        copies[-1].start()
        done += size
    rest_ref[...] = base[pl.ds(mate + done - half, rest_ref.shape[0])]
    for copy in copies:
        copy.wait()


def late_update_kernel(rest_ref, mate_last, so_far_hbm, out_hbm, new, sem):
    size = mate_last.shape[0]
    half = out_hbm.shape[0] // 2
    at = (2 - lax.axis_index("shot") % 2) * half - size
    new[...] = rest_ref[...] - 0.125 * mate_last[...].astype(f32)
    copy = pltpu.make_async_copy(new, out_hbm.at[pl.ds(at, size)], sem)
    copy.start()
    copy.wait()


def per_device(nshot, nband, sens, bund, cblk, state, prior, observed, pick_weight):
    nblk = sens.shape[0]
    samples = state.shape[1]
    owned, rays = observed.shape
    bundles = owned * nband
    cells = state.shape[0] // CBLK
    sizes = sizes_of(cells // 4)
    parts = len(sizes)
    ny = nshot // 2
    flops = 2 * nblk * rays * CBLK * samples
    sens_bytes = nblk * rays * CBLK * 2

    state_b = state.reshape(cells, CBLK, samples)
    prior_b = prior.reshape(cells, CBLK, samples)

    def other_core(array):
        return lax.ppermute(array, "shot", [(i, i ^ 1) for i in range(nshot)])

    def other_chips(array):
        return [array] + [
            lax.ppermute(array, "shot", [(i, i ^ (2 * d)) for i in range(nshot)])
            for d in range(1, ny)
        ]

    def over_band(array):
        return lax.all_to_all(array, "band", split_axis=0, concat_axis=0, tiled=True)

    part_out = arr((bundles, rays, samples), bf16)
    dense_bf16 = [arr((size, bundles * rays, 2 * CBLK), bf16) for size in sizes]
    small_token = arr((8, CBLK), f32)
    dense_flops = 2 * bundles * rays * cells * CBLK * samples
    dense_bytes = 2 * bundles * rays * cells * CBLK
    part_bf16 = [arr((2 * size, CBLK, samples), bf16) for size in sizes]
    part_f32 = [arr((2 * size, CBLK, samples), f32) for size in sizes]
    order = pltpu.VMEM((ny, samples, CBLK), bf16)

    def residual(part, after, name, keep):
        parts = over_band(part).reshape(nband, owned, rays, samples)
        outs = (arr((nband, owned, samples, rays), bf16),)
        if keep:
            outs += (arr((owned, samples, rays), f32),)
        copies, *resid = call(
            residual_kernel, outs, [], [VMEM] * 3 + [ANY], name, bytes_accessed=1 << 20
        )(parts, observed, pick_weight, after)
        return resid, over_band(copies).reshape(bundles, samples, rays)

    def adjoint(dense, resid_all, name):
        def kernel(picked, after):
            share = sum(sizes[p // 2] for p in picked)
            return call(
                adjoint_kernel,
                tuple(part_f32[p // 2] if p % 2 else part_bf16[p // 2] for p in picked),
                [],
                [VMEM, ANY] + [VMEM] * len(picked),
                name,
                dense_flops * 2 * share // cells,
                dense_bytes * 2 * share // cells,
            )(resid_all, after, *[dense[p] for p in picked])

        sums = []
        (give,) = kernel((0,), token)
        before = token
        for part in range(parts):
            got = other_core(give)
            if part + 1 < parts:
                keep, give = kernel((2 * part + 1, 2 * part + 2), before if part else give)
            else:
                (keep,) = kernel((2 * part + 1,), before)
            pair = call(
                pair_kernel,
                part_bf16[part],
                [],
                [VMEM, VMEM, ANY],
                name + "_pair",
                bytes_accessed=1 << 19,
            )(keep, got, before)
            before = pair
            sums.append(other_chips(pair))
        return sums, keep

    part1 = call(
        first_forward_kernel,
        part_out,
        [
            pltpu.VMEM((bundles, rays, samples), f32),
            pltpu.VMEM((cells, CBLK, samples), bf16),
            pltpu.SMEM((nblk,), i32),
            pltpu.SMEM((nblk,), i32),
            pltpu.VMEM(sens.shape, bf16),
            pltpu.VMEM(state_b.shape, f32),
            pltpu.VMEM(state_b.shape, f32),
            pltpu.SemaphoreType.DMA((6 + CHUNKS,)),
        ],
        [HBM] * 5,
        "forward1",
        flops,
        sens_bytes,
        vmem=FIRST_VMEM,
    )(bund, cblk, sens, state_b, prior_b)
    *dense, token = call(
        dense_kernel,
        tuple(d for d in dense_bf16 for _ in range(2)) + (small_token,),
        [pltpu.VMEM((2, cells // 4, bundles * rays, 2 * CBLK), f32)],
        [SMEM, SMEM, VMEM],
        "dense",
        0,
        16 << 20,
        vmem=3 * dense_bytes + 2 * sens_bytes + (2 << 20),
    )(bund, cblk, sens)
    _, resid_all1 = residual(part1, token, "residual1", False)
    sums1, after = adjoint(dense, resid_all1, "adjoint1")

    *fields, base = call(
        prepare_kernel,
        (*part_f32, arr((cells, CBLK, samples), f32)),
        [],
        [VMEM, VMEM, ANY],
        "prepare",
        bytes_accessed=4 << 20,
    )(state_b, prior_b, after)
    own, grad1, mate, before = [], [], [], token
    for part, (field, sums) in enumerate(zip(fields, sums1)):
        probe, grad = call(
            functools.partial(probe_kernel, ny),
            (part_bf16[part], part_f32[part]),
            [order],
            [VMEM, ANY] + [VMEM] * ny,
            "probe2",
            bytes_accessed=1 << 19,
        )(field, before, *sums)
        before = probe
        own.append(probe)
        grad1.append(grad)
        mate.append(other_core(probe))

    early = call(
        early_forward_kernel,
        arr((bundles, rays, samples), f32),
        [],
        [VMEM] * (4 * parts - 2),
        "forward2_early",
        dense_flops * 7 // 8,
        dense_bytes * 7 // 8,
    )(*dense[1::2], *dense[0:-2:2], *own, *mate[:-1])
    part2 = call(
        late_forward_kernel,
        part_out,
        [],
        [VMEM] * 3,
        "forward2_late",
        dense_flops // 8,
        dense_bytes // 8,
    )(dense[-2], mate[-1], early)

    (resid2_t,), resid_all2 = residual(part2, token, "residual2", True)
    sums2, _ = adjoint(dense, resid_all2, "adjoint2")
    resid2, turned = call(
        turn_kernel,
        (arr((owned, rays, samples), f32), small_token),
        [],
        [VMEM],
        "turn",
        bytes_accessed=1 << 20,
    )(resid2_t)
    own, mate, after = [], [], [turned, *dense[:-1]]
    for part, (grad, sums) in enumerate(zip(grad1, sums2)):
        total = call(
            functools.partial(total_kernel, ny, len(after)),
            part_bf16[part],
            [order],
            [VMEM] + [ANY] * len(after) + [VMEM] * ny,
            "total",
            bytes_accessed=1 << 19,
        )(grad, *after, *sums)
        own.append(total)
        after = [total]
        mate.append(other_core(total))
    whole = arr((cells, CBLK, samples), f32)
    last = 2 * sizes[-1]
    so_far, rest = call(
        functools.partial(early_update_kernel, parts),
        (whole, part_f32[-1]),
        [
            pltpu.VMEM((cells - last, CBLK, samples), f32),
            pltpu.SemaphoreType.DMA((2 * parts - 1,)),
        ],
        [VMEM] * (2 * parts),
        "new_state_early",
        bytes_accessed=3 << 20,
        out_specs=(HBM, VMEM),
    )(base, *own, *mate[:-1])
    new_state = call(
        late_update_kernel,
        whole,
        [pltpu.VMEM((last, CBLK, samples), f32), pltpu.SemaphoreType.DMA],
        [VMEM, VMEM, HBM],
        "new_state_late",
        bytes_accessed=1 << 20,
        out_specs=HBM,
        input_output_aliases={2: 0},
    )(rest, mate[-1], so_far)
    return new_state.reshape(state.shape), resid2


def solution(mesh):
    in_specs = (
        P(("shot", "band"), None, None),
        P(("shot", "band")),
        P(("shot", "band")),
        P("band", None),
        P("band", None),
        P(("shot", "band"), None),
        P(("shot", "band"), None),
    )
    out_specs = (P("band", None), P(("shot", "band"), None, None))
    return jax.shard_map(
        functools.partial(per_device, mesh.shape["shot"], mesh.shape["band"]),
        mesh=mesh,
        in_specs=in_specs,
        out_specs=out_specs,
        check_vma=False,
    )
```

```python
import functools

import jax
import jax.numpy as jnp
from jax import lax
from jax.experimental import pallas as pl
from jax.experimental.pallas import tpu as pltpu
from jax.sharding import PartitionSpec as P

CBLK = 128
GROUP = 32
CHUNKS = 2
FIRST_VMEM = 55 << 20

VMEM = pl.BlockSpec(memory_space=pltpu.VMEM)
SMEM = pl.BlockSpec(memory_space=pltpu.SMEM)
HBM = pl.BlockSpec(memory_space=pltpu.HBM)
ANY = pl.BlockSpec(memory_space=pl.ANY)

bf16, f32, i32 = jnp.bfloat16, jnp.float32, jnp.int32
arr = jax.ShapeDtypeStruct

def call(body, outs, scratch, in_specs, name, flops=0, bytes_accessed=0, vmem=32 << 20, **more):
    if "out_specs" not in more:
        more["out_specs"] = jax.tree.map(lambda _: VMEM, outs)
    return pl.pallas_call(
        body,
        out_shape=outs,
        in_specs=in_specs,
        scratch_shapes=scratch,
        compiler_params=pltpu.CompilerParams(vmem_limit_bytes=vmem),
        cost_estimate=pl.CostEstimate(
            flops=flops, bytes_accessed=bytes_accessed, transcendentals=0
        ),
        name=name,
        **more,
    )


def first_forward_kernel(
    bund_hbm,
    cblk_hbm,
    sens_hbm,
    state_hbm,
    prior_hbm,
    out_ref,
    acc,
    probe,
    bund,
    cblk,
    sens,
    state,
    prior,
    sems,
):
    nblk = sens.shape[0]
    step = nblk // CHUNKS
    cells = state.shape[0]
    half = cells // 2
    small = [
        pltpu.make_async_copy(bund_hbm, bund, sems.at[0]),
        pltpu.make_async_copy(cblk_hbm, cblk, sems.at[1]),
    ]
    fields = []
    for h in range(2):
        part = pl.ds(h * half, half)
        fields.append(
            [
                pltpu.make_async_copy(state_hbm.at[part], state.at[part], sems.at[2 + 2 * h]),
                pltpu.make_async_copy(prior_hbm.at[part], prior.at[part], sems.at[3 + 2 * h]),
            ]
        )

    def block_copy(c):
        part = pl.ds(c * step, step)
        return pltpu.make_async_copy(sens_hbm.at[part], sens.at[part], sems.at[6 + c])

    for copy in small + fields[0] + fields[1] + [block_copy(0)]:
        copy.start()
    acc[...] = jnp.zeros_like(acc)

    for h in range(2):
        part = pl.ds(h * half, half)
        for copy in fields[h]:
            copy.wait()
        if h == 0:
            for c in range(1, CHUNKS):
                block_copy(c).start()
        probe[part] = (state[part] + 0.5 * prior[part]).astype(bf16)
    for copy in small:
        copy.wait()

    def chunk(c, carry):
        block_copy(c).wait()
        for g in range(step // GROUP):
            ks = [c * step + g * GROUP + j for j in range(GROUP)]
            prods = [
                jnp.dot(sens[k], probe[cblk[k]], preferred_element_type=f32) for k in ks
            ]
            for k, prod in zip(ks, prods):
                acc[bund[k]] += prod
        return carry

    lax.fori_loop(0, CHUNKS, chunk, 0)
    out_ref[...] = acc[...].astype(bf16)


def sizes_of(pairs):
    return (pairs - 2 * (pairs // 4), pairs // 4, pairs // 4)


def dense_kernel(bund, cblk, sens, *rest):
    out_refs, (token_ref, total) = rest[:-2], rest[-2:]
    rays = sens.shape[1]
    pairs = total.shape[1]
    core = lax.axis_index("shot") % 2
    total[...] = jnp.zeros_like(total)

    def place(k, carry):
        pair = cblk[k] // 2
        kept = jnp.where(pair // pairs == core, 1, 0)
        rows = pl.ds(pl.multiple_of(bund[k] * rays, rays), rays)
        lanes = pl.ds(pl.multiple_of(cblk[k] % 2 * CBLK, CBLK), CBLK)
        total[kept, pair % pairs, rows, lanes] += sens[k].astype(f32)
        return carry

    lax.fori_loop(0, sens.shape[0], place, 0)
    at = 0
    for p in range(len(out_refs) // 2):
        size = out_refs[2 * p].shape[0]
        for kept in range(2):
            out_refs[2 * p + kept][...] = total[kept, at : at + size].astype(bf16)
        at += size
    token_ref[...] = jnp.zeros_like(token_ref)


def dense_forward(columns, store):
    step = 2 * CBLK
    probe = jnp.concatenate(
        [part[...].reshape(CBLK * part.shape[0], -1) for _, part in columns], axis=0
    )
    for m in range(columns[0][0].shape[1] // step):
        rows = pl.ds(m * step, step)
        lhs = jnp.concatenate(
            [dense[pair, rows, :] for dense, _ in columns for pair in range(dense.shape[0])],
            axis=1,
        )
        total = jnp.dot(lhs, probe, preferred_element_type=f32)
        store(pl.ds(2 * m, 2), total.reshape(2, CBLK, -1))


def early_forward_kernel(*refs):
    acc = refs[-1]
    count = len(refs) // 2

    def store(rows, value):
        acc[rows] = value

    dense_forward(list(zip(refs[:count], refs[count : 2 * count])), store)


def late_forward_kernel(dense_last, mate_last, early, out_ref):
    def store(rows, value):
        out_ref[rows] = (early[rows] + value).astype(bf16)

    dense_forward([(dense_last, mate_last)], store)


def adjoint_kernel(resid, after_ref, *refs):
    lhs = jnp.concatenate([resid[m] for m in range(resid.shape[0])], axis=1)
    count = len(refs) // 2
    for dense, out_ref in zip(refs[:count], refs[count:]):
        for pair in range(dense.shape[0]):
            both = jnp.dot(lhs, dense[pair], preferred_element_type=f32)
            both = both.astype(out_ref.dtype)
            out_ref[2 * pair] = both[:, :CBLK]
            out_ref[2 * pair + 1] = both[:, CBLK:]


def pair_kernel(keep_ref, got_ref, after_ref, out_ref):
    out_ref[...] = (keep_ref[...] + got_ref[...].astype(f32)).astype(bf16)


def residual_kernel(parts_ref, obs_ref, wt_ref, after_ref, out_ref, *resid_ref):
    for i in range(parts_ref.shape[1]):
        total = parts_ref[0, i].astype(f32)
        for d in range(1, parts_ref.shape[0]):
            total += parts_ref[d, i].astype(f32)
        resid = wt_ref[pl.ds(i, 1), :] * (total.T - obs_ref[pl.ds(i, 1), :])
        if resid_ref:
            resid_ref[0][i] = resid
        rounded = resid.astype(bf16)
        for d in range(parts_ref.shape[0]):
            out_ref[d, i] = rounded


def turn_kernel(in_ref, out_ref, token_ref):
    for i in range(in_ref.shape[0]):
        out_ref[i] = in_ref[i].T
    token_ref[...] = jnp.zeros_like(token_ref)


def prepare_kernel(state, prior, after_ref, *rest):
    field_refs, base_ref = rest[:-1], rest[-1]
    at = lax.axis_index("shot") % 2 * (state.shape[0] // 2)
    for field_ref in field_refs:
        part = pl.ds(at, field_ref.shape[0])
        field_ref[...] = state[part] + prior[part]
        at += field_ref.shape[0]
    base_ref[...] = state[...] + 0.5 * prior[...]


def sum_over_y(chip_y, part_refs, order, i):
    if len(part_refs) > 2:
        for d, part_ref in enumerate(part_refs):
            order[chip_y ^ d] = part_ref[i]
        parts = [order[y] for y in range(len(part_refs))]
    else:
        parts = [part_ref[i] for part_ref in part_refs]
    total = parts[0].astype(f32)
    for part in parts[1:]:
        total += part.astype(f32)
    return total.T


def probe_kernel(ny, field_ref, after_ref, *rest):
    part_refs, (out_ref, grad_ref, order) = rest[:ny], rest[ny:]
    for i in range(out_ref.shape[0]):
        grad = sum_over_y(lax.axis_index("shot") // 2, part_refs, order, i)
        grad_ref[i] = grad
        out_ref[i] = (field_ref[i] - 0.25 * grad).astype(bf16)


def total_kernel(ny, after, grad_ref, *rest):
    rest = rest[after:]
    part_refs, (out_ref, order) = rest[:ny], rest[ny:]
    for i in range(out_ref.shape[0]):
        grad2 = sum_over_y(lax.axis_index("shot") // 2, part_refs, order, i)
        out_ref[i] = (grad_ref[i] + grad2).astype(bf16)


def early_update_kernel(parts, base, *refs):
    part_refs, (out_hbm, rest_ref, new, sems) = refs[:-4], refs[-4:]
    half = base.shape[0] // 2
    core = lax.axis_index("shot") % 2
    own, mate = core * half, (1 - core) * half
    done, copies = 0, []
    for n, part_ref in enumerate(part_refs):
        size = part_ref.shape[0]
        at = own + done if n < parts else mate + done - half
        new[done : done + size] = base[pl.ds(at, size)] - 0.125 * part_ref[...].astype(f32)
        copies.append(
            pltpu.make_async_copy(
                new.at[pl.ds(done, size)], out_hbm.at[pl.ds(at, size)], sems.at[n]
            )
        )
        copies[-1].start()
        done += size
    rest_ref[...] = base[pl.ds(mate + done - half, rest_ref.shape[0])]
    for copy in copies:
        copy.wait()


def late_update_kernel(rest_ref, mate_last, so_far_hbm, out_hbm, new, sem):
    size = mate_last.shape[0]
    half = out_hbm.shape[0] // 2
    at = (2 - lax.axis_index("shot") % 2) * half - size
    new[...] = rest_ref[...] - 0.125 * mate_last[...].astype(f32)
    copy = pltpu.make_async_copy(new, out_hbm.at[pl.ds(at, size)], sem)
    copy.start()
    copy.wait()


def per_device(nshot, nband, sens, bund, cblk, state, prior, observed, pick_weight):
    nblk = sens.shape[0]
    samples = state.shape[1]
    owned, rays = observed.shape
    bundles = owned * nband
    cells = state.shape[0] // CBLK
    sizes = sizes_of(cells // 4)
    parts = len(sizes)
    ny = nshot // 2
    flops = 2 * nblk * rays * CBLK * samples
    sens_bytes = nblk * rays * CBLK * 2

    state_b = state.reshape(cells, CBLK, samples)
    prior_b = prior.reshape(cells, CBLK, samples)

    def other_core(array):
        return lax.ppermute(array, "shot", [(i, i ^ 1) for i in range(nshot)])

    def other_chips(array):
        return [array] + [
            lax.ppermute(array, "shot", [(i, i ^ (2 * d)) for i in range(nshot)])
            for d in range(1, ny)
        ]

    def over_band(array):
        return lax.all_to_all(array, "band", split_axis=0, concat_axis=0, tiled=True)

    part_out = arr((bundles, rays, samples), bf16)
    dense_bf16 = [arr((size, bundles * rays, 2 * CBLK), bf16) for size in sizes]
    small_token = arr((8, CBLK), f32)
    dense_flops = 2 * bundles * rays * cells * CBLK * samples
    dense_bytes = 2 * bundles * rays * cells * CBLK
    part_bf16 = [arr((2 * size, CBLK, samples), bf16) for size in sizes]
    part_f32 = [arr((2 * size, CBLK, samples), f32) for size in sizes]
    order = pltpu.VMEM((ny, samples, CBLK), bf16)

    def residual(part, after, name, keep):
        parts = over_band(part).reshape(nband, owned, rays, samples)
        outs = (arr((nband, owned, samples, rays), bf16),)
        if keep:
            outs += (arr((owned, samples, rays), f32),)
        copies, *resid = call(
            residual_kernel, outs, [], [VMEM] * 3 + [ANY], name, bytes_accessed=1 << 20
        )(parts, observed, pick_weight, after)
        return resid, over_band(copies).reshape(bundles, samples, rays)

    def adjoint(dense, resid_all, name):
        def kernel(picked, after):
            share = sum(sizes[p // 2] for p in picked)
            return call(
                adjoint_kernel,
                tuple(part_f32[p // 2] if p % 2 else part_bf16[p // 2] for p in picked),
                [],
                [VMEM, ANY] + [VMEM] * len(picked),
                name,
                dense_flops * 2 * share // cells,
                dense_bytes * 2 * share // cells,
            )(resid_all, after, *[dense[p] for p in picked])

        (give,) = kernel((0,), token)
        got = [other_core(give)]
        first, *gives = kernel((1,) + tuple(range(2, 2 * parts, 2)), give)
        got += [other_core(give) for give in gives]
        keeps = [first, *kernel(tuple(range(3, 2 * parts, 2)), first)]
        sums, before = [], token
        for part in range(parts):
            before = call(
                pair_kernel,
                part_bf16[part],
                [],
                [VMEM, VMEM, ANY],
                name + "_pair",
                bytes_accessed=1 << 19,
            )(keeps[part], got[part], before)
            sums.append(other_chips(before))
        return sums, keeps[-1]

    part1 = call(
        first_forward_kernel,
        part_out,
        [
            pltpu.VMEM((bundles, rays, samples), f32),
            pltpu.VMEM((cells, CBLK, samples), bf16),
            pltpu.SMEM((nblk,), i32),
            pltpu.SMEM((nblk,), i32),
            pltpu.VMEM(sens.shape, bf16),
            pltpu.VMEM(state_b.shape, f32),
            pltpu.VMEM(state_b.shape, f32),
            pltpu.SemaphoreType.DMA((6 + CHUNKS,)),
        ],
        [HBM] * 5,
        "forward1",
        flops,
        sens_bytes,
        vmem=FIRST_VMEM,
    )(bund, cblk, sens, state_b, prior_b)
    *dense, token = call(
        dense_kernel,
        tuple(d for d in dense_bf16 for _ in range(2)) + (small_token,),
        [pltpu.VMEM((2, cells // 4, bundles * rays, 2 * CBLK), f32)],
        [SMEM, SMEM, VMEM],
        "dense",
        0,
        16 << 20,
        vmem=3 * dense_bytes + 2 * sens_bytes + (2 << 20),
    )(bund, cblk, sens)
    _, resid_all1 = residual(part1, token, "residual1", False)
    sums1, after = adjoint(dense, resid_all1, "adjoint1")

    *fields, base = call(
        prepare_kernel,
        (*part_f32, arr((cells, CBLK, samples), f32)),
        [],
        [VMEM, VMEM, ANY],
        "prepare",
        bytes_accessed=4 << 20,
    )(state_b, prior_b, after)
    own, grad1, mate, before = [], [], [], sums1[-1][0]
    for part, (field, sums) in enumerate(zip(fields, sums1)):
        probe, grad = call(
            functools.partial(probe_kernel, ny),
            (part_bf16[part], part_f32[part]),
            [order],
            [VMEM, ANY] + [VMEM] * ny,
            "probe2",
            bytes_accessed=1 << 19,
        )(field, before, *sums)
        before = probe
        own.append(probe)
        grad1.append(grad)
        mate.append(other_core(probe))

    early = call(
        early_forward_kernel,
        arr((bundles, rays, samples), f32),
        [],
        [VMEM] * (4 * parts - 2),
        "forward2_early",
        dense_flops * 7 // 8,
        dense_bytes * 7 // 8,
    )(*dense[1::2], *dense[0:-2:2], *own, *mate[:-1])
    part2 = call(
        late_forward_kernel,
        part_out,
        [],
        [VMEM] * 3,
        "forward2_late",
        dense_flops // 8,
        dense_bytes // 8,
    )(dense[-2], mate[-1], early)

    (resid2_t,), resid_all2 = residual(part2, token, "residual2", True)
    sums2, _ = adjoint(dense, resid_all2, "adjoint2")
    resid2, turned = call(
        turn_kernel,
        (arr((owned, rays, samples), f32), small_token),
        [],
        [VMEM],
        "turn",
        bytes_accessed=1 << 20,
    )(resid2_t)
    own, mate, after = [], [], [turned, sums2[-1][0], *dense[:-1]]
    for part, (grad, sums) in enumerate(zip(grad1, sums2)):
        total = call(
            functools.partial(total_kernel, ny, len(after)),
            part_bf16[part],
            [order],
            [VMEM] + [ANY] * len(after) + [VMEM] * ny,
            "total",
            bytes_accessed=1 << 19,
        )(grad, *after, *sums)
        own.append(total)
        after = [total]
        mate.append(other_core(total))
    whole = arr((cells, CBLK, samples), f32)
    last = 2 * sizes[-1]
    so_far, rest = call(
        functools.partial(early_update_kernel, parts),
        (whole, part_f32[-1]),
        [
            pltpu.VMEM((cells - last, CBLK, samples), f32),
            pltpu.SemaphoreType.DMA((2 * parts - 1,)),
        ],
        [VMEM] * (2 * parts),
        "new_state_early",
        bytes_accessed=3 << 20,
        out_specs=(HBM, VMEM),
    )(base, *own, *mate[:-1])
    new_state = call(
        late_update_kernel,
        whole,
        [pltpu.VMEM((last, CBLK, samples), f32), pltpu.SemaphoreType.DMA],
        [VMEM, VMEM, HBM],
        "new_state_late",
        bytes_accessed=1 << 20,
        out_specs=HBM,
        input_output_aliases={2: 0},
    )(rest, mate[-1], so_far)
    return new_state.reshape(state.shape), resid2


def solution(mesh):
    in_specs = (
        P(("shot", "band"), None, None),
        P(("shot", "band")),
        P(("shot", "band")),
        P("band", None),
        P("band", None),
        P(("shot", "band"), None),
        P(("shot", "band"), None),
    )
    out_specs = (P("band", None), P(("shot", "band"), None, None))
    return jax.shard_map(
        functools.partial(per_device, mesh.shape["shot"], mesh.shape["band"]),
        mesh=mesh,
        in_specs=in_specs,
        out_specs=out_specs,
        check_vma=False,
    )
```

```python
import functools

import jax
import jax.numpy as jnp
from jax import lax
from jax.experimental import pallas as pl
from jax.experimental.pallas import tpu as pltpu
from jax.sharding import PartitionSpec as P

CBLK = 128
GROUP = 32
CHUNKS = 2
FIELDS = 4
FIRST_VMEM = 55 << 20
GIVE_A, KEEP_A, GIVE_B, KEEP_B = range(4)

VMEM = pl.BlockSpec(memory_space=pltpu.VMEM)
SMEM = pl.BlockSpec(memory_space=pltpu.SMEM)
HBM = pl.BlockSpec(memory_space=pltpu.HBM)
ANY = pl.BlockSpec(memory_space=pl.ANY)

bf16, f32, i32 = jnp.bfloat16, jnp.float32, jnp.int32
arr = jax.ShapeDtypeStruct

def call(body, outs, scratch, in_specs, name, flops=0, bytes_accessed=0, vmem=32 << 20, **more):
    if "out_specs" not in more:
        more["out_specs"] = jax.tree.map(lambda _: VMEM, outs)
    return pl.pallas_call(
        body,
        out_shape=outs,
        in_specs=in_specs,
        scratch_shapes=scratch,
        compiler_params=pltpu.CompilerParams(vmem_limit_bytes=vmem),
        cost_estimate=pl.CostEstimate(
            flops=flops, bytes_accessed=bytes_accessed, transcendentals=0
        ),
        name=name,
        **more,
    )


def first_forward_kernel(
    bund_hbm,
    cblk_hbm,
    sens_hbm,
    state_hbm,
    prior_hbm,
    out_ref,
    acc,
    probe,
    bund,
    cblk,
    sens,
    state,
    prior,
    sems,
):
    nblk = sens.shape[0]
    step = nblk // CHUNKS
    cells = state.shape[0]
    share = cells // FIELDS
    small = [
        pltpu.make_async_copy(bund_hbm, bund, sems.at[0]),
        pltpu.make_async_copy(cblk_hbm, cblk, sems.at[1]),
    ]
    fields = []
    for h in range(FIELDS):
        part = pl.ds(h * share, share)
        fields.append(
            [
                pltpu.make_async_copy(state_hbm.at[part], state.at[part], sems.at[2 + 2 * h]),
                pltpu.make_async_copy(prior_hbm.at[part], prior.at[part], sems.at[3 + 2 * h]),
            ]
        )

    def block_copies(c):
        size = step // 2
        copies = []
        for h in range(2):
            part = pl.ds(c * step + h * size, size)
            sem = sems.at[2 + 2 * FIELDS + 2 * c + h]
            copies.append(pltpu.make_async_copy(sens_hbm.at[part], sens.at[part], sem))
        return copies

    for copy in small + [copy for field in fields for copy in field]:
        copy.start()
    for c in range(CHUNKS):
        for copy in block_copies(c):
            copy.start()
    acc[...] = jnp.zeros_like(acc)

    for h in range(FIELDS):
        part = pl.ds(h * share, share)
        for copy in fields[h]:
            copy.wait()
        probe[part] = (state[part] + 0.5 * prior[part]).astype(bf16)
    for copy in small:
        copy.wait()

    def chunk(c, carry):
        for copy in block_copies(c):
            copy.wait()
        for g in range(step // GROUP):
            ks = [c * step + g * GROUP + j for j in range(GROUP)]
            prods = [
                jnp.dot(sens[k], probe[cblk[k]], preferred_element_type=f32) for k in ks
            ]
            for k, prod in zip(ks, prods):
                acc[bund[k]] += prod
        return carry

    lax.fori_loop(0, CHUNKS, chunk, 0)
    out_ref[...] = acc[...].astype(bf16)


def dense_kernel(bund, cblk, sens, *rest):
    out_refs, (token_ref, total) = rest[:4], rest[4:]
    rays = sens.shape[1]
    quarter = 2 * total.shape[1]
    core = lax.axis_index("shot") % 2
    total[...] = jnp.zeros_like(total)

    def place(k, carry):
        cell = cblk[k]
        kept = jnp.where(cell // (2 * quarter) == core, 1, 0)
        part = 2 * (cell // quarter % 2) + kept
        rows = pl.ds(pl.multiple_of(bund[k] * rays, rays), rays)
        lanes = pl.ds(pl.multiple_of(cell % 2 * CBLK, CBLK), CBLK)
        total[part, cell % quarter // 2, rows, lanes] += sens[k].astype(f32)
        return carry

    lax.fori_loop(0, sens.shape[0], place, 0)
    for part, out_ref in zip((KEEP_B, GIVE_A, KEEP_A, GIVE_B), out_refs):
        out_ref[...] = total[part].astype(bf16)
    token_ref[...] = jnp.zeros_like(token_ref)


def dense_forward(columns, store):
    step = 2 * CBLK
    pairs = columns[0][0].shape[0]
    probe = jnp.concatenate(
        [part[...].reshape(2 * CBLK * pairs, -1) for _, part in columns], axis=0
    )
    for m in range(columns[0][0].shape[1] // step):
        rows = pl.ds(m * step, step)
        lhs = jnp.concatenate(
            [dense[pair, rows, :] for dense, _ in columns for pair in range(pairs)], axis=1
        )
        total = jnp.dot(lhs, probe, preferred_element_type=f32)
        store(pl.ds(2 * m, 2), total.reshape(2, CBLK, -1))


def early_forward_kernel(dense_own_a, dense_own_b, dense_mate_a, own_a, own_b, mate_a, acc):
    def store(rows, value):
        acc[rows] = value

    columns = [(dense_own_a, own_a), (dense_own_b, own_b), (dense_mate_a, mate_a)]
    dense_forward(columns, store)


def late_forward_kernel(dense_mate_b, mate_b, early, out_ref):
    def store(rows, value):
        out_ref[rows] = (early[rows] + value).astype(bf16)

    dense_forward([(dense_mate_b, mate_b)], store)


def adjoint_kernel(resid, *refs):
    lhs = jnp.concatenate([resid[m] for m in range(resid.shape[0])], axis=1)
    count = len(refs) // 2
    for dense, out_ref in zip(refs[:count], refs[count:]):
        for pair in range(dense.shape[0]):
            both = jnp.dot(lhs, dense[pair], preferred_element_type=f32)
            both = both.astype(out_ref.dtype)
            out_ref[2 * pair] = both[:, :CBLK]
            out_ref[2 * pair + 1] = both[:, CBLK:]


def pair_kernel(keep_ref, got_ref, out_ref):
    out_ref[...] = (keep_ref[...] + got_ref[...].astype(f32)).astype(bf16)


def residual_kernel(parts_ref, obs_ref, wt_ref, after_ref, out_ref, *resid_ref):
    for i in range(parts_ref.shape[1]):
        total = parts_ref[0, i].astype(f32)
        for d in range(1, parts_ref.shape[0]):
            total += parts_ref[d, i].astype(f32)
        resid = wt_ref[pl.ds(i, 1), :] * (total.T - obs_ref[pl.ds(i, 1), :])
        if resid_ref:
            resid_ref[0][i] = resid
        rounded = resid.astype(bf16)
        for d in range(parts_ref.shape[0]):
            out_ref[d, i] = rounded


def turn_kernel(in_ref, out_ref, token_ref):
    for i in range(in_ref.shape[0]):
        out_ref[i] = in_ref[i].T
    token_ref[...] = jnp.zeros_like(token_ref)


def prepare_kernel(state, prior, after_ref, field_a, field_b, base_ref):
    quarter = field_a.shape[0]
    own = lax.axis_index("shot") % 2 * (2 * quarter)
    for at, field_ref in ((own, field_a), (own + quarter, field_b)):
        part = pl.ds(at, quarter)
        field_ref[...] = state[part] + prior[part]
    base_ref[...] = state[...] + 0.5 * prior[...]


def sum_over_y(chip_y, part_refs, order, i):
    if len(part_refs) > 2:
        for d, part_ref in enumerate(part_refs):
            order[chip_y ^ d] = part_ref[i]
        parts = [order[y] for y in range(len(part_refs))]
    else:
        parts = [part_ref[i] for part_ref in part_refs]
    total = parts[0].astype(f32)
    for part in parts[1:]:
        total += part.astype(f32)
    return total.T


def probe_kernel(ny, field_ref, *rest):
    part_refs, (out_ref, grad_ref, order) = rest[:ny], rest[ny:]
    for i in range(out_ref.shape[0]):
        grad = sum_over_y(lax.axis_index("shot") // 2, part_refs, order, i)
        grad_ref[i] = grad
        out_ref[i] = (field_ref[i] - 0.25 * grad).astype(bf16)


def total_kernel(ny, after, grad_ref, *rest):
    rest = rest[after:]
    part_refs, (out_ref, order) = rest[:ny], rest[ny:]
    for i in range(out_ref.shape[0]):
        grad2 = sum_over_y(lax.axis_index("shot") // 2, part_refs, order, i)
        out_ref[i] = (grad_ref[i] + grad2).astype(bf16)


def early_update_kernel(base, own_a, own_b, mate_a, out_hbm, rest_ref, new, sems):
    quarter = own_a.shape[0]
    core = lax.axis_index("shot") % 2
    own, mate = core * (2 * quarter), (1 - core) * (2 * quarter)
    copies = []
    for n, (at, part_ref) in enumerate(((own, own_a), (own + quarter, own_b), (mate, mate_a))):
        new[n] = base[pl.ds(at, quarter)] - 0.125 * part_ref[...].astype(f32)
        copies.append(
            pltpu.make_async_copy(new.at[n], out_hbm.at[pl.ds(at, quarter)], sems.at[n])
        )
        copies[-1].start()
    rest_ref[...] = base[pl.ds(mate + quarter, quarter)]
    for copy in copies:
        copy.wait()


def late_update_kernel(rest_ref, mate_b, so_far_hbm, out_hbm, new, sem):
    quarter = mate_b.shape[0]
    at = (1 - lax.axis_index("shot") % 2) * (2 * quarter) + quarter
    new[...] = rest_ref[...] - 0.125 * mate_b[...].astype(f32)
    copy = pltpu.make_async_copy(new, out_hbm.at[pl.ds(at, quarter)], sem)
    copy.start()
    copy.wait()


def per_device(nshot, nband, sens, bund, cblk, state, prior, observed, pick_weight):
    nblk = sens.shape[0]
    samples = state.shape[1]
    owned, rays = observed.shape
    bundles = owned * nband
    cells = state.shape[0] // CBLK
    quarter = cells // 4
    ny = nshot // 2
    flops = 2 * nblk * rays * CBLK * samples
    sens_bytes = nblk * rays * CBLK * 2

    state_b = state.reshape(cells, CBLK, samples)
    prior_b = prior.reshape(cells, CBLK, samples)

    def other_core(array):
        return lax.ppermute(array, "shot", [(i, i ^ 1) for i in range(nshot)])

    def other_chips(array):
        return [array] + [
            lax.ppermute(array, "shot", [(i, i ^ (2 * d)) for i in range(nshot)])
            for d in range(1, ny)
        ]

    def over_band(array):
        return lax.all_to_all(array, "band", split_axis=0, concat_axis=0, tiled=True)

    part_out = arr((bundles, rays, samples), bf16)
    dense_shape = (quarter // 2, bundles * rays, 2 * CBLK)
    small_token = arr((8, CBLK), f32)
    dense_flops = 2 * bundles * rays * cells * CBLK * samples
    dense_bytes = 2 * bundles * rays * cells * CBLK
    quarter_bf16 = arr((quarter, CBLK, samples), bf16)
    quarter_f32 = arr((quarter, CBLK, samples), f32)
    order = pltpu.VMEM((ny, samples, CBLK), bf16)

    def residual(part, after, name, keep):
        parts = over_band(part).reshape(nband, owned, rays, samples)
        outs = (arr((nband, owned, samples, rays), bf16),)
        if keep:
            outs += (arr((owned, samples, rays), f32),)
        copies, *resid = call(
            residual_kernel, outs, [], [VMEM] * 3 + [ANY], name, bytes_accessed=1 << 20
        )(parts, observed, pick_weight, after)
        return resid, over_band(copies).reshape(bundles, samples, rays)

    def adjoint(dense, resid_all, name):
        def kernel(parts, part):
            return call(
                adjoint_kernel,
                tuple(quarter_f32 if p % 2 else quarter_bf16 for p in parts),
                [],
                [VMEM] * (1 + len(parts)),
                name + part,
                dense_flops * len(parts) // 4,
                dense_bytes * len(parts) // 4,
            )(resid_all, *[dense[p] for p in parts])

        def pair(keep, got, part):
            return call(
                pair_kernel,
                quarter_bf16,
                [],
                [VMEM] * 2,
                name + "_pair" + part,
                bytes_accessed=1 << 19,
            )(keep, got)

        (give_a,) = kernel((GIVE_A,), "_give_a")
        got_a = other_core(give_a)
        keep_a, give_b = kernel((KEEP_A, GIVE_B), "_keep_a")
        got_b = other_core(give_b)
        sums_a = other_chips(pair(keep_a, got_a, "_a"))
        (keep_b,) = kernel((KEEP_B,), "_keep_b")
        sums_b = other_chips(pair(keep_b, got_b, "_b"))
        return sums_a, sums_b, keep_b

    part1 = call(
        first_forward_kernel,
        part_out,
        [
            pltpu.VMEM((bundles, rays, samples), f32),
            pltpu.VMEM((cells, CBLK, samples), bf16),
            pltpu.SMEM((nblk,), i32),
            pltpu.SMEM((nblk,), i32),
            pltpu.VMEM(sens.shape, bf16),
            pltpu.VMEM(state_b.shape, f32),
            pltpu.VMEM(state_b.shape, f32),
            pltpu.SemaphoreType.DMA((2 + 2 * FIELDS + 2 * CHUNKS,)),
        ],
        [HBM] * 5,
        "forward1",
        flops,
        sens_bytes,
        vmem=FIRST_VMEM,
    )(bund, cblk, sens, state_b, prior_b)
    dense_keep_b, *dense, token = call(
        dense_kernel,
        (arr(dense_shape, bf16),) * 4 + (small_token,),
        [pltpu.VMEM((4,) + dense_shape, f32)],
        [SMEM, SMEM, VMEM],
        "dense",
        0,
        16 << 20,
        vmem=3 * dense_bytes + 2 * sens_bytes + (2 << 20),
    )(bund, cblk, sens)
    dense.append(dense_keep_b)
    _, resid_all1 = residual(part1, token, "residual1", False)
    *sums1, after = adjoint(dense, resid_all1, "adjoint1")

    *fields, base = call(
        prepare_kernel,
        (quarter_f32, quarter_f32, arr((cells, CBLK, samples), f32)),
        [],
        [VMEM, VMEM, ANY],
        "prepare",
        bytes_accessed=4 << 20,
    )(state_b, prior_b, after)
    own, grad1, mate = [], [], []
    for field, sums, part in zip(fields, sums1, "ab"):
        probe, grad = call(
            functools.partial(probe_kernel, ny),
            (quarter_bf16, quarter_f32),
            [order],
            [VMEM] * (1 + ny),
            "probe2_" + part,
            bytes_accessed=1 << 19,
        )(field, *sums)
        own.append(probe)
        grad1.append(grad)
        mate.append(other_core(probe))

    early = call(
        early_forward_kernel,
        arr((bundles, rays, samples), f32),
        [],
        [VMEM] * 6,
        "forward2_early",
        dense_flops * 3 // 4,
        dense_bytes * 3 // 4,
    )(dense[KEEP_A], dense[KEEP_B], dense[GIVE_A], own[0], own[1], mate[0])
    part2 = call(
        late_forward_kernel,
        part_out,
        [],
        [VMEM] * 3,
        "forward2_late",
        dense_flops // 4,
        dense_bytes // 4,
    )(dense[GIVE_B], mate[1], early)

    (resid2_t,), resid_all2 = residual(part2, token, "residual2", True)
    *sums2, _ = adjoint(dense, resid_all2, "adjoint2")
    resid2, turned = call(
        turn_kernel,
        (arr((owned, rays, samples), f32), small_token),
        [],
        [VMEM],
        "turn",
        bytes_accessed=1 << 20,
    )(resid2_t)
    own, mate, after = [], [], [turned, dense[GIVE_A], dense[KEEP_A], dense[GIVE_B]]
    for grad, sums, part in zip(grad1, sums2, "ab"):
        total = call(
            functools.partial(total_kernel, ny, len(after)),
            quarter_bf16,
            [order],
            [VMEM] + [ANY] * len(after) + [VMEM] * ny,
            "total_" + part,
            bytes_accessed=1 << 19,
        )(grad, *after, *sums)
        own.append(total)
        after = []
        mate.append(other_core(total))
    whole = arr((cells, CBLK, samples), f32)
    so_far, rest = call(
        early_update_kernel,
        (whole, quarter_f32),
        [pltpu.VMEM((3, quarter, CBLK, samples), f32), pltpu.SemaphoreType.DMA((3,))],
        [VMEM] * 4,
        "new_state_early",
        bytes_accessed=3 << 20,
        out_specs=(HBM, VMEM),
    )(base, own[0], own[1], mate[0])
    new_state = call(
        late_update_kernel,
        whole,
        [pltpu.VMEM((quarter, CBLK, samples), f32), pltpu.SemaphoreType.DMA],
        [VMEM, VMEM, HBM],
        "new_state_late",
        bytes_accessed=1 << 20,
        out_specs=HBM,
        input_output_aliases={2: 0},
    )(rest, mate[1], so_far)
    return new_state.reshape(state.shape), resid2


def solution(mesh):
    in_specs = (
        P(("shot", "band"), None, None),
        P(("shot", "band")),
        P(("shot", "band")),
        P("band", None),
        P("band", None),
        P(("shot", "band"), None),
        P(("shot", "band"), None),
    )
    out_specs = (P("band", None), P(("shot", "band"), None, None))
    return jax.shard_map(
        functools.partial(per_device, mesh.shape["shot"], mesh.shape["band"]),
        mesh=mesh,
        in_specs=in_specs,
        out_specs=out_specs,
        check_vma=False,
    )
```

```python
import functools

import jax
import jax.numpy as jnp
from jax import lax
from jax.experimental import pallas as pl
from jax.experimental.pallas import tpu as pltpu
from jax.sharding import PartitionSpec as P

CBLK = 128
GROUP = 32
CHUNKS = 2
FIELDS = 4
FIRST_VMEM = 55 << 20
GIVE_A, KEEP_A, GIVE_B, KEEP_B = range(4)

VMEM = pl.BlockSpec(memory_space=pltpu.VMEM)
SMEM = pl.BlockSpec(memory_space=pltpu.SMEM)
HBM = pl.BlockSpec(memory_space=pltpu.HBM)
ANY = pl.BlockSpec(memory_space=pl.ANY)

bf16, f32, i32 = jnp.bfloat16, jnp.float32, jnp.int32
arr = jax.ShapeDtypeStruct

def call(body, outs, scratch, in_specs, name, flops=0, bytes_accessed=0, vmem=32 << 20, **more):
    if "out_specs" not in more:
        more["out_specs"] = jax.tree.map(lambda _: VMEM, outs)
    return pl.pallas_call(
        body,
        out_shape=outs,
        in_specs=in_specs,
        scratch_shapes=scratch,
        compiler_params=pltpu.CompilerParams(vmem_limit_bytes=vmem),
        cost_estimate=pl.CostEstimate(
            flops=flops, bytes_accessed=bytes_accessed, transcendentals=0
        ),
        name=name,
        **more,
    )


def first_forward_kernel(
    bund_hbm,
    cblk_hbm,
    sens_hbm,
    state_hbm,
    prior_hbm,
    out_ref,
    acc,
    acc_odd,
    probe,
    bund,
    cblk,
    sens,
    state,
    prior,
    sems,
):
    nblk = sens.shape[0]
    step = nblk // CHUNKS
    cells = state.shape[0]
    share = cells // FIELDS
    small = [
        pltpu.make_async_copy(bund_hbm, bund, sems.at[0]),
        pltpu.make_async_copy(cblk_hbm, cblk, sems.at[1]),
    ]
    fields = []
    for h in range(FIELDS):
        part = pl.ds(h * share, share)
        fields.append(
            [
                pltpu.make_async_copy(state_hbm.at[part], state.at[part], sems.at[2 + 2 * h]),
                pltpu.make_async_copy(prior_hbm.at[part], prior.at[part], sems.at[3 + 2 * h]),
            ]
        )

    def block_copies(c):
        size = step // 2
        copies = []
        for h in range(2):
            part = pl.ds(c * step + h * size, size)
            sem = sems.at[2 + 2 * FIELDS + 2 * c + h]
            copies.append(pltpu.make_async_copy(sens_hbm.at[part], sens.at[part], sem))
        return copies

    for copy in small + [copy for field in fields for copy in field]:
        copy.start()
    for c in range(CHUNKS):
        for copy in block_copies(c):
            copy.start()
    accs = (acc, acc_odd)
    for ref in accs:
        ref[...] = jnp.zeros_like(ref)

    for h in range(FIELDS):
        part = pl.ds(h * share, share)
        for copy in fields[h]:
            copy.wait()
        probe[part] = (state[part] + 0.5 * prior[part]).astype(bf16)
    for copy in small:
        copy.wait()

    def chunk(c, carry):
        for copy in block_copies(c):
            copy.wait()
        for g in range(step // GROUP):
            ks = [c * step + g * GROUP + j for j in range(GROUP)]
            prods = [
                jnp.dot(sens[k], probe[cblk[k]], preferred_element_type=f32) for k in ks
            ]
            for j, (k, prod) in enumerate(zip(ks, prods)):
                accs[j % 2][bund[k]] += prod
        return carry

    lax.fori_loop(0, CHUNKS, chunk, 0)
    out_ref[...] = (acc[...] + acc_odd[...]).astype(bf16)


def dense_kernel(bund, cblk, sens, *rest):
    out_refs, (token_ref, total) = rest[:4], rest[4:]
    rays = sens.shape[1]
    quarter = 2 * total.shape[1]
    core = lax.axis_index("shot") % 2
    total[...] = jnp.zeros_like(total)

    def place(k, carry):
        cell = cblk[k]
        kept = jnp.where(cell // (2 * quarter) == core, 1, 0)
        part = 2 * (cell // quarter % 2) + kept
        rows = pl.ds(pl.multiple_of(bund[k] * rays, rays), rays)
        lanes = pl.ds(pl.multiple_of(cell % 2 * CBLK, CBLK), CBLK)
        total[part, cell % quarter // 2, rows, lanes] += sens[k].astype(f32)
        return carry

    lax.fori_loop(0, sens.shape[0], place, 0)
    for part, out_ref in zip((KEEP_B, GIVE_A, KEEP_A, GIVE_B), out_refs):
        out_ref[...] = total[part].astype(bf16)
    token_ref[...] = jnp.zeros_like(token_ref)


def dense_forward(columns, store):
    step = 2 * CBLK
    pairs = columns[0][0].shape[0]
    probe = jnp.concatenate(
        [part[...].reshape(2 * CBLK * pairs, -1) for _, part in columns], axis=0
    )
    for m in range(columns[0][0].shape[1] // step):
        rows = pl.ds(m * step, step)
        lhs = jnp.concatenate(
            [dense[pair, rows, :] for dense, _ in columns for pair in range(pairs)], axis=1
        )
        total = jnp.dot(lhs, probe, preferred_element_type=f32)
        store(pl.ds(2 * m, 2), total.reshape(2, CBLK, -1))


def early_forward_kernel(dense_own_a, dense_own_b, dense_mate_a, own_a, own_b, mate_a, acc):
    def store(rows, value):
        acc[rows] = value

    columns = [(dense_own_a, own_a), (dense_own_b, own_b), (dense_mate_a, mate_a)]
    dense_forward(columns, store)


def late_forward_kernel(dense_mate_b, mate_b, early, out_ref):
    def store(rows, value):
        out_ref[rows] = (early[rows] + value).astype(bf16)

    dense_forward([(dense_mate_b, mate_b)], store)


def adjoint_kernel(resid, *refs):
    lhs = jnp.concatenate([resid[m] for m in range(resid.shape[0])], axis=1)
    count = len(refs) // 2
    for dense, out_ref in zip(refs[:count], refs[count:]):
        for pair in range(dense.shape[0]):
            both = jnp.dot(lhs, dense[pair], preferred_element_type=f32)
            both = both.astype(out_ref.dtype)
            out_ref[2 * pair] = both[:, :CBLK]
            out_ref[2 * pair + 1] = both[:, CBLK:]


def pair_kernel(keep_ref, got_ref, out_ref):
    out_ref[...] = (keep_ref[...] + got_ref[...].astype(f32)).astype(bf16)


def residual_kernel(parts_ref, obs_ref, wt_ref, after_ref, out_ref, *resid_ref):
    for i in range(parts_ref.shape[1]):
        total = parts_ref[0, i].astype(f32)
        for d in range(1, parts_ref.shape[0]):
            total += parts_ref[d, i].astype(f32)
        resid = wt_ref[pl.ds(i, 1), :] * (total.T - obs_ref[pl.ds(i, 1), :])
        if resid_ref:
            resid_ref[0][i] = resid
        rounded = resid.astype(bf16)
        for d in range(parts_ref.shape[0]):
            out_ref[d, i] = rounded


def turn_kernel(in_ref, out_ref, token_ref):
    for i in range(in_ref.shape[0]):
        out_ref[i] = in_ref[i].T
    token_ref[...] = jnp.zeros_like(token_ref)


def prepare_kernel(state, prior, after_ref, field_a, field_b, base_ref):
    quarter = field_a.shape[0]
    own = lax.axis_index("shot") % 2 * (2 * quarter)
    for at, field_ref in ((own, field_a), (own + quarter, field_b)):
        part = pl.ds(at, quarter)
        field_ref[...] = state[part] + prior[part]
    base_ref[...] = state[...] + 0.5 * prior[...]


def sum_over_y(chip_y, part_refs, order, i):
    if len(part_refs) > 2:
        for d, part_ref in enumerate(part_refs):
            order[chip_y ^ d] = part_ref[i]
        parts = [order[y] for y in range(len(part_refs))]
    else:
        parts = [part_ref[i] for part_ref in part_refs]
    total = parts[0].astype(f32)
    for part in parts[1:]:
        total += part.astype(f32)
    return total.T


def probe_kernel(ny, field_ref, *rest):
    part_refs, (out_ref, grad_ref, order) = rest[:ny], rest[ny:]
    for i in range(out_ref.shape[0]):
        grad = sum_over_y(lax.axis_index("shot") // 2, part_refs, order, i)
        grad_ref[i] = grad
        out_ref[i] = (field_ref[i] - 0.25 * grad).astype(bf16)


def total_kernel(ny, after, grad_ref, *rest):
    rest = rest[after:]
    part_refs, (out_ref, order) = rest[:ny], rest[ny:]
    for i in range(out_ref.shape[0]):
        grad2 = sum_over_y(lax.axis_index("shot") // 2, part_refs, order, i)
        out_ref[i] = (grad_ref[i] + grad2).astype(bf16)


def early_update_kernel(base, own_a, own_b, mate_a, out_hbm, rest_ref, new, sems):
    quarter = own_a.shape[0]
    core = lax.axis_index("shot") % 2
    own, mate = core * (2 * quarter), (1 - core) * (2 * quarter)
    copies = []
    for n, (at, part_ref) in enumerate(((own, own_a), (own + quarter, own_b), (mate, mate_a))):
        new[n] = base[pl.ds(at, quarter)] - 0.125 * part_ref[...].astype(f32)
        copies.append(
            pltpu.make_async_copy(new.at[n], out_hbm.at[pl.ds(at, quarter)], sems.at[n])
        )
        copies[-1].start()
    rest_ref[...] = base[pl.ds(mate + quarter, quarter)]
    for copy in copies:
        copy.wait()


def late_update_kernel(rest_ref, mate_b, so_far_hbm, out_hbm, new, sem):
    quarter = mate_b.shape[0]
    at = (1 - lax.axis_index("shot") % 2) * (2 * quarter) + quarter
    new[...] = rest_ref[...] - 0.125 * mate_b[...].astype(f32)
    copy = pltpu.make_async_copy(new, out_hbm.at[pl.ds(at, quarter)], sem)
    copy.start()
    copy.wait()


def per_device(nshot, nband, sens, bund, cblk, state, prior, observed, pick_weight):
    nblk = sens.shape[0]
    samples = state.shape[1]
    owned, rays = observed.shape
    bundles = owned * nband
    cells = state.shape[0] // CBLK
    quarter = cells // 4
    ny = nshot // 2
    flops = 2 * nblk * rays * CBLK * samples
    sens_bytes = nblk * rays * CBLK * 2

    state_b = state.reshape(cells, CBLK, samples)
    prior_b = prior.reshape(cells, CBLK, samples)

    def other_core(array):
        return lax.ppermute(array, "shot", [(i, i ^ 1) for i in range(nshot)])

    def other_chips(array):
        return [array] + [
            lax.ppermute(array, "shot", [(i, i ^ (2 * d)) for i in range(nshot)])
            for d in range(1, ny)
        ]

    def over_band(array):
        return lax.all_to_all(array, "band", split_axis=0, concat_axis=0, tiled=True)

    part_out = arr((bundles, rays, samples), bf16)
    dense_shape = (quarter // 2, bundles * rays, 2 * CBLK)
    small_token = arr((8, CBLK), f32)
    dense_flops = 2 * bundles * rays * cells * CBLK * samples
    dense_bytes = 2 * bundles * rays * cells * CBLK
    quarter_bf16 = arr((quarter, CBLK, samples), bf16)
    quarter_f32 = arr((quarter, CBLK, samples), f32)
    order = pltpu.VMEM((ny, samples, CBLK), bf16)

    def residual(part, after, name, keep):
        parts = over_band(part).reshape(nband, owned, rays, samples)
        outs = (arr((nband, owned, samples, rays), bf16),)
        if keep:
            outs += (arr((owned, samples, rays), f32),)
        copies, *resid = call(
            residual_kernel, outs, [], [VMEM] * 3 + [ANY], name, bytes_accessed=1 << 20
        )(parts, observed, pick_weight, after)
        return resid, over_band(copies).reshape(bundles, samples, rays)

    def adjoint(dense, resid_all, name):
        def kernel(parts, part):
            return call(
                adjoint_kernel,
                tuple(quarter_f32 if p % 2 else quarter_bf16 for p in parts),
                [],
                [VMEM] * (1 + len(parts)),
                name + part,
                dense_flops * len(parts) // 4,
                dense_bytes * len(parts) // 4,
            )(resid_all, *[dense[p] for p in parts])

        def pair(keep, got, part):
            return call(
                pair_kernel,
                quarter_bf16,
                [],
                [VMEM] * 2,
                name + "_pair" + part,
                bytes_accessed=1 << 19,
            )(keep, got)

        (give_a,) = kernel((GIVE_A,), "_give_a")
        got_a = other_core(give_a)
        keep_a, give_b = kernel((KEEP_A, GIVE_B), "_keep_a")
        got_b = other_core(give_b)
        sums_a = other_chips(pair(keep_a, got_a, "_a"))
        (keep_b,) = kernel((KEEP_B,), "_keep_b")
        sums_b = other_chips(pair(keep_b, got_b, "_b"))
        return sums_a, sums_b, keep_b

    part1 = call(
        first_forward_kernel,
        part_out,
        [
            pltpu.VMEM((bundles, rays, samples), f32),
            pltpu.VMEM((bundles, rays, samples), f32),
            pltpu.VMEM((cells, CBLK, samples), bf16),
            pltpu.SMEM((nblk,), i32),
            pltpu.SMEM((nblk,), i32),
            pltpu.VMEM(sens.shape, bf16),
            pltpu.VMEM(state_b.shape, f32),
            pltpu.VMEM(state_b.shape, f32),
            pltpu.SemaphoreType.DMA((2 + 2 * FIELDS + 2 * CHUNKS,)),
        ],
        [HBM] * 5,
        "forward1",
        flops,
        sens_bytes,
        vmem=FIRST_VMEM,
    )(bund, cblk, sens, state_b, prior_b)
    dense_keep_b, *dense, token = call(
        dense_kernel,
        (arr(dense_shape, bf16),) * 4 + (small_token,),
        [pltpu.VMEM((4,) + dense_shape, f32)],
        [SMEM, SMEM, VMEM],
        "dense",
        0,
        16 << 20,
        vmem=3 * dense_bytes + 2 * sens_bytes + (2 << 20),
    )(bund, cblk, sens)
    dense.append(dense_keep_b)
    _, resid_all1 = residual(part1, token, "residual1", False)
    *sums1, after = adjoint(dense, resid_all1, "adjoint1")

    *fields, base = call(
        prepare_kernel,
        (quarter_f32, quarter_f32, arr((cells, CBLK, samples), f32)),
        [],
        [VMEM, VMEM, ANY],
        "prepare",
        bytes_accessed=4 << 20,
    )(state_b, prior_b, after)
    own, grad1, mate = [], [], []
    for field, sums, part in zip(fields, sums1, "ab"):
        probe, grad = call(
            functools.partial(probe_kernel, ny),
            (quarter_bf16, quarter_f32),
            [order],
            [VMEM] * (1 + ny),
            "probe2_" + part,
            bytes_accessed=1 << 19,
        )(field, *sums)
        own.append(probe)
        grad1.append(grad)
        mate.append(other_core(probe))

    early = call(
        early_forward_kernel,
        arr((bundles, rays, samples), f32),
        [],
        [VMEM] * 6,
        "forward2_early",
        dense_flops * 3 // 4,
        dense_bytes * 3 // 4,
    )(dense[KEEP_A], dense[KEEP_B], dense[GIVE_A], own[0], own[1], mate[0])
    part2 = call(
        late_forward_kernel,
        part_out,
        [],
        [VMEM] * 3,
        "forward2_late",
        dense_flops // 4,
        dense_bytes // 4,
    )(dense[GIVE_B], mate[1], early)

    (resid2_t,), resid_all2 = residual(part2, token, "residual2", True)
    *sums2, _ = adjoint(dense, resid_all2, "adjoint2")
    resid2, turned = call(
        turn_kernel,
        (arr((owned, rays, samples), f32), small_token),
        [],
        [VMEM],
        "turn",
        bytes_accessed=1 << 20,
    )(resid2_t)
    own, mate, after = [], [], [turned, dense[GIVE_A], dense[KEEP_A], dense[GIVE_B]]
    for grad, sums, part in zip(grad1, sums2, "ab"):
        total = call(
            functools.partial(total_kernel, ny, len(after)),
            quarter_bf16,
            [order],
            [VMEM] + [ANY] * len(after) + [VMEM] * ny,
            "total_" + part,
            bytes_accessed=1 << 19,
        )(grad, *after, *sums)
        own.append(total)
        after = []
        mate.append(other_core(total))
    whole = arr((cells, CBLK, samples), f32)
    so_far, rest = call(
        early_update_kernel,
        (whole, quarter_f32),
        [pltpu.VMEM((3, quarter, CBLK, samples), f32), pltpu.SemaphoreType.DMA((3,))],
        [VMEM] * 4,
        "new_state_early",
        bytes_accessed=3 << 20,
        out_specs=(HBM, VMEM),
    )(base, own[0], own[1], mate[0])
    new_state = call(
        late_update_kernel,
        whole,
        [pltpu.VMEM((quarter, CBLK, samples), f32), pltpu.SemaphoreType.DMA],
        [VMEM, VMEM, HBM],
        "new_state_late",
        bytes_accessed=1 << 20,
        out_specs=HBM,
        input_output_aliases={2: 0},
    )(rest, mate[1], so_far)
    return new_state.reshape(state.shape), resid2


def solution(mesh):
    in_specs = (
        P(("shot", "band"), None, None),
        P(("shot", "band")),
        P(("shot", "band")),
        P("band", None),
        P("band", None),
        P(("shot", "band"), None),
        P(("shot", "band"), None),
    )
    out_specs = (P("band", None), P(("shot", "band"), None, None))
    return jax.shard_map(
        functools.partial(per_device, mesh.shape["shot"], mesh.shape["band"]),
        mesh=mesh,
        in_specs=in_specs,
        out_specs=out_specs,
        check_vma=False,
    )
```

```python
import functools

import jax
import jax.numpy as jnp
from jax import lax
from jax.experimental import pallas as pl
from jax.experimental.pallas import tpu as pltpu
from jax.sharding import PartitionSpec as P

CBLK = 128
GROUP = 32
CHUNKS = 2
FIELDS = 4
FIRST_VMEM = 55 << 20
GIVE_A, KEEP_A, GIVE_B, KEEP_B = range(4)

VMEM = pl.BlockSpec(memory_space=pltpu.VMEM)
SMEM = pl.BlockSpec(memory_space=pltpu.SMEM)
HBM = pl.BlockSpec(memory_space=pltpu.HBM)
ANY = pl.BlockSpec(memory_space=pl.ANY)

bf16, f32, i32 = jnp.bfloat16, jnp.float32, jnp.int32
arr = jax.ShapeDtypeStruct

def call(body, outs, scratch, in_specs, name, flops=0, bytes_accessed=0, vmem=32 << 20, **more):
    if "out_specs" not in more:
        more["out_specs"] = jax.tree.map(lambda _: VMEM, outs)
    return pl.pallas_call(
        body,
        out_shape=outs,
        in_specs=in_specs,
        scratch_shapes=scratch,
        compiler_params=pltpu.CompilerParams(vmem_limit_bytes=vmem),
        cost_estimate=pl.CostEstimate(
            flops=flops, bytes_accessed=bytes_accessed, transcendentals=0
        ),
        name=name,
        **more,
    )


def first_forward_kernel(
    bund_hbm,
    cblk_hbm,
    sens_hbm,
    state_hbm,
    prior_hbm,
    out_ref,
    acc,
    probe,
    bund,
    cblk,
    sens,
    state,
    prior,
    sems,
):
    nblk = sens.shape[0]
    step = nblk // CHUNKS
    cells = state.shape[0]
    share = cells // FIELDS
    small = [
        pltpu.make_async_copy(bund_hbm, bund, sems.at[0]),
        pltpu.make_async_copy(cblk_hbm, cblk, sems.at[1]),
    ]
    fields = []
    for h in range(FIELDS):
        part = pl.ds(h * share, share)
        fields.append(
            [
                pltpu.make_async_copy(state_hbm.at[part], state.at[part], sems.at[2 + 2 * h]),
                pltpu.make_async_copy(prior_hbm.at[part], prior.at[part], sems.at[3 + 2 * h]),
            ]
        )

    def block_copies(c):
        size = step // 2
        copies = []
        for h in range(2):
            part = pl.ds(c * step + h * size, size)
            sem = sems.at[2 + 2 * FIELDS + 2 * c + h]
            copies.append(pltpu.make_async_copy(sens_hbm.at[part], sens.at[part], sem))
        return copies

    for copy in small + [copy for field in fields for copy in field]:
        copy.start()
    for c in range(CHUNKS):
        for copy in block_copies(c):
            copy.start()
    acc[...] = jnp.zeros_like(acc)

    for h in range(FIELDS):
        part = pl.ds(h * share, share)
        for copy in fields[h]:
            copy.wait()
        probe[part] = (state[part] + 0.5 * prior[part]).astype(bf16)
    for copy in small:
        copy.wait()

    samples = acc.shape[2]
    none = jnp.zeros(probe.shape[1:], bf16)

    def two_products(k1, k2):
        rhs = jnp.concatenate(
            [
                jnp.concatenate([probe[cblk[k1]], none], axis=1),
                jnp.concatenate([none, probe[cblk[k2]]], axis=1),
            ],
            axis=0,
        )
        lhs = jnp.concatenate([sens[k1], sens[k2]], axis=1)
        return jnp.dot(lhs, rhs, preferred_element_type=f32)

    def chunk(c, carry):
        for copy in block_copies(c):
            copy.wait()
        for g in range(step // GROUP):
            ks = [c * step + g * GROUP + j for j in range(GROUP)]
            prods = [two_products(k1, k2) for k1, k2 in zip(ks[0::2], ks[1::2])]
            for j, k in enumerate(ks):
                lanes = slice(j % 2 * samples, (j % 2 + 1) * samples)
                acc[bund[k]] += prods[j // 2][:, lanes]
        return carry

    lax.fori_loop(0, CHUNKS, chunk, 0)
    out_ref[...] = acc[...].astype(bf16)


def dense_kernel(bund, cblk, sens, *rest):
    out_refs, (token_ref, total) = rest[:4], rest[4:]
    rays = sens.shape[1]
    quarter = 2 * total.shape[1]
    core = lax.axis_index("shot") % 2
    total[...] = jnp.zeros_like(total)

    def place(k, carry):
        cell = cblk[k]
        kept = jnp.where(cell // (2 * quarter) == core, 1, 0)
        part = 2 * (cell // quarter % 2) + kept
        rows = pl.ds(pl.multiple_of(bund[k] * rays, rays), rays)
        lanes = pl.ds(pl.multiple_of(cell % 2 * CBLK, CBLK), CBLK)
        total[part, cell % quarter // 2, rows, lanes] += sens[k].astype(f32)
        return carry

    lax.fori_loop(0, sens.shape[0], place, 0)
    for part, out_ref in zip((KEEP_B, GIVE_A, KEEP_A, GIVE_B), out_refs):
        out_ref[...] = total[part].astype(bf16)
    token_ref[...] = jnp.zeros_like(token_ref)


def dense_forward(columns, store):
    step = 2 * CBLK
    pairs = columns[0][0].shape[0]
    probe = jnp.concatenate(
        [part[...].reshape(2 * CBLK * pairs, -1) for _, part in columns], axis=0
    )
    for m in range(columns[0][0].shape[1] // step):
        rows = pl.ds(m * step, step)
        lhs = jnp.concatenate(
            [dense[pair, rows, :] for dense, _ in columns for pair in range(pairs)], axis=1
        )
        total = jnp.dot(lhs, probe, preferred_element_type=f32)
        store(pl.ds(2 * m, 2), total.reshape(2, CBLK, -1))


def early_forward_kernel(dense_own_a, dense_own_b, dense_mate_a, own_a, own_b, mate_a, acc):
    def store(rows, value):
        acc[rows] = value

    columns = [(dense_own_a, own_a), (dense_own_b, own_b), (dense_mate_a, mate_a)]
    dense_forward(columns, store)


def late_forward_kernel(dense_mate_b, mate_b, early, out_ref):
    def store(rows, value):
        out_ref[rows] = (early[rows] + value).astype(bf16)

    dense_forward([(dense_mate_b, mate_b)], store)


def adjoint_kernel(resid, *refs):
    lhs = jnp.concatenate([resid[m] for m in range(resid.shape[0])], axis=1)
    count = len(refs) // 2
    for dense, out_ref in zip(refs[:count], refs[count:]):
        for pair in range(dense.shape[0]):
            both = jnp.dot(lhs, dense[pair], preferred_element_type=f32)
            both = both.astype(out_ref.dtype)
            out_ref[2 * pair] = both[:, :CBLK]
            out_ref[2 * pair + 1] = both[:, CBLK:]


def pair_kernel(keep_ref, got_ref, out_ref):
    out_ref[...] = (keep_ref[...] + got_ref[...].astype(f32)).astype(bf16)


def residual_kernel(parts_ref, obs_ref, wt_ref, after_ref, out_ref, *resid_ref):
    for i in range(parts_ref.shape[1]):
        total = parts_ref[0, i].astype(f32)
        for d in range(1, parts_ref.shape[0]):
            total += parts_ref[d, i].astype(f32)
        resid = wt_ref[pl.ds(i, 1), :] * (total.T - obs_ref[pl.ds(i, 1), :])
        if resid_ref:
            resid_ref[0][i] = resid
        rounded = resid.astype(bf16)
        for d in range(parts_ref.shape[0]):
            out_ref[d, i] = rounded


def turn_kernel(in_ref, out_ref, token_ref):
    for i in range(in_ref.shape[0]):
        out_ref[i] = in_ref[i].T
    token_ref[...] = jnp.zeros_like(token_ref)


def prepare_kernel(state, prior, after_ref, field_a, field_b, base_ref):
    quarter = field_a.shape[0]
    own = lax.axis_index("shot") % 2 * (2 * quarter)
    for at, field_ref in ((own, field_a), (own + quarter, field_b)):
        part = pl.ds(at, quarter)
        field_ref[...] = state[part] + prior[part]
    base_ref[...] = state[...] + 0.5 * prior[...]


def sum_over_y(chip_y, part_refs, order, i):
    if len(part_refs) > 2:
        for d, part_ref in enumerate(part_refs):
            order[chip_y ^ d] = part_ref[i]
        parts = [order[y] for y in range(len(part_refs))]
    else:
        parts = [part_ref[i] for part_ref in part_refs]
    total = parts[0].astype(f32)
    for part in parts[1:]:
        total += part.astype(f32)
    return total.T


def probe_kernel(ny, field_ref, *rest):
    part_refs, (out_ref, grad_ref, order) = rest[:ny], rest[ny:]
    for i in range(out_ref.shape[0]):
        grad = sum_over_y(lax.axis_index("shot") // 2, part_refs, order, i)
        grad_ref[i] = grad
        out_ref[i] = (field_ref[i] - 0.25 * grad).astype(bf16)


def total_kernel(ny, after, grad_ref, *rest):
    rest = rest[after:]
    part_refs, (out_ref, order) = rest[:ny], rest[ny:]
    for i in range(out_ref.shape[0]):
        grad2 = sum_over_y(lax.axis_index("shot") // 2, part_refs, order, i)
        out_ref[i] = (grad_ref[i] + grad2).astype(bf16)


def early_update_kernel(base, own_a, own_b, mate_a, out_hbm, rest_ref, new, sems):
    quarter = own_a.shape[0]
    core = lax.axis_index("shot") % 2
    own, mate = core * (2 * quarter), (1 - core) * (2 * quarter)
    copies = []
    for n, (at, part_ref) in enumerate(((own, own_a), (own + quarter, own_b), (mate, mate_a))):
        new[n] = base[pl.ds(at, quarter)] - 0.125 * part_ref[...].astype(f32)
        copies.append(
            pltpu.make_async_copy(new.at[n], out_hbm.at[pl.ds(at, quarter)], sems.at[n])
        )
        copies[-1].start()
    rest_ref[...] = base[pl.ds(mate + quarter, quarter)]
    for copy in copies:
        copy.wait()


def late_update_kernel(rest_ref, mate_b, so_far_hbm, out_hbm, new, sem):
    quarter = mate_b.shape[0]
    at = (1 - lax.axis_index("shot") % 2) * (2 * quarter) + quarter
    new[...] = rest_ref[...] - 0.125 * mate_b[...].astype(f32)
    copy = pltpu.make_async_copy(new, out_hbm.at[pl.ds(at, quarter)], sem)
    copy.start()
    copy.wait()


def per_device(nshot, nband, sens, bund, cblk, state, prior, observed, pick_weight):
    nblk = sens.shape[0]
    samples = state.shape[1]
    owned, rays = observed.shape
    bundles = owned * nband
    cells = state.shape[0] // CBLK
    quarter = cells // 4
    ny = nshot // 2
    flops = 2 * nblk * rays * CBLK * samples
    sens_bytes = nblk * rays * CBLK * 2

    state_b = state.reshape(cells, CBLK, samples)
    prior_b = prior.reshape(cells, CBLK, samples)

    def other_core(array):
        return lax.ppermute(array, "shot", [(i, i ^ 1) for i in range(nshot)])

    def other_chips(array):
        return [array] + [
            lax.ppermute(array, "shot", [(i, i ^ (2 * d)) for i in range(nshot)])
            for d in range(1, ny)
        ]

    def over_band(array):
        return lax.all_to_all(array, "band", split_axis=0, concat_axis=0, tiled=True)

    part_out = arr((bundles, rays, samples), bf16)
    dense_shape = (quarter // 2, bundles * rays, 2 * CBLK)
    small_token = arr((8, CBLK), f32)
    dense_flops = 2 * bundles * rays * cells * CBLK * samples
    dense_bytes = 2 * bundles * rays * cells * CBLK
    quarter_bf16 = arr((quarter, CBLK, samples), bf16)
    quarter_f32 = arr((quarter, CBLK, samples), f32)
    order = pltpu.VMEM((ny, samples, CBLK), bf16)

    def residual(part, after, name, keep):
        parts = over_band(part).reshape(nband, owned, rays, samples)
        outs = (arr((nband, owned, samples, rays), bf16),)
        if keep:
            outs += (arr((owned, samples, rays), f32),)
        copies, *resid = call(
            residual_kernel, outs, [], [VMEM] * 3 + [ANY], name, bytes_accessed=1 << 20
        )(parts, observed, pick_weight, after)
        return resid, over_band(copies).reshape(bundles, samples, rays)

    def adjoint(dense, resid_all, name):
        def kernel(parts, part):
            return call(
                adjoint_kernel,
                tuple(quarter_f32 if p % 2 else quarter_bf16 for p in parts),
                [],
                [VMEM] * (1 + len(parts)),
                name + part,
                dense_flops * len(parts) // 4,
                dense_bytes * len(parts) // 4,
            )(resid_all, *[dense[p] for p in parts])

        def pair(keep, got, part):
            return call(
                pair_kernel,
                quarter_bf16,
                [],
                [VMEM] * 2,
                name + "_pair" + part,
                bytes_accessed=1 << 19,
            )(keep, got)

        (give_a,) = kernel((GIVE_A,), "_give_a")
        got_a = other_core(give_a)
        keep_a, give_b = kernel((KEEP_A, GIVE_B), "_keep_a")
        got_b = other_core(give_b)
        sums_a = other_chips(pair(keep_a, got_a, "_a"))
        (keep_b,) = kernel((KEEP_B,), "_keep_b")
        sums_b = other_chips(pair(keep_b, got_b, "_b"))
        return sums_a, sums_b, keep_b

    part1 = call(
        first_forward_kernel,
        part_out,
        [
            pltpu.VMEM((bundles, rays, samples), f32),
            pltpu.VMEM((cells, CBLK, samples), bf16),
            pltpu.SMEM((nblk,), i32),
            pltpu.SMEM((nblk,), i32),
            pltpu.VMEM(sens.shape, bf16),
            pltpu.VMEM(state_b.shape, f32),
            pltpu.VMEM(state_b.shape, f32),
            pltpu.SemaphoreType.DMA((2 + 2 * FIELDS + 2 * CHUNKS,)),
        ],
        [HBM] * 5,
        "forward1",
        flops,
        sens_bytes,
        vmem=FIRST_VMEM,
    )(bund, cblk, sens, state_b, prior_b)
    dense_keep_b, *dense, token = call(
        dense_kernel,
        (arr(dense_shape, bf16),) * 4 + (small_token,),
        [pltpu.VMEM((4,) + dense_shape, f32)],
        [SMEM, SMEM, VMEM],
        "dense",
        0,
        16 << 20,
        vmem=3 * dense_bytes + 2 * sens_bytes + (2 << 20),
    )(bund, cblk, sens)
    dense.append(dense_keep_b)
    _, resid_all1 = residual(part1, token, "residual1", False)
    *sums1, after = adjoint(dense, resid_all1, "adjoint1")

    *fields, base = call(
        prepare_kernel,
        (quarter_f32, quarter_f32, arr((cells, CBLK, samples), f32)),
        [],
        [VMEM, VMEM, ANY],
        "prepare",
        bytes_accessed=4 << 20,
    )(state_b, prior_b, after)
    own, grad1, mate = [], [], []
    for field, sums, part in zip(fields, sums1, "ab"):
        probe, grad = call(
            functools.partial(probe_kernel, ny),
            (quarter_bf16, quarter_f32),
            [order],
            [VMEM] * (1 + ny),
            "probe2_" + part,
            bytes_accessed=1 << 19,
        )(field, *sums)
        own.append(probe)
        grad1.append(grad)
        mate.append(other_core(probe))

    early = call(
        early_forward_kernel,
        arr((bundles, rays, samples), f32),
        [],
        [VMEM] * 6,
        "forward2_early",
        dense_flops * 3 // 4,
        dense_bytes * 3 // 4,
    )(dense[KEEP_A], dense[KEEP_B], dense[GIVE_A], own[0], own[1], mate[0])
    part2 = call(
        late_forward_kernel,
        part_out,
        [],
        [VMEM] * 3,
        "forward2_late",
        dense_flops // 4,
        dense_bytes // 4,
    )(dense[GIVE_B], mate[1], early)

    (resid2_t,), resid_all2 = residual(part2, token, "residual2", True)
    *sums2, _ = adjoint(dense, resid_all2, "adjoint2")
    resid2, turned = call(
        turn_kernel,
        (arr((owned, rays, samples), f32), small_token),
        [],
        [VMEM],
        "turn",
        bytes_accessed=1 << 20,
    )(resid2_t)
    own, mate, after = [], [], [turned, dense[GIVE_A], dense[KEEP_A], dense[GIVE_B]]
    for grad, sums, part in zip(grad1, sums2, "ab"):
        total = call(
            functools.partial(total_kernel, ny, len(after)),
            quarter_bf16,
            [order],
            [VMEM] + [ANY] * len(after) + [VMEM] * ny,
            "total_" + part,
            bytes_accessed=1 << 19,
        )(grad, *after, *sums)
        own.append(total)
        after = []
        mate.append(other_core(total))
    whole = arr((cells, CBLK, samples), f32)
    so_far, rest = call(
        early_update_kernel,
        (whole, quarter_f32),
        [pltpu.VMEM((3, quarter, CBLK, samples), f32), pltpu.SemaphoreType.DMA((3,))],
        [VMEM] * 4,
        "new_state_early",
        bytes_accessed=3 << 20,
        out_specs=(HBM, VMEM),
    )(base, own[0], own[1], mate[0])
    new_state = call(
        late_update_kernel,
        whole,
        [pltpu.VMEM((quarter, CBLK, samples), f32), pltpu.SemaphoreType.DMA],
        [VMEM, VMEM, HBM],
        "new_state_late",
        bytes_accessed=1 << 20,
        out_specs=HBM,
        input_output_aliases={2: 0},
    )(rest, mate[1], so_far)
    return new_state.reshape(state.shape), resid2


def solution(mesh):
    in_specs = (
        P(("shot", "band"), None, None),
        P(("shot", "band")),
        P(("shot", "band")),
        P("band", None),
        P("band", None),
        P(("shot", "band"), None),
        P(("shot", "band"), None),
    )
    out_specs = (P("band", None), P(("shot", "band"), None, None))
    return jax.shard_map(
        functools.partial(per_device, mesh.shape["shot"], mesh.shape["band"]),
        mesh=mesh,
        in_specs=in_specs,
        out_specs=out_specs,
        check_vma=False,
    )
```

```python
import functools

import jax
import jax.numpy as jnp
from jax import lax
from jax.experimental import pallas as pl
from jax.experimental.pallas import tpu as pltpu
from jax.sharding import PartitionSpec as P

CBLK = 128
GROUP = 32
CHUNKS = 2
FIELDS = 4
WRITES = 4
FIRST_VMEM = 55 << 20
GIVE_A, KEEP_A, GIVE_B, KEEP_B = range(4)

VMEM = pl.BlockSpec(memory_space=pltpu.VMEM)
SMEM = pl.BlockSpec(memory_space=pltpu.SMEM)
HBM = pl.BlockSpec(memory_space=pltpu.HBM)
ANY = pl.BlockSpec(memory_space=pl.ANY)

bf16, f32, i32 = jnp.bfloat16, jnp.float32, jnp.int32
arr = jax.ShapeDtypeStruct

def call(body, outs, scratch, in_specs, name, flops=0, bytes_accessed=0, vmem=32 << 20, **more):
    if "out_specs" not in more:
        more["out_specs"] = jax.tree.map(lambda _: VMEM, outs)
    return pl.pallas_call(
        body,
        out_shape=outs,
        in_specs=in_specs,
        scratch_shapes=scratch,
        compiler_params=pltpu.CompilerParams(vmem_limit_bytes=vmem),
        cost_estimate=pl.CostEstimate(
            flops=flops, bytes_accessed=bytes_accessed, transcendentals=0
        ),
        name=name,
        **more,
    )


def first_forward_kernel(
    bund_hbm,
    cblk_hbm,
    sens_hbm,
    state_hbm,
    prior_hbm,
    out_hbm,
    acc,
    probe,
    bund,
    cblk,
    sens,
    state,
    prior,
    sems,
    out,
    out_sems,
):
    nblk = sens.shape[0]
    step = nblk // CHUNKS
    cells = state.shape[0]
    share = cells // FIELDS
    small = [
        pltpu.make_async_copy(bund_hbm, bund, sems.at[0]),
        pltpu.make_async_copy(cblk_hbm, cblk, sems.at[1]),
    ]
    fields = []
    for h in range(FIELDS):
        part = pl.ds(h * share, share)
        fields.append(
            [
                pltpu.make_async_copy(state_hbm.at[part], state.at[part], sems.at[2 + 2 * h]),
                pltpu.make_async_copy(prior_hbm.at[part], prior.at[part], sems.at[3 + 2 * h]),
            ]
        )

    def block_copies(c):
        size = step // 2
        copies = []
        for h in range(2):
            part = pl.ds(c * step + h * size, size)
            sem = sems.at[2 + 2 * FIELDS + 2 * c + h]
            copies.append(pltpu.make_async_copy(sens_hbm.at[part], sens.at[part], sem))
        return copies

    for copy in small + [copy for field in fields for copy in field]:
        copy.start()
    for c in range(CHUNKS):
        for copy in block_copies(c):
            copy.start()
    acc[...] = jnp.zeros_like(acc)

    for h in range(FIELDS):
        part = pl.ds(h * share, share)
        for copy in fields[h]:
            copy.wait()
        probe[part] = (state[part] + 0.5 * prior[part]).astype(bf16)
    for copy in small:
        copy.wait()

    def chunk(c, carry):
        for copy in block_copies(c):
            copy.wait()
        for g in range(step // GROUP):
            ks = [c * step + g * GROUP + j for j in range(GROUP)]
            prods = [
                jnp.dot(sens[k], probe[cblk[k]], preferred_element_type=f32) for k in ks
            ]
            for k, prod in zip(ks, prods):
                acc[bund[k]] += prod
        return carry

    lax.fori_loop(0, CHUNKS, chunk, 0)
    share = out_hbm.shape[0] // WRITES
    writes = []
    for n in range(WRITES):
        part = pl.ds(n * share, share)
        out[part] = acc[part].astype(bf16)
        writes.append(pltpu.make_async_copy(out.at[part], out_hbm.at[part], out_sems.at[n]))
        writes[-1].start()
    for copy in writes:
        copy.wait()


def dense_kernel(bund, cblk, sens, *rest):
    out_refs, (token_ref, total) = rest[:4], rest[4:]
    rays = sens.shape[1]
    quarter = 2 * total.shape[1]
    core = lax.axis_index("shot") % 2
    total[...] = jnp.zeros_like(total)

    def place(k, carry):
        cell = cblk[k]
        kept = jnp.where(cell // (2 * quarter) == core, 1, 0)
        part = 2 * (cell // quarter % 2) + kept
        rows = pl.ds(pl.multiple_of(bund[k] * rays, rays), rays)
        lanes = pl.ds(pl.multiple_of(cell % 2 * CBLK, CBLK), CBLK)
        total[part, cell % quarter // 2, rows, lanes] += sens[k].astype(f32)
        return carry

    lax.fori_loop(0, sens.shape[0], place, 0)
    for part, out_ref in zip((KEEP_B, GIVE_A, KEEP_A, GIVE_B), out_refs):
        out_ref[...] = total[part].astype(bf16)
    token_ref[...] = jnp.zeros_like(token_ref)


def dense_forward(columns, store):
    step = 2 * CBLK
    pairs = columns[0][0].shape[0]
    probe = jnp.concatenate(
        [part[...].reshape(2 * CBLK * pairs, -1) for _, part in columns], axis=0
    )
    for m in range(columns[0][0].shape[1] // step):
        rows = pl.ds(m * step, step)
        lhs = jnp.concatenate(
            [dense[pair, rows, :] for dense, _ in columns for pair in range(pairs)], axis=1
        )
        total = jnp.dot(lhs, probe, preferred_element_type=f32)
        store(pl.ds(2 * m, 2), total.reshape(2, CBLK, -1))


def early_forward_kernel(dense_own_a, dense_own_b, dense_mate_a, own_a, own_b, mate_a, acc):
    def store(rows, value):
        acc[rows] = value

    columns = [(dense_own_a, own_a), (dense_own_b, own_b), (dense_mate_a, mate_a)]
    dense_forward(columns, store)


def late_forward_kernel(dense_mate_b, mate_b, early, out_ref):
    def store(rows, value):
        out_ref[rows] = (early[rows] + value).astype(bf16)

    dense_forward([(dense_mate_b, mate_b)], store)


def adjoint_kernel(resid, *refs):
    lhs = jnp.concatenate([resid[m] for m in range(resid.shape[0])], axis=1)
    count = len(refs) // 2
    for dense, out_ref in zip(refs[:count], refs[count:]):
        for pair in range(dense.shape[0]):
            both = jnp.dot(lhs, dense[pair], preferred_element_type=f32)
            both = both.astype(out_ref.dtype)
            out_ref[2 * pair] = both[:, :CBLK]
            out_ref[2 * pair + 1] = both[:, CBLK:]


def pair_kernel(keep_ref, got_ref, out_ref):
    out_ref[...] = (keep_ref[...] + got_ref[...].astype(f32)).astype(bf16)


def residual_kernel(parts_ref, obs_ref, wt_ref, after_ref, out_ref, *resid_ref):
    for i in range(parts_ref.shape[1]):
        total = parts_ref[0, i].astype(f32)
        for d in range(1, parts_ref.shape[0]):
            total += parts_ref[d, i].astype(f32)
        resid = wt_ref[pl.ds(i, 1), :] * (total.T - obs_ref[pl.ds(i, 1), :])
        if resid_ref:
            resid_ref[0][i] = resid
        rounded = resid.astype(bf16)
        for d in range(parts_ref.shape[0]):
            out_ref[d, i] = rounded


def turn_kernel(in_ref, out_ref, token_ref):
    for i in range(in_ref.shape[0]):
        out_ref[i] = in_ref[i].T
    token_ref[...] = jnp.zeros_like(token_ref)


def prepare_kernel(state, prior, after_ref, field_a, field_b, base_ref):
    quarter = field_a.shape[0]
    own = lax.axis_index("shot") % 2 * (2 * quarter)
    for at, field_ref in ((own, field_a), (own + quarter, field_b)):
        part = pl.ds(at, quarter)
        field_ref[...] = state[part] + prior[part]
    base_ref[...] = state[...] + 0.5 * prior[...]


def sum_over_y(chip_y, part_refs, order, i):
    if len(part_refs) > 2:
        for d, part_ref in enumerate(part_refs):
            order[chip_y ^ d] = part_ref[i]
        parts = [order[y] for y in range(len(part_refs))]
    else:
        parts = [part_ref[i] for part_ref in part_refs]
    total = parts[0].astype(f32)
    for part in parts[1:]:
        total += part.astype(f32)
    return total.T


def probe_kernel(ny, field_ref, *rest):
    part_refs, (out_ref, grad_ref, order) = rest[:ny], rest[ny:]
    for i in range(out_ref.shape[0]):
        grad = sum_over_y(lax.axis_index("shot") // 2, part_refs, order, i)
        grad_ref[i] = grad
        out_ref[i] = (field_ref[i] - 0.25 * grad).astype(bf16)


def total_kernel(ny, after, grad_ref, *rest):
    rest = rest[after:]
    part_refs, (out_ref, order) = rest[:ny], rest[ny:]
    for i in range(out_ref.shape[0]):
        grad2 = sum_over_y(lax.axis_index("shot") // 2, part_refs, order, i)
        out_ref[i] = (grad_ref[i] + grad2).astype(bf16)


def early_update_kernel(base, own_a, own_b, mate_a, out_hbm, rest_ref, new, sems):
    quarter = own_a.shape[0]
    core = lax.axis_index("shot") % 2
    own, mate = core * (2 * quarter), (1 - core) * (2 * quarter)
    copies = []
    for n, (at, part_ref) in enumerate(((own, own_a), (own + quarter, own_b), (mate, mate_a))):
        new[n] = base[pl.ds(at, quarter)] - 0.125 * part_ref[...].astype(f32)
        copies.append(
            pltpu.make_async_copy(new.at[n], out_hbm.at[pl.ds(at, quarter)], sems.at[n])
        )
        copies[-1].start()
    rest_ref[...] = base[pl.ds(mate + quarter, quarter)]
    for copy in copies:
        copy.wait()


def late_update_kernel(rest_ref, mate_b, so_far_hbm, out_hbm, new, sems):
    quarter = mate_b.shape[0]
    at = (1 - lax.axis_index("shot") % 2) * (2 * quarter) + quarter
    copies = []
    for n in range(quarter):
        new[n] = rest_ref[n] - 0.125 * mate_b[n].astype(f32)
        copies.append(pltpu.make_async_copy(new.at[n], out_hbm.at[at + n], sems.at[n]))
        copies[-1].start()
    for copy in copies:
        copy.wait()


def per_device(nshot, nband, sens, bund, cblk, state, prior, observed, pick_weight):
    nblk = sens.shape[0]
    samples = state.shape[1]
    owned, rays = observed.shape
    bundles = owned * nband
    cells = state.shape[0] // CBLK
    quarter = cells // 4
    ny = nshot // 2
    flops = 2 * nblk * rays * CBLK * samples
    sens_bytes = nblk * rays * CBLK * 2

    state_b = state.reshape(cells, CBLK, samples)
    prior_b = prior.reshape(cells, CBLK, samples)

    def other_core(array):
        return lax.ppermute(array, "shot", [(i, i ^ 1) for i in range(nshot)])

    def other_chips(array):
        return [array] + [
            lax.ppermute(array, "shot", [(i, i ^ (2 * d)) for i in range(nshot)])
            for d in range(1, ny)
        ]

    def over_band(array):
        return lax.all_to_all(array, "band", split_axis=0, concat_axis=0, tiled=True)

    part_out = arr((bundles, rays, samples), bf16)
    dense_shape = (quarter // 2, bundles * rays, 2 * CBLK)
    small_token = arr((8, CBLK), f32)
    dense_flops = 2 * bundles * rays * cells * CBLK * samples
    dense_bytes = 2 * bundles * rays * cells * CBLK
    quarter_bf16 = arr((quarter, CBLK, samples), bf16)
    quarter_f32 = arr((quarter, CBLK, samples), f32)
    order = pltpu.VMEM((ny, samples, CBLK), bf16)

    def residual(part, after, name, keep):
        parts = over_band(part).reshape(nband, owned, rays, samples)
        outs = (arr((nband, owned, samples, rays), bf16),)
        if keep:
            outs += (arr((owned, samples, rays), f32),)
        copies, *resid = call(
            residual_kernel, outs, [], [VMEM] * 3 + [ANY], name, bytes_accessed=1 << 20
        )(parts, observed, pick_weight, after)
        return resid, over_band(copies).reshape(bundles, samples, rays)

    def adjoint(dense, resid_all, name):
        def kernel(parts, part):
            return call(
                adjoint_kernel,
                tuple(quarter_f32 if p % 2 else quarter_bf16 for p in parts),
                [],
                [VMEM] * (1 + len(parts)),
                name + part,
                dense_flops * len(parts) // 4,
                dense_bytes * len(parts) // 4,
            )(resid_all, *[dense[p] for p in parts])

        def pair(keep, got, part):
            return call(
                pair_kernel,
                quarter_bf16,
                [],
                [VMEM] * 2,
                name + "_pair" + part,
                bytes_accessed=1 << 19,
            )(keep, got)

        (give_a,) = kernel((GIVE_A,), "_give_a")
        got_a = other_core(give_a)
        keep_a, give_b = kernel((KEEP_A, GIVE_B), "_keep_a")
        got_b = other_core(give_b)
        sums_a = other_chips(pair(keep_a, got_a, "_a"))
        (keep_b,) = kernel((KEEP_B,), "_keep_b")
        sums_b = other_chips(pair(keep_b, got_b, "_b"))
        return sums_a, sums_b, keep_b

    part1 = call(
        first_forward_kernel,
        part_out,
        [
            pltpu.VMEM((bundles, rays, samples), f32),
            pltpu.VMEM((cells, CBLK, samples), bf16),
            pltpu.SMEM((nblk,), i32),
            pltpu.SMEM((nblk,), i32),
            pltpu.VMEM(sens.shape, bf16),
            pltpu.VMEM(state_b.shape, f32),
            pltpu.VMEM(state_b.shape, f32),
            pltpu.SemaphoreType.DMA((2 + 2 * FIELDS + 2 * CHUNKS,)),
            pltpu.VMEM((bundles, rays, samples), bf16),
            pltpu.SemaphoreType.DMA((WRITES,)),
        ],
        [HBM] * 5,
        "forward1",
        flops,
        sens_bytes,
        vmem=FIRST_VMEM,
        out_specs=HBM,
    )(bund, cblk, sens, state_b, prior_b)
    dense_keep_b, *dense, token = call(
        dense_kernel,
        (arr(dense_shape, bf16),) * 4 + (small_token,),
        [pltpu.VMEM((4,) + dense_shape, f32)],
        [SMEM, SMEM, VMEM],
        "dense",
        0,
        16 << 20,
        vmem=3 * dense_bytes + 2 * sens_bytes + (2 << 20),
    )(bund, cblk, sens)
    dense.append(dense_keep_b)
    _, resid_all1 = residual(part1, token, "residual1", False)
    *sums1, after = adjoint(dense, resid_all1, "adjoint1")

    *fields, base = call(
        prepare_kernel,
        (quarter_f32, quarter_f32, arr((cells, CBLK, samples), f32)),
        [],
        [VMEM, VMEM, ANY],
        "prepare",
        bytes_accessed=4 << 20,
    )(state_b, prior_b, after)
    own, grad1, mate = [], [], []
    for field, sums, part in zip(fields, sums1, "ab"):
        probe, grad = call(
            functools.partial(probe_kernel, ny),
            (quarter_bf16, quarter_f32),
            [order],
            [VMEM] * (1 + ny),
            "probe2_" + part,
            bytes_accessed=1 << 19,
        )(field, *sums)
        own.append(probe)
        grad1.append(grad)
        mate.append(other_core(probe))

    early = call(
        early_forward_kernel,
        arr((bundles, rays, samples), f32),
        [],
        [VMEM] * 6,
        "forward2_early",
        dense_flops * 3 // 4,
        dense_bytes * 3 // 4,
    )(dense[KEEP_A], dense[KEEP_B], dense[GIVE_A], own[0], own[1], mate[0])
    part2 = call(
        late_forward_kernel,
        part_out,
        [],
        [VMEM] * 3,
        "forward2_late",
        dense_flops // 4,
        dense_bytes // 4,
    )(dense[GIVE_B], mate[1], early)

    (resid2_t,), resid_all2 = residual(part2, token, "residual2", True)
    *sums2, _ = adjoint(dense, resid_all2, "adjoint2")
    resid2, turned = call(
        turn_kernel,
        (arr((owned, rays, samples), f32), small_token),
        [],
        [VMEM],
        "turn",
        bytes_accessed=1 << 20,
    )(resid2_t)
    own, mate, after = [], [], [turned, dense[GIVE_A], dense[KEEP_A], dense[GIVE_B]]
    for grad, sums, part in zip(grad1, sums2, "ab"):
        total = call(
            functools.partial(total_kernel, ny, len(after)),
            quarter_bf16,
            [order],
            [VMEM] + [ANY] * len(after) + [VMEM] * ny,
            "total_" + part,
            bytes_accessed=1 << 19,
        )(grad, *after, *sums)
        own.append(total)
        after = []
        mate.append(other_core(total))
    whole = arr((cells, CBLK, samples), f32)
    so_far, rest = call(
        early_update_kernel,
        (whole, quarter_f32),
        [pltpu.VMEM((3, quarter, CBLK, samples), f32), pltpu.SemaphoreType.DMA((3,))],
        [VMEM] * 4,
        "new_state_early",
        bytes_accessed=3 << 20,
        out_specs=(HBM, VMEM),
    )(base, own[0], own[1], mate[0])
    new_state = call(
        late_update_kernel,
        whole,
        [pltpu.VMEM((quarter, CBLK, samples), f32), pltpu.SemaphoreType.DMA((quarter,))],
        [VMEM, VMEM, HBM],
        "new_state_late",
        bytes_accessed=1 << 20,
        out_specs=HBM,
        input_output_aliases={2: 0},
    )(rest, mate[1], so_far)
    return new_state.reshape(state.shape), resid2


def solution(mesh):
    in_specs = (
        P(("shot", "band"), None, None),
        P(("shot", "band")),
        P(("shot", "band")),
        P("band", None),
        P("band", None),
        P(("shot", "band"), None),
        P(("shot", "band"), None),
    )
    out_specs = (P("band", None), P(("shot", "band"), None, None))
    return jax.shard_map(
        functools.partial(per_device, mesh.shape["shot"], mesh.shape["band"]),
        mesh=mesh,
        in_specs=in_specs,
        out_specs=out_specs,
        check_vma=False,
    )
```

```python
import functools

import jax
import jax.numpy as jnp
from jax import lax
from jax.experimental import pallas as pl
from jax.experimental.pallas import tpu as pltpu
from jax.sharding import PartitionSpec as P

CBLK = 128
GROUP = 32
CHUNKS = 2
FIELDS = 4
FIRST_VMEM = 55 << 20
GIVE_A, KEEP_A, GIVE_B, KEEP_B = range(4)

VMEM = pl.BlockSpec(memory_space=pltpu.VMEM)
SMEM = pl.BlockSpec(memory_space=pltpu.SMEM)
HBM = pl.BlockSpec(memory_space=pltpu.HBM)
ANY = pl.BlockSpec(memory_space=pl.ANY)

bf16, f32, i32 = jnp.bfloat16, jnp.float32, jnp.int32
arr = jax.ShapeDtypeStruct

def call(body, outs, scratch, in_specs, name, flops=0, bytes_accessed=0, vmem=32 << 20, **more):
    if "out_specs" not in more:
        more["out_specs"] = jax.tree.map(lambda _: VMEM, outs)
    return pl.pallas_call(
        body,
        out_shape=outs,
        in_specs=in_specs,
        scratch_shapes=scratch,
        compiler_params=pltpu.CompilerParams(vmem_limit_bytes=vmem),
        cost_estimate=pl.CostEstimate(
            flops=flops, bytes_accessed=bytes_accessed, transcendentals=0
        ),
        name=name,
        **more,
    )


def first_forward_kernel(
    bund_hbm,
    cblk_hbm,
    sens_hbm,
    state_hbm,
    prior_hbm,
    out_ref,
    acc,
    probe,
    bund,
    cblk,
    sens,
    state,
    prior,
    sems,
):
    nblk = sens.shape[0]
    step = nblk // CHUNKS
    cells = state.shape[0]
    share = cells // FIELDS
    small = [
        pltpu.make_async_copy(bund_hbm, bund, sems.at[0]),
        pltpu.make_async_copy(cblk_hbm, cblk, sems.at[1]),
    ]
    fields = []
    for h in range(FIELDS):
        part = pl.ds(h * share, share)
        fields.append(
            [
                pltpu.make_async_copy(state_hbm.at[part], state.at[part], sems.at[2 + 2 * h]),
                pltpu.make_async_copy(prior_hbm.at[part], prior.at[part], sems.at[3 + 2 * h]),
            ]
        )

    def block_copies(c):
        size = step // 2
        copies = []
        for h in range(2):
            part = pl.ds(c * step + h * size, size)
            sem = sems.at[2 + 2 * FIELDS + 2 * c + h]
            copies.append(pltpu.make_async_copy(sens_hbm.at[part], sens.at[part], sem))
        return copies

    for copy in small + [copy for field in fields for copy in field]:
        copy.start()
    for c in range(CHUNKS):
        for copy in block_copies(c):
            copy.start()
    acc[...] = jnp.zeros_like(acc)

    for h in range(FIELDS):
        part = pl.ds(h * share, share)
        for copy in fields[h]:
            copy.wait()
        probe[part] = (state[part] + 0.5 * prior[part]).astype(bf16)
    for copy in small:
        copy.wait()

    def chunk(c, carry):
        for copy in block_copies(c):
            copy.wait()
        for g in range(step // GROUP):
            ks = [c * step + g * GROUP + j for j in range(GROUP)]
            prods = [
                jnp.dot(sens[k], probe[cblk[k]], preferred_element_type=f32) for k in ks
            ]
            for k, prod in zip(ks, prods):
                acc[bund[k]] += prod
        return carry

    lax.fori_loop(0, CHUNKS, chunk, 0)
    out_ref[...] = acc[...].astype(bf16)


def dense_kernel(bund, cblk, sens, *rest):
    out_refs, (token_ref, total) = rest[:4], rest[4:]
    rays = sens.shape[1]
    quarter = 2 * total.shape[1]
    core = lax.axis_index("shot") % 2
    total[...] = jnp.zeros_like(total)

    def place(k, carry):
        cell = cblk[k]
        kept = jnp.where(cell // (2 * quarter) == core, 1, 0)
        part = 2 * (cell // quarter % 2) + kept
        rows = pl.ds(pl.multiple_of(bund[k] * rays, rays), rays)
        lanes = pl.ds(pl.multiple_of(cell % 2 * CBLK, CBLK), CBLK)
        total[part, cell % quarter // 2, rows, lanes] += sens[k].astype(f32)
        return carry

    lax.fori_loop(0, sens.shape[0], place, 0)
    for part, out_ref in zip((KEEP_B, GIVE_A, KEEP_A, GIVE_B), out_refs):
        out_ref[...] = total[part].astype(bf16)
    token_ref[...] = jnp.zeros_like(token_ref)


def dense_forward(columns, store):
    step = 2 * CBLK
    pairs = columns[0][0].shape[0]
    probe = jnp.concatenate(
        [part[...].reshape(2 * CBLK * pairs, -1) for _, part in columns], axis=0
    )
    for m in range(columns[0][0].shape[1] // step):
        rows = pl.ds(m * step, step)
        lhs = jnp.concatenate(
            [dense[pair, rows, :] for dense, _ in columns for pair in range(pairs)], axis=1
        )
        total = jnp.dot(lhs, probe, preferred_element_type=f32)
        store(pl.ds(2 * m, 2), total.reshape(2, CBLK, -1))


def early_forward_kernel(dense_own_a, dense_own_b, dense_mate_a, own_a, own_b, mate_a, acc):
    def store(rows, value):
        acc[rows] = value

    columns = [(dense_own_a, own_a), (dense_own_b, own_b), (dense_mate_a, mate_a)]
    dense_forward(columns, store)


def late_forward_kernel(dense_mate_b, mate_b, early, out_ref):
    def store(rows, value):
        out_ref[rows] = (early[rows] + value).astype(bf16)

    dense_forward([(dense_mate_b, mate_b)], store)


def adjoint_kernel(resid, *refs):
    lhs = jnp.concatenate([resid[m] for m in range(resid.shape[0])], axis=1)
    count = len(refs) // 2
    for dense, out_ref in zip(refs[:count], refs[count:]):
        for pair in range(dense.shape[0]):
            both = jnp.dot(lhs, dense[pair], preferred_element_type=f32)
            both = both.astype(out_ref.dtype)
            out_ref[2 * pair] = both[:, :CBLK]
            out_ref[2 * pair + 1] = both[:, CBLK:]


def pair_kernel(keep_ref, got_ref, out_ref):
    for i in range(out_ref.shape[0]):
        out_ref[i] = (keep_ref[i] + got_ref[i].astype(f32)).T.astype(bf16)


def residual_kernel(parts_ref, obs_ref, wt_ref, after_ref, out_ref, *resid_ref):
    for i in range(parts_ref.shape[1]):
        total = parts_ref[0, i].astype(f32)
        for d in range(1, parts_ref.shape[0]):
            total += parts_ref[d, i].astype(f32)
        resid = wt_ref[pl.ds(i, 1), :] * (total.T - obs_ref[pl.ds(i, 1), :])
        if resid_ref:
            resid_ref[0][i] = resid
        rounded = resid.astype(bf16)
        for d in range(parts_ref.shape[0]):
            out_ref[d, i] = rounded


def turn_kernel(in_ref, out_ref, token_ref):
    for i in range(in_ref.shape[0]):
        out_ref[i] = in_ref[i].T
    token_ref[...] = jnp.zeros_like(token_ref)


def prepare_kernel(state, prior, after_ref, field_a, field_b, base_ref):
    quarter = field_a.shape[0]
    own = lax.axis_index("shot") % 2 * (2 * quarter)
    for at, field_ref in ((own, field_a), (own + quarter, field_b)):
        part = pl.ds(at, quarter)
        field_ref[...] = state[part] + prior[part]
    base_ref[...] = state[...] + 0.5 * prior[...]


def sum_over_y(chip_y, part_refs, order, i):
    if len(part_refs) > 2:
        for d, part_ref in enumerate(part_refs):
            order[chip_y ^ d] = part_ref[i]
        parts = [order[y] for y in range(len(part_refs))]
    else:
        parts = [part_ref[i] for part_ref in part_refs]
    total = parts[0].astype(f32)
    for part in parts[1:]:
        total += part.astype(f32)
    return total


def probe_kernel(ny, field_ref, *rest):
    part_refs, (out_ref, grad_ref, order) = rest[:ny], rest[ny:]
    for i in range(out_ref.shape[0]):
        grad = sum_over_y(lax.axis_index("shot") // 2, part_refs, order, i)
        grad_ref[i] = grad
        out_ref[i] = (field_ref[i] - 0.25 * grad).astype(bf16)


def total_kernel(ny, after, grad_ref, *rest):
    rest = rest[after:]
    part_refs, (out_ref, order) = rest[:ny], rest[ny:]
    for i in range(out_ref.shape[0]):
        grad2 = sum_over_y(lax.axis_index("shot") // 2, part_refs, order, i)
        out_ref[i] = (grad_ref[i] + grad2).astype(bf16)


def early_update_kernel(base, own_a, own_b, mate_a, out_hbm, rest_ref, new, sems):
    quarter = own_a.shape[0]
    core = lax.axis_index("shot") % 2
    own, mate = core * (2 * quarter), (1 - core) * (2 * quarter)
    copies = []
    for n, (at, part_ref) in enumerate(((own, own_a), (own + quarter, own_b), (mate, mate_a))):
        new[n] = base[pl.ds(at, quarter)] - 0.125 * part_ref[...].astype(f32)
        copies.append(
            pltpu.make_async_copy(new.at[n], out_hbm.at[pl.ds(at, quarter)], sems.at[n])
        )
        copies[-1].start()
    rest_ref[...] = base[pl.ds(mate + quarter, quarter)]
    for copy in copies:
        copy.wait()


def late_update_kernel(rest_ref, mate_b, so_far_hbm, out_hbm, new, sem):
    quarter = mate_b.shape[0]
    at = (1 - lax.axis_index("shot") % 2) * (2 * quarter) + quarter
    new[...] = rest_ref[...] - 0.125 * mate_b[...].astype(f32)
    copy = pltpu.make_async_copy(new, out_hbm.at[pl.ds(at, quarter)], sem)
    copy.start()
    copy.wait()


def per_device(nshot, nband, sens, bund, cblk, state, prior, observed, pick_weight):
    nblk = sens.shape[0]
    samples = state.shape[1]
    owned, rays = observed.shape
    bundles = owned * nband
    cells = state.shape[0] // CBLK
    quarter = cells // 4
    ny = nshot // 2
    flops = 2 * nblk * rays * CBLK * samples
    sens_bytes = nblk * rays * CBLK * 2

    state_b = state.reshape(cells, CBLK, samples)
    prior_b = prior.reshape(cells, CBLK, samples)

    def other_core(array):
        return lax.ppermute(array, "shot", [(i, i ^ 1) for i in range(nshot)])

    def other_chips(array):
        return [array] + [
            lax.ppermute(array, "shot", [(i, i ^ (2 * d)) for i in range(nshot)])
            for d in range(1, ny)
        ]

    def over_band(array):
        return lax.all_to_all(array, "band", split_axis=0, concat_axis=0, tiled=True)

    part_out = arr((bundles, rays, samples), bf16)
    dense_shape = (quarter // 2, bundles * rays, 2 * CBLK)
    small_token = arr((8, CBLK), f32)
    dense_flops = 2 * bundles * rays * cells * CBLK * samples
    dense_bytes = 2 * bundles * rays * cells * CBLK
    quarter_bf16 = arr((quarter, CBLK, samples), bf16)
    quarter_f32 = arr((quarter, CBLK, samples), f32)
    order = pltpu.VMEM((ny, samples, CBLK), bf16)

    def residual(part, after, name, keep):
        parts = over_band(part).reshape(nband, owned, rays, samples)
        outs = (arr((nband, owned, samples, rays), bf16),)
        if keep:
            outs += (arr((owned, samples, rays), f32),)
        copies, *resid = call(
            residual_kernel, outs, [], [VMEM] * 3 + [ANY], name, bytes_accessed=1 << 20
        )(parts, observed, pick_weight, after)
        return resid, over_band(copies).reshape(bundles, samples, rays)

    def adjoint(dense, resid_all, name):
        def kernel(parts, part):
            return call(
                adjoint_kernel,
                tuple(quarter_f32 if p % 2 else quarter_bf16 for p in parts),
                [],
                [VMEM] * (1 + len(parts)),
                name + part,
                dense_flops * len(parts) // 4,
                dense_bytes * len(parts) // 4,
            )(resid_all, *[dense[p] for p in parts])

        def pair(keep, got, part):
            return call(
                pair_kernel,
                quarter_bf16,
                [],
                [VMEM] * 2,
                name + "_pair" + part,
                bytes_accessed=1 << 19,
            )(keep, got)

        (give_a,) = kernel((GIVE_A,), "_give_a")
        got_a = other_core(give_a)
        keep_a, give_b = kernel((KEEP_A, GIVE_B), "_keep_a")
        got_b = other_core(give_b)
        sums_a = other_chips(pair(keep_a, got_a, "_a"))
        (keep_b,) = kernel((KEEP_B,), "_keep_b")
        sums_b = other_chips(pair(keep_b, got_b, "_b"))
        return sums_a, sums_b, keep_b

    part1 = call(
        first_forward_kernel,
        part_out,
        [
            pltpu.VMEM((bundles, rays, samples), f32),
            pltpu.VMEM((cells, CBLK, samples), bf16),
            pltpu.SMEM((nblk,), i32),
            pltpu.SMEM((nblk,), i32),
            pltpu.VMEM(sens.shape, bf16),
            pltpu.VMEM(state_b.shape, f32),
            pltpu.VMEM(state_b.shape, f32),
            pltpu.SemaphoreType.DMA((2 + 2 * FIELDS + 2 * CHUNKS,)),
        ],
        [HBM] * 5,
        "forward1",
        flops,
        sens_bytes,
        vmem=FIRST_VMEM,
    )(bund, cblk, sens, state_b, prior_b)
    dense_keep_b, *dense, token = call(
        dense_kernel,
        (arr(dense_shape, bf16),) * 4 + (small_token,),
        [pltpu.VMEM((4,) + dense_shape, f32)],
        [SMEM, SMEM, VMEM],
        "dense",
        0,
        16 << 20,
        vmem=3 * dense_bytes + 2 * sens_bytes + (2 << 20),
    )(bund, cblk, sens)
    dense.append(dense_keep_b)
    _, resid_all1 = residual(part1, token, "residual1", False)
    *sums1, after = adjoint(dense, resid_all1, "adjoint1")

    *fields, base = call(
        prepare_kernel,
        (quarter_f32, quarter_f32, arr((cells, CBLK, samples), f32)),
        [],
        [VMEM, VMEM, ANY],
        "prepare",
        bytes_accessed=4 << 20,
    )(state_b, prior_b, after)
    own, grad1, mate = [], [], []
    for field, sums, part in zip(fields, sums1, "ab"):
        probe, grad = call(
            functools.partial(probe_kernel, ny),
            (quarter_bf16, quarter_f32),
            [order],
            [VMEM] * (1 + ny),
            "probe2_" + part,
            bytes_accessed=1 << 19,
        )(field, *sums)
        own.append(probe)
        grad1.append(grad)
        mate.append(other_core(probe))

    early = call(
        early_forward_kernel,
        arr((bundles, rays, samples), f32),
        [],
        [VMEM] * 6,
        "forward2_early",
        dense_flops * 3 // 4,
        dense_bytes * 3 // 4,
    )(dense[KEEP_A], dense[KEEP_B], dense[GIVE_A], own[0], own[1], mate[0])
    part2 = call(
        late_forward_kernel,
        part_out,
        [],
        [VMEM] * 3,
        "forward2_late",
        dense_flops // 4,
        dense_bytes // 4,
    )(dense[GIVE_B], mate[1], early)

    (resid2_t,), resid_all2 = residual(part2, token, "residual2", True)
    *sums2, _ = adjoint(dense, resid_all2, "adjoint2")
    resid2, turned = call(
        turn_kernel,
        (arr((owned, rays, samples), f32), small_token),
        [],
        [VMEM],
        "turn",
        bytes_accessed=1 << 20,
    )(resid2_t)
    own, mate, after = [], [], [turned, dense[GIVE_A], dense[KEEP_A], dense[GIVE_B]]
    for grad, sums, part in zip(grad1, sums2, "ab"):
        total = call(
            functools.partial(total_kernel, ny, len(after)),
            quarter_bf16,
            [order],
            [VMEM] + [ANY] * len(after) + [VMEM] * ny,
            "total_" + part,
            bytes_accessed=1 << 19,
        )(grad, *after, *sums)
        own.append(total)
        after = []
        mate.append(other_core(total))
    whole = arr((cells, CBLK, samples), f32)
    so_far, rest = call(
        early_update_kernel,
        (whole, quarter_f32),
        [pltpu.VMEM((3, quarter, CBLK, samples), f32), pltpu.SemaphoreType.DMA((3,))],
        [VMEM] * 4,
        "new_state_early",
        bytes_accessed=3 << 20,
        out_specs=(HBM, VMEM),
    )(base, own[0], own[1], mate[0])
    new_state = call(
        late_update_kernel,
        whole,
        [pltpu.VMEM((quarter, CBLK, samples), f32), pltpu.SemaphoreType.DMA],
        [VMEM, VMEM, HBM],
        "new_state_late",
        bytes_accessed=1 << 20,
        out_specs=HBM,
        input_output_aliases={2: 0},
    )(rest, mate[1], so_far)
    return new_state.reshape(state.shape), resid2


def solution(mesh):
    in_specs = (
        P(("shot", "band"), None, None),
        P(("shot", "band")),
        P(("shot", "band")),
        P("band", None),
        P("band", None),
        P(("shot", "band"), None),
        P(("shot", "band"), None),
    )
    out_specs = (P("band", None), P(("shot", "band"), None, None))
    return jax.shard_map(
        functools.partial(per_device, mesh.shape["shot"], mesh.shape["band"]),
        mesh=mesh,
        in_specs=in_specs,
        out_specs=out_specs,
        check_vma=False,
    )
```

```python
import functools

import jax
import jax.numpy as jnp
from jax import lax
from jax.experimental import pallas as pl
from jax.experimental.pallas import tpu as pltpu
from jax.sharding import PartitionSpec as P

CBLK = 128
GROUP = 32
CHUNKS = 2
FIELDS = 4
FIRST_VMEM = 55 << 20
GIVE_A, KEEP_A, GIVE_B, KEEP_B = range(4)

VMEM = pl.BlockSpec(memory_space=pltpu.VMEM)
SMEM = pl.BlockSpec(memory_space=pltpu.SMEM)
HBM = pl.BlockSpec(memory_space=pltpu.HBM)
ANY = pl.BlockSpec(memory_space=pl.ANY)

bf16, f32, i32 = jnp.bfloat16, jnp.float32, jnp.int32
arr = jax.ShapeDtypeStruct

def call(body, outs, scratch, in_specs, name, flops=0, bytes_accessed=0, vmem=32 << 20, **more):
    if "out_specs" not in more:
        more["out_specs"] = jax.tree.map(lambda _: VMEM, outs)
    return pl.pallas_call(
        body,
        out_shape=outs,
        in_specs=in_specs,
        scratch_shapes=scratch,
        compiler_params=pltpu.CompilerParams(vmem_limit_bytes=vmem),
        cost_estimate=pl.CostEstimate(
            flops=flops, bytes_accessed=bytes_accessed, transcendentals=0
        ),
        name=name,
        **more,
    )


def first_forward_kernel(
    bund_hbm,
    cblk_hbm,
    sens_hbm,
    state_hbm,
    prior_hbm,
    out_ref,
    acc,
    probe,
    bund,
    cblk,
    sens,
    state,
    prior,
    sems,
):
    nblk = sens.shape[0]
    step = nblk // CHUNKS
    cells = state.shape[0]
    share = cells // FIELDS
    small = [
        pltpu.make_async_copy(bund_hbm, bund, sems.at[0]),
        pltpu.make_async_copy(cblk_hbm, cblk, sems.at[1]),
    ]
    fields = []
    for h in range(FIELDS):
        part = pl.ds(h * share, share)
        fields.append(
            [
                pltpu.make_async_copy(state_hbm.at[part], state.at[part], sems.at[2 + 2 * h]),
                pltpu.make_async_copy(prior_hbm.at[part], prior.at[part], sems.at[3 + 2 * h]),
            ]
        )

    def block_copies(c):
        size = step // 2
        copies = []
        for h in range(2):
            part = pl.ds(c * step + h * size, size)
            sem = sems.at[2 + 2 * FIELDS + 2 * c + h]
            copies.append(pltpu.make_async_copy(sens_hbm.at[part], sens.at[part], sem))
        return copies

    for copy in small + [copy for field in fields for copy in field]:
        copy.start()
    for c in range(CHUNKS):
        for copy in block_copies(c):
            copy.start()
    acc[...] = jnp.zeros_like(acc)

    for h in range(FIELDS):
        part = pl.ds(h * share, share)
        for copy in fields[h]:
            copy.wait()
        probe[part] = (state[part] + 0.5 * prior[part]).astype(bf16)
    for copy in small:
        copy.wait()

    def chunk(c, carry):
        for copy in block_copies(c):
            copy.wait()
        for g in range(step // GROUP):
            ks = [c * step + g * GROUP + j for j in range(GROUP)]
            prods = [
                jnp.dot(sens[k], probe[cblk[k]], preferred_element_type=f32) for k in ks
            ]
            for k, prod in zip(ks, prods):
                acc[bund[k]] += prod
        return carry

    lax.fori_loop(0, CHUNKS, chunk, 0)
    out_ref[...] = acc[...].astype(bf16)


def dense_kernel(bund, cblk, sens, *rest):
    out_refs, (token_ref, total) = rest[:4], rest[4:]
    rays = sens.shape[1]
    quarter = 2 * total.shape[1]
    core = lax.axis_index("shot") % 2
    total[...] = jnp.zeros_like(total)

    def place(k, carry):
        cell = cblk[k]
        kept = jnp.where(cell // (2 * quarter) == core, 1, 0)
        part = 2 * (cell // quarter % 2) + kept
        rows = pl.ds(pl.multiple_of(bund[k] * rays, rays), rays)
        lanes = pl.ds(pl.multiple_of(cell % 2 * CBLK, CBLK), CBLK)
        total[part, cell % quarter // 2, rows, lanes] += sens[k].astype(f32)
        return carry

    lax.fori_loop(0, sens.shape[0], place, 0)
    for part, out_ref in zip((KEEP_B, GIVE_A, KEEP_A, GIVE_B), out_refs):
        out_ref[...] = total[part].astype(bf16)
    token_ref[...] = jnp.zeros_like(token_ref)


def dense_forward(columns, store):
    step = 4 * CBLK
    pairs = columns[0][0].shape[0]
    probe = jnp.concatenate(
        [part[...].reshape(2 * CBLK * pairs, -1) for _, part in columns], axis=0
    )
    for m in range(columns[0][0].shape[1] // step):
        rows = pl.ds(m * step, step)
        lhs = jnp.concatenate(
            [dense[pair, rows, :] for dense, _ in columns for pair in range(pairs)], axis=1
        )
        total = jnp.dot(lhs, probe, preferred_element_type=f32)
        store(pl.ds(4 * m, 4), total.reshape(4, CBLK, -1))


def early_forward_kernel(dense_own_a, dense_own_b, dense_mate_a, own_a, own_b, mate_a, acc):
    def store(rows, value):
        acc[rows] = value

    columns = [(dense_own_a, own_a), (dense_own_b, own_b), (dense_mate_a, mate_a)]
    dense_forward(columns, store)


def late_forward_kernel(dense_mate_b, mate_b, early, out_ref):
    def store(rows, value):
        out_ref[rows] = (early[rows] + value).astype(bf16)

    dense_forward([(dense_mate_b, mate_b)], store)


def adjoint_kernel(resid, *refs):
    lhs = jnp.concatenate([resid[m] for m in range(resid.shape[0])], axis=1)
    count = len(refs) // 2
    for dense, out_ref in zip(refs[:count], refs[count:]):
        for pair in range(dense.shape[0]):
            both = jnp.dot(lhs, dense[pair], preferred_element_type=f32)
            both = both.astype(out_ref.dtype)
            out_ref[2 * pair] = both[:, :CBLK]
            out_ref[2 * pair + 1] = both[:, CBLK:]


def pair_kernel(keep_ref, got_ref, out_ref):
    out_ref[...] = (keep_ref[...] + got_ref[...].astype(f32)).astype(bf16)


def residual_kernel(parts_ref, obs_ref, wt_ref, after_ref, out_ref, *resid_ref):
    for i in range(parts_ref.shape[1]):
        total = parts_ref[0, i].astype(f32)
        for d in range(1, parts_ref.shape[0]):
            total += parts_ref[d, i].astype(f32)
        resid = wt_ref[pl.ds(i, 1), :] * (total.T - obs_ref[pl.ds(i, 1), :])
        if resid_ref:
            resid_ref[0][i] = resid
        rounded = resid.astype(bf16)
        for d in range(parts_ref.shape[0]):
            out_ref[d, i] = rounded


def turn_kernel(in_ref, out_ref, token_ref):
    for i in range(in_ref.shape[0]):
        out_ref[i] = in_ref[i].T
    token_ref[...] = jnp.zeros_like(token_ref)


def prepare_kernel(state, prior, after_ref, field_a, field_b, base_ref):
    quarter = field_a.shape[0]
    own = lax.axis_index("shot") % 2 * (2 * quarter)
    for at, field_ref in ((own, field_a), (own + quarter, field_b)):
        part = pl.ds(at, quarter)
        field_ref[...] = state[part] + prior[part]
    base_ref[...] = state[...] + 0.5 * prior[...]


def sum_over_y(chip_y, part_refs, order, i):
    if len(part_refs) > 2:
        for d, part_ref in enumerate(part_refs):
            order[chip_y ^ d] = part_ref[i]
        parts = [order[y] for y in range(len(part_refs))]
    else:
        parts = [part_ref[i] for part_ref in part_refs]
    total = parts[0].astype(f32)
    for part in parts[1:]:
        total += part.astype(f32)
    return total.T


def probe_kernel(ny, field_ref, *rest):
    part_refs, (out_ref, grad_ref, order) = rest[:ny], rest[ny:]
    for i in range(out_ref.shape[0]):
        grad = sum_over_y(lax.axis_index("shot") // 2, part_refs, order, i)
        grad_ref[i] = grad
        out_ref[i] = (field_ref[i] - 0.25 * grad).astype(bf16)


def total_kernel(ny, after, grad_ref, *rest):
    rest = rest[after:]
    part_refs, (out_ref, order) = rest[:ny], rest[ny:]
    for i in range(out_ref.shape[0]):
        grad2 = sum_over_y(lax.axis_index("shot") // 2, part_refs, order, i)
        out_ref[i] = (grad_ref[i] + grad2).astype(bf16)


def early_update_kernel(base, own_a, own_b, mate_a, out_hbm, rest_ref, new, sems):
    quarter = own_a.shape[0]
    core = lax.axis_index("shot") % 2
    own, mate = core * (2 * quarter), (1 - core) * (2 * quarter)
    copies = []
    for n, (at, part_ref) in enumerate(((own, own_a), (own + quarter, own_b), (mate, mate_a))):
        new[n] = base[pl.ds(at, quarter)] - 0.125 * part_ref[...].astype(f32)
        copies.append(
            pltpu.make_async_copy(new.at[n], out_hbm.at[pl.ds(at, quarter)], sems.at[n])
        )
        copies[-1].start()
    rest_ref[...] = base[pl.ds(mate + quarter, quarter)]
    for copy in copies:
        copy.wait()


def late_update_kernel(rest_ref, mate_b, so_far_hbm, out_hbm, new, sem):
    quarter = mate_b.shape[0]
    at = (1 - lax.axis_index("shot") % 2) * (2 * quarter) + quarter
    new[...] = rest_ref[...] - 0.125 * mate_b[...].astype(f32)
    copy = pltpu.make_async_copy(new, out_hbm.at[pl.ds(at, quarter)], sem)
    copy.start()
    copy.wait()


def per_device(nshot, nband, sens, bund, cblk, state, prior, observed, pick_weight):
    nblk = sens.shape[0]
    samples = state.shape[1]
    owned, rays = observed.shape
    bundles = owned * nband
    cells = state.shape[0] // CBLK
    quarter = cells // 4
    ny = nshot // 2
    flops = 2 * nblk * rays * CBLK * samples
    sens_bytes = nblk * rays * CBLK * 2

    state_b = state.reshape(cells, CBLK, samples)
    prior_b = prior.reshape(cells, CBLK, samples)

    def other_core(array):
        return lax.ppermute(array, "shot", [(i, i ^ 1) for i in range(nshot)])

    def other_chips(array):
        return [array] + [
            lax.ppermute(array, "shot", [(i, i ^ (2 * d)) for i in range(nshot)])
            for d in range(1, ny)
        ]

    def over_band(array):
        return lax.all_to_all(array, "band", split_axis=0, concat_axis=0, tiled=True)

    part_out = arr((bundles, rays, samples), bf16)
    dense_shape = (quarter // 2, bundles * rays, 2 * CBLK)
    small_token = arr((8, CBLK), f32)
    dense_flops = 2 * bundles * rays * cells * CBLK * samples
    dense_bytes = 2 * bundles * rays * cells * CBLK
    quarter_bf16 = arr((quarter, CBLK, samples), bf16)
    quarter_f32 = arr((quarter, CBLK, samples), f32)
    order = pltpu.VMEM((ny, samples, CBLK), bf16)

    def residual(part, after, name, keep):
        parts = over_band(part).reshape(nband, owned, rays, samples)
        outs = (arr((nband, owned, samples, rays), bf16),)
        if keep:
            outs += (arr((owned, samples, rays), f32),)
        copies, *resid = call(
            residual_kernel, outs, [], [VMEM] * 3 + [ANY], name, bytes_accessed=1 << 20
        )(parts, observed, pick_weight, after)
        return resid, over_band(copies).reshape(bundles, samples, rays)

    def adjoint(dense, resid_all, name):
        def kernel(parts, part):
            return call(
                adjoint_kernel,
                tuple(quarter_f32 if p % 2 else quarter_bf16 for p in parts),
                [],
                [VMEM] * (1 + len(parts)),
                name + part,
                dense_flops * len(parts) // 4,
                dense_bytes * len(parts) // 4,
            )(resid_all, *[dense[p] for p in parts])

        def pair(keep, got, part):
            return call(
                pair_kernel,
                quarter_bf16,
                [],
                [VMEM] * 2,
                name + "_pair" + part,
                bytes_accessed=1 << 19,
            )(keep, got)

        (give_a,) = kernel((GIVE_A,), "_give_a")
        got_a = other_core(give_a)
        keep_a, give_b = kernel((KEEP_A, GIVE_B), "_keep_a")
        got_b = other_core(give_b)
        sums_a = other_chips(pair(keep_a, got_a, "_a"))
        (keep_b,) = kernel((KEEP_B,), "_keep_b")
        sums_b = other_chips(pair(keep_b, got_b, "_b"))
        return sums_a, sums_b, keep_b

    part1 = call(
        first_forward_kernel,
        part_out,
        [
            pltpu.VMEM((bundles, rays, samples), f32),
            pltpu.VMEM((cells, CBLK, samples), bf16),
            pltpu.SMEM((nblk,), i32),
            pltpu.SMEM((nblk,), i32),
            pltpu.VMEM(sens.shape, bf16),
            pltpu.VMEM(state_b.shape, f32),
            pltpu.VMEM(state_b.shape, f32),
            pltpu.SemaphoreType.DMA((2 + 2 * FIELDS + 2 * CHUNKS,)),
        ],
        [HBM] * 5,
        "forward1",
        flops,
        sens_bytes,
        vmem=FIRST_VMEM,
    )(bund, cblk, sens, state_b, prior_b)
    dense_keep_b, *dense, token = call(
        dense_kernel,
        (arr(dense_shape, bf16),) * 4 + (small_token,),
        [pltpu.VMEM((4,) + dense_shape, f32)],
        [SMEM, SMEM, VMEM],
        "dense",
        0,
        16 << 20,
        vmem=3 * dense_bytes + 2 * sens_bytes + (2 << 20),
    )(bund, cblk, sens)
    dense.append(dense_keep_b)
    _, resid_all1 = residual(part1, token, "residual1", False)
    *sums1, after = adjoint(dense, resid_all1, "adjoint1")

    *fields, base = call(
        prepare_kernel,
        (quarter_f32, quarter_f32, arr((cells, CBLK, samples), f32)),
        [],
        [VMEM, VMEM, ANY],
        "prepare",
        bytes_accessed=4 << 20,
    )(state_b, prior_b, after)
    own, grad1, mate = [], [], []
    for field, sums, part in zip(fields, sums1, "ab"):
        probe, grad = call(
            functools.partial(probe_kernel, ny),
            (quarter_bf16, quarter_f32),
            [order],
            [VMEM] * (1 + ny),
            "probe2_" + part,
            bytes_accessed=1 << 19,
        )(field, *sums)
        own.append(probe)
        grad1.append(grad)
        mate.append(other_core(probe))

    early = call(
        early_forward_kernel,
        arr((bundles, rays, samples), f32),
        [],
        [VMEM] * 6,
        "forward2_early",
        dense_flops * 3 // 4,
        dense_bytes * 3 // 4,
    )(dense[KEEP_A], dense[KEEP_B], dense[GIVE_A], own[0], own[1], mate[0])
    part2 = call(
        late_forward_kernel,
        part_out,
        [],
        [VMEM] * 3,
        "forward2_late",
        dense_flops // 4,
        dense_bytes // 4,
    )(dense[GIVE_B], mate[1], early)

    (resid2_t,), resid_all2 = residual(part2, token, "residual2", True)
    *sums2, _ = adjoint(dense, resid_all2, "adjoint2")
    resid2, turned = call(
        turn_kernel,
        (arr((owned, rays, samples), f32), small_token),
        [],
        [VMEM],
        "turn",
        bytes_accessed=1 << 20,
    )(resid2_t)
    own, mate, after = [], [], [turned, dense[GIVE_A], dense[KEEP_A], dense[GIVE_B]]
    for grad, sums, part in zip(grad1, sums2, "ab"):
        total = call(
            functools.partial(total_kernel, ny, len(after)),
            quarter_bf16,
            [order],
            [VMEM] + [ANY] * len(after) + [VMEM] * ny,
            "total_" + part,
            bytes_accessed=1 << 19,
        )(grad, *after, *sums)
        own.append(total)
        after = []
        mate.append(other_core(total))
    whole = arr((cells, CBLK, samples), f32)
    so_far, rest = call(
        early_update_kernel,
        (whole, quarter_f32),
        [pltpu.VMEM((3, quarter, CBLK, samples), f32), pltpu.SemaphoreType.DMA((3,))],
        [VMEM] * 4,
        "new_state_early",
        bytes_accessed=3 << 20,
        out_specs=(HBM, VMEM),
    )(base, own[0], own[1], mate[0])
    new_state = call(
        late_update_kernel,
        whole,
        [pltpu.VMEM((quarter, CBLK, samples), f32), pltpu.SemaphoreType.DMA],
        [VMEM, VMEM, HBM],
        "new_state_late",
        bytes_accessed=1 << 20,
        out_specs=HBM,
        input_output_aliases={2: 0},
    )(rest, mate[1], so_far)
    return new_state.reshape(state.shape), resid2


def solution(mesh):
    in_specs = (
        P(("shot", "band"), None, None),
        P(("shot", "band")),
        P(("shot", "band")),
        P("band", None),
        P("band", None),
        P(("shot", "band"), None),
        P(("shot", "band"), None),
    )
    out_specs = (P("band", None), P(("shot", "band"), None, None))
    return jax.shard_map(
        functools.partial(per_device, mesh.shape["shot"], mesh.shape["band"]),
        mesh=mesh,
        in_specs=in_specs,
        out_specs=out_specs,
        check_vma=False,
    )
```
